128 devices in a mesh: grp: 8 (over z, core), dev: 16 (over y, x).
Axes of the slice: x: 4, y: 4, z: 4, core: 2. Of those that a mesh axis runs over, the one named last changes fastest.
Arguments:
- divergence: float32 [512, 16, 256], P(('grp', 'dev')), may hold values from -4 to 4
- box_coords: int32 [512, 3], replicated, may hold values from 0 to 7, as said below
- neighbors: int32 [512, 6], replicated, may hold values from -1 to 511, as said below
Outputs:
- potential: float32 [512, 16, 256], P(('grp', 'dev'))
- residual: float32 [512, 16, 256], P(('grp', 'dev'))
The draws below stay inside these ranges and needn't reach their ends.
Inputs may be any that keep to these rules, and one draw needn't show every extreme that they name: `box_coords`: every lattice position of 8 x 8 x 8 is held by exactly one box. Box b is held by index b // 4 of grp+dev in mesh order; the device at index g of grp and index d of dev holds the four boxes with x = g, y equal to 2 * (d // 4) or one more, and z equal to 2 * (d % 4) or one more, in an order that varies from device to device. neighbors[b, f] is the index of the box next to box b on side f, or -1 at the edge of the lattice.
All inputs are finite; a program needn't handle non-finite values.
Results may differ from the reference program's by a relative error of at most 0.00025.
Values sent between devices are 32-bit elements; how exact they have to be, the bound alone decides.
No kernel may reach another device: no remote copies, remote signals or barrier semaphores. Data moves between devices by JAX's collectives and lax.ppermute only.
A program may use at most 64 MiB of HBM per device.

```python
import jax
import jax.numpy as jnp

BOX = 16
BPD = 4
KC = 4
CYCLES = 2
LZ = 8
LX = 8
LY = 8
NB = 512


def box_layout(key):
    device_count = NB // BPD
    brick_y = LY // 2
    brick_z = LZ // 2
    bricks = jnp.arange(device_count, dtype=jnp.int32)
    sub_keys = jax.random.split(jax.random.fold_in(key, 11), device_count)
    box_order = jax.vmap(lambda sub_key: jax.random.permutation(sub_key, BPD))(sub_keys).astype(jnp.int32).reshape(-1)
    brick_x_pos = bricks // (brick_y * brick_z)
    brick_y_pos = bricks // brick_z % brick_y
    brick_z_pos = bricks % brick_z
    coord_x = jnp.repeat(brick_x_pos, BPD)
    coord_y = 2 * jnp.repeat(brick_y_pos, BPD) + box_order // 2
    coord_z = 2 * jnp.repeat(brick_z_pos, BPD) + box_order % 2
    box_pos = jnp.stack([coord_x, coord_y, coord_z], axis=1)
    lattice = (coord_x * LY + coord_y) * LZ + coord_z
    storage = jnp.zeros((NB,), jnp.int32).at[lattice].set(jnp.arange(NB, dtype=jnp.int32))
    columns = []
    for axis_index in range(3):
        axis_limit = (LX, LY, LZ)[axis_index]
        for step_sign in (-1, 1):
            moved_pos = box_pos.at[:, axis_index].add(step_sign)
            inside = (moved_pos[:, axis_index] >= 0) & (moved_pos[:, axis_index] < axis_limit)
            moved_id = (moved_pos[:, 0] * LY + moved_pos[:, 1]) * LZ + moved_pos[:, 2]
            columns.append(jnp.where(inside, storage[jnp.clip(moved_id, 0, NB - 1)], -1))
    return (box_pos, jnp.stack(columns, axis=1).astype(jnp.int32))


def draw_box_coords(key, part):
    layout = box_layout(key)
    return layout[0]


def draw_neighbors(key, part):
    layout = box_layout(key)
    return layout[1]


def draw_divergence(key, part):
    key = jax.random.fold_in(key, 3)
    values = jnp.clip(jax.random.normal(key, (NB, BOX, BOX * BOX)), -4.0, 4.0)
    return values.astype(jnp.float32)


def setup_inputs(seed: int = 0) -> dict:
    key_list = jax.random.split(jax.random.key(seed), 4)
    divergence = draw_divergence(jax.random.fold_in(key_list[3], 71), 0)
    box_coords = draw_box_coords(jax.random.fold_in(key_list[3], 71), 0)
    neighbors = draw_neighbors(jax.random.fold_in(key_list[3], 71), 0)
    return dict(divergence=divergence, box_coords=box_coords, neighbors=neighbors)


RELAX_WEIGHT = 0.8
FACE_OPPOSITE = (1, 0, 3, 2, 5, 4)


def box_faces(grid_field):
    box_count, box_edge, box_plane = grid_field.shape
    return jnp.stack([grid_field[:, 0, :], grid_field[:, box_edge - 1, :],
                      grid_field[:, :, :box_edge].reshape(box_count, box_plane),
                      grid_field[:, :, box_plane - box_edge:].reshape(box_count, box_plane),
                      grid_field[:, :, 0::box_edge].reshape(box_count, box_plane),
                      grid_field[:, :, box_edge - 1::box_edge].reshape(box_count, box_plane)], axis=1)


def neighbor_total(grid_field, ghost):
    box_count, box_edge, box_plane = grid_field.shape
    k_index = jnp.arange(box_plane, dtype=jnp.int32) % box_edge
    zero_column = jnp.zeros((box_count, box_edge, 1), grid_field.dtype)
    up_x = jnp.concatenate([grid_field[:, 1:, :], ghost[:, 1][:, None, :]], axis=1)
    down_x = jnp.concatenate([ghost[:, 0][:, None, :], grid_field[:, :-1, :]], axis=1)
    up_y = jnp.concatenate([grid_field[:, :, box_edge:], ghost[:, 3].reshape(box_count, box_edge, box_edge)], axis=2)
    down_y = jnp.concatenate([ghost[:, 2].reshape(box_count, box_edge, box_edge), grid_field[:, :, :box_plane - box_edge]], axis=2)
    up_z = jnp.where(k_index == box_edge - 1, jnp.repeat(ghost[:, 5].reshape(box_count, box_edge, box_edge), box_edge, axis=2),
                     jnp.concatenate([grid_field[:, :, 1:], zero_column], axis=2))
    down_z = jnp.where(k_index == 0, jnp.repeat(ghost[:, 4].reshape(box_count, box_edge, box_edge), box_edge, axis=2),
                       jnp.concatenate([zero_column, grid_field[:, :, :-1]], axis=2))
    return ((up_x + down_x) + (up_y + down_y)) + (up_z + down_z)


def operate(grid_field, ghost):
    return 6.0 * grid_field - neighbor_total(grid_field, ghost)


def restrict_boxes(residual_now):
    box_count, box_edge, box_plane = residual_now.shape
    half_edge = box_edge // 2
    grouped = residual_now.reshape(box_count, half_edge, 2, half_edge, 2, half_edge, 2)
    coarse_blocks = jnp.sum(grouped, axis=(2, 4, 6)) * 0.125
    return jnp.transpose(coarse_blocks, (0, 3, 1, 2))


def prolong_boxes(blocks, box_edge):
    box_count = blocks.shape[0]
    fine_blocks = jnp.transpose(blocks, (0, 2, 3, 1))
    fine_blocks = jnp.repeat(jnp.repeat(jnp.repeat(fine_blocks, 2, axis=1), 2, axis=2), 2, axis=3)
    return fine_blocks.reshape(box_count, box_edge, box_edge * box_edge)


def coarse_neighbors(padded):
    center = padded[1:-1]
    zero_x = jnp.zeros_like(center[:, :1, :])
    zero_y = jnp.zeros_like(center[:, :, :1])
    along_x = jnp.concatenate([center[:, 1:, :], zero_x], axis=1) + jnp.concatenate([zero_x, center[:, :-1, :]], axis=1)
    along_y = jnp.concatenate([center[:, :, 1:], zero_y], axis=2) + jnp.concatenate([zero_y, center[:, :, :-1]], axis=2)
    return ((padded[2:] + padded[:-2]) + along_x) + along_y


def coarse_sweep(correction, coarse_source, padded):
    return correction + (RELAX_WEIGHT / 1.5) * (coarse_source - 0.25 * (6.0 * correction - coarse_neighbors(padded)))


def block_index(box_pos, half_edge, z_base):
    offsets = jnp.arange(half_edge, dtype=jnp.int32)
    z_index = box_pos[:, 2, None, None, None] * half_edge + offsets[None, :, None, None] - z_base
    x_index = box_pos[:, 0, None, None, None] * half_edge + offsets[None, None, :, None]
    y_index = box_pos[:, 1, None, None, None] * half_edge + offsets[None, None, None, :]
    return z_index, x_index, y_index


def fine_ghosts(grid_field, neighbors):
    box_count, box_edge, box_plane = grid_field.shape
    all_faces = box_faces(grid_field).reshape(box_count * 6, box_plane)
    opposite = jnp.array(FACE_OPPOSITE, dtype=jnp.int32)
    face_index = neighbors * 6 + opposite[None, :]
    taken_rows = all_faces[jnp.clip(face_index, 0, box_count * 6 - 1)]
    return jnp.where((neighbors >= 0)[:, :, None], taken_rows, 0.0)


def reference(divergence, box_coords, neighbors):
    box_count, box_edge, box_plane = divergence.shape
    half_edge = box_edge // 2
    potential = jnp.zeros_like(divergence)
    z_index, x_index, y_index = block_index(box_coords, half_edge, 0)
    for cycle_index in range(CYCLES):
        potential = potential + (RELAX_WEIGHT / 6.0) * (divergence - operate(potential, fine_ghosts(potential, neighbors)))
        residual_now = divergence - operate(potential, fine_ghosts(potential, neighbors))
        coarse_source = jnp.zeros((LZ * half_edge, LX * half_edge, LY * half_edge), divergence.dtype)
        coarse_source = coarse_source.at[z_index, x_index, y_index].set(restrict_boxes(residual_now))
        coarse_source = coarse_source - jnp.mean(coarse_source)
        correction = jnp.zeros_like(coarse_source)
        for sweep_index in range(KC):
            padded = jnp.pad(correction, ((1, 1), (0, 0), (0, 0)))
            correction = coarse_sweep(correction, coarse_source, padded)
        potential = potential + prolong_boxes(correction[z_index, x_index, y_index], box_edge)
        potential = potential + (RELAX_WEIGHT / 6.0) * (divergence - operate(potential, fine_ghosts(potential, neighbors)))
    residual = divergence - operate(potential, fine_ghosts(potential, neighbors))
    return potential, residual
```

```python
import functools

import numpy as np

import jax
import jax.numpy as jnp
from jax import lax
from jax.experimental import pallas as pl
from jax.experimental.pallas import tpu as pltpu
from jax.sharding import PartitionSpec as P

KC = 4
CYCLES = 2
W = 0.8 / 6.0
BETA = 0.8 / 1.5
CELLS = 128**3
BLOCK = 16
LANES = 128
F32 = jnp.float32


def _apply(v):
    total = 6.0 * v
    for axis in range(3):
        lo = [slice(None)] * 3
        hi = [slice(None)] * 3
        lo[axis], hi[axis] = slice(None, -1), slice(1, None)
        total[tuple(lo)] -= v[tuple(hi)]
        total[tuple(hi)] -= v[tuple(lo)]
    return total


def _mean_weights():
    ones = np.ones((128, 128, 128))
    relax = lambda v: v - W * _apply(v)
    k0 = _apply(ones)
    k1 = relax(k0)
    k2 = relax(k1)
    q = k2.reshape(64, 2, 64, 2, 64, 2).sum(axis=(1, 3, 5))
    s = np.zeros_like(q)
    for _ in range(KC):
        s = s + BETA * (q - 0.25 * _apply(s))
    back = np.repeat(np.repeat(np.repeat(s, 2, 0), 2, 1), 2, 2) / 8.0
    full = ones - W * (k0 + k1 + k2) - relax(back) + (s.sum() / CELLS) * relax(ones)
    blocks = []
    for x in (0, 3, 7):
        for y in (0, 1, 3):
            for z in (0, 1, 3):
                b = full[16 * x : 16 * x + 16, 32 * y : 32 * y + 32, 32 * z : 32 * z + 32]
                b = b.reshape(16, 4, 8, 2, 16).transpose(1, 3, 0, 2, 4)
                blocks.append(b.reshape(8, 16, LANES))
    return np.stack(blocks).astype(np.float32)


def _iota(shape, dim):
    return lax.broadcasted_iota(jnp.int32, shape, dim)


def _roll(v, shift, axis):
    shift = shift % v.shape[axis]
    return v if shift == 0 else pltpu.roll(v, shift, axis)


def _position():
    d = lax.axis_index("dev")
    return lax.axis_index("grp"), d // 4, d % 4


def _blk(ref, i):
    return ref[BLOCK * i : BLOCK * (i + 1), :]


def _put(ref, i, v):
    ref[BLOCK * i : BLOCK * (i + 1), :] = v


def _fetch_kernel(div, w2, raw, weight, sem):
    g, yb, zb = _position()
    kind = lambda i, n: jnp.where(i == 0, 0, jnp.where(i == n - 1, 2, 1))
    which = kind(g, 8) * 9 + kind(yb, 4) * 3 + kind(zb, 4)
    copies = (
        pltpu.make_async_copy(div, raw, sem.at[0]),
        pltpu.make_async_copy(w2.at[which], weight, sem.at[1]),
    )
    for copy in copies:
        copy.start()
    for copy in copies:
        copy.wait()


def _sort_kernel(coords, raw, weight, own, sums, order, plain):
    g, yb, zb = _position()
    row = _iota((16, LANES), 0)
    lane = _iota((16, LANES), 1)
    j, k = lane // 16, lane % 16
    edge_x = ((row == 0) & (g == 0)).astype(F32) + ((row == 15) & (g == 7)).astype(F32)
    s1 = jnp.zeros((16, LANES), F32)
    s2 = jnp.zeros((16, LANES), F32)
    box_of = _box_of(coords, g, yb, zb)
    row8 = _iota((8, LANES), 0)
    order[...] = sum(jnp.where(row8 == h, box_of[h], 0) for h in range(4))
    for o in range(4):
        for h in range(2):
            v = raw[box_of[(o // 2) * 2 + h], :, (o % 2) * LANES : (o % 2 + 1) * LANES]
            at = BLOCK * (o * 2 + h)
            plain[at : at + BLOCK, :] = v
            edge = edge_x
            if o == 0:
                edge += ((j == 0) & (yb == 0)).astype(F32)
            if o == 3:
                edge += ((j == 7) & (yb == 3)).astype(F32)
            if h == 0:
                edge += ((k == 0) & (zb == 0)).astype(F32)
            else:
                edge += ((k == 15) & (zb == 3)).astype(F32)
            s1 += (1.0 - W * edge) * v
            s2 += weight[o * 2 + h] * v
    for i in range(16):
        own[8 * i : 8 * i + 8, :] = plain[pl.ds(BLOCK * (i // 2) + i % 2, 8, stride=2), :]
    s1, s2 = (jnp.sum(v, axis=0, keepdims=True) for v in (s1, s2))
    sums[...] = jnp.where(row8 == 0, s1, jnp.where(row8 == 1, s2, 0.0))


def _box_of(coords, g, yb, zb):
    mine = (g * 4 + yb) * 4 + zb
    at = pl.ds(pl.multiple_of(mine // 32 * LANES, LANES), LANES)
    slot = coords[1:2, at] % 2 * 2 + coords[2:3, at] % 2
    box = _iota((1, LANES), 1) - mine % 32 * 4
    inside = (box >= 0) & (box < 4)
    return [jnp.sum(jnp.where(inside & (slot == h), box, 0)) for h in range(4)]


def _ext(own, below, above, q, h):
    if q == 0:
        return _roll(_blk(below, 4), 64 * h, 1)
    if q < 3:
        return _blk(below, (q - 1) * 2 + h)
    if q < 7:
        return _blk(own, (q - 3) * 2 + h)
    if q < 9:
        return _blk(above, (q - 7) * 2 + h)
    return _roll(_blk(above, 4), 64 * h, 1)


def _pack_quads(pieces, src_quad):
    quad = _iota(pieces[0].shape, 1) % 16 // 4
    out = _roll(pieces[0], 4 * (0 - src_quad), 1)
    for s in range(1, len(pieces)):
        out = jnp.where(quad == s, _roll(pieces[s], 4 * (s - src_quad), 1), out)
    return out


Y_FAR, Y_SUMS, Y_MESSAGE = 64, 80, 88


def _y_kernel(own, sums, up, down):
    half = _iota((BLOCK, LANES), 1) < 64
    for i in range(4):
        _put(up, i, _blk(own, i + 4))
        _put(down, i, _blk(own, i))
    _put(up, 4, jnp.where(half, _roll(_blk(own, 3), 64, 1), _blk(own, 2)))
    _put(down, 4, jnp.where(half, _blk(own, 4), _roll(_blk(own, 5), 64, 1)))
    for ref in (up, down):
        ref[Y_SUMS:Y_MESSAGE, :] = sums[...]


def _total_kernel(sums, below, above, across, total):
    total[...] = sums[...] + below[Y_SUMS:Y_MESSAGE, :] + above[Y_SUMS:Y_MESSAGE, :] + across[...]


def _z_kernel(own, below, above, total, up, down):
    ext = lambda q, h: _ext(own, below, above, q, h)
    for q in range(1, 9):
        _put(up, q - 1, ext(q, 1))
        _put(down, q - 1, ext(q, 0))
    for ref, near, quad in ((up, 1, 3), (down, 0, 0)):
        far = [ext(q, 1 - near) for q in range(2, 8)]
        _put(ref, 8, _pack_quads(far[:4], quad))
        _put(ref, 9, _pack_quads([*far[4:], ext(0, near), ext(9, near)], quad))
        ref[160:168, :] = total[...]


OUTER, TAIL, SUMS, MESSAGE = 384, 480, 512, 520
OWN_EY, OWN_COLS = 512, 576


def _rows_to(pieces):
    row = _iota((8, LANES), 0)
    out = None
    for i, (v, r) in enumerate(pieces):
        v = _roll(v, 2 * i - r, 0)
        out = v if out is None else jnp.where(row < 2 * i, out, v)
    return out


def _share(lo, hi, near):
    row, lane = _iota((8, LANES), 0), _iota((8, LANES), 1)
    middle = jnp.where(lane % 16 < 8, hi, lo)
    edge = jnp.where((row // 2) == near // 2, lo, _roll(hi, 2 if near else -2, 0))
    return jnp.where((row >= 2) & (row < 6), middle, edge)


def _x_kernel(own, below, above, zbelow, zabove, total, across, mine, up, down, high, low, part):
    ext = lambda q, h: _ext(own, below, above, q, h)
    two_away = []
    for q in range(1, 9):
        pieces = (_blk(zbelow, q - 1), ext(q, 0), ext(q, 1), _blk(zabove, q - 1))
        for p in range(4):
            _put(mine, (q - 1) * 4 + p, pieces[p])
        if 2 <= q <= 7:
            two_away += pieces[1:3]
            for p in range(4):
                _put(up, (q - 2) * 4 + p, pieces[p])
                _put(down, (q - 2) * 4 + p, pieces[p])
            continue
        at = OUTER + (0 if q == 1 else 48)
        for ref, near in ((up, 6), (down, 0)):
            ref[at : at + 16, :] = pieces[1]
            ref[at + 16 : at + 32, :] = pieces[2]
            for s in (0, 8):
                ref[at + 32 + s : at + 40 + s, :] = _share(pieces[0][s : s + 8], pieces[3][s : s + 8], near)
    for src, quad in ((zbelow, 3), (zabove, 0)):
        near = [_blk(src, q - 1) for q in range(2, 8)]
        two_away += [_pack_quads(near[:4], quad), _pack_quads(near[4:], quad)]
    for ref, r in ((high, 6), (low, 0)):
        for i in range(0, 16, 2):
            a, b = two_away[i : i + 2]
            ref[4 * i : 4 * i + 8, :] = _rows_to([(a[:8], r), (b[:8], r), (a[8:], r), (b[8:], r)])
    extra = [ext(q, h) for q in (0, 9) for h in range(2)]
    extra += [_blk(zbelow, 8), _blk(zbelow, 9), _blk(zabove, 8), _blk(zabove, 9)]
    for i, v in enumerate(extra):
        _put(mine, 32 + i, v)
    for ref, r in ((up, 6), (down, 0)):
        for t in range(4):
            rows = slice(8 * (t % 2), 8 * (t % 2) + 8)
            tile = _rows_to([(v[rows], r) for v in extra[4 * (t // 2) : 4 * (t // 2) + 4]])
            ref[TAIL + 8 * t : TAIL + 8 * t + 8, :] = tile
    t = total[...] + zbelow[160:168, :] + zabove[160:168, :] + across[...]
    part[...] = t
    for ref, at in ((up, SUMS), (down, SUMS), (high, 64), (low, 64)):
        ref[at : at + 8, :] = t


def _window_kernel(mine, xm1, xp1, xm2, xp2, out, send):
    odd = _position()[0] % 2 == 1
    low = xm1[SUMS:MESSAGE, :] + xm2[64:72, :]
    high = xp1[SUMS:MESSAGE, :] + xp2[64:72, :]
    out[...] = mine[...] + (low + high)
    send[...] = mine[...] + jnp.where(odd, high, low)


FINE, COARSE = 40, 20


def _inside(pos, start, limit):
    return ((pos + start >= 0) & (pos + start < limit)).astype(F32)


def _ring_mask(g, zb):
    row = _iota((32, LANES), 0)
    offset = jnp.where(row < 4, row + 16, row - 16)
    return _inside(offset, g * 8, 64) * _inside(_iota((32, LANES), 1) % 64 - 16, zb * 32, 128)


def _fold_mask(yb):
    below, above = (yb > 0).astype(F32), (yb < 3).astype(F32)
    return jnp.where(_iota((8, LANES), 1) < 64, below, above)


def _tall(mask, n):
    return jnp.concatenate([mask] * (n // 8), axis=0)


def _blocks(first, count, size, fn):
    n = (count - 1) // size
    if n:

        def step(i, _):
            fn(first + i * size, size)
            return 0

        lax.fori_loop(0, n, step, 0)
    fn(first + n * size, count - n * size)


def _store(ref, i, v, last):
    ref[i] = v
    if isinstance(i, int) and i == last:
        ref[i + 1] = _roll(v, 64, 1)


def _lanes():
    lane = _iota((8, LANES), 1)
    return lane < 64, lane // 16


def _pick(cond, a, b):
    if a is None and b is None:
        return None
    return jnp.where(cond, 0.0 if a is None else a, 0.0 if b is None else b)


def _turn(v, shift):
    return None if v is None else _roll(v, shift, 1)


def _unfold(groups):
    half, block = _lanes()
    vs = [
        [_pick(half, a, c) for a, c in zip(low, high)] + [_turn(_pick(half, c, a), 64) for a, c in zip(low, high)]
        for low, high in groups
    ]
    for bit in (2, 1):
        vs = [_swap_bit(v, block, bit) for v in vs]
    return [[_pick(half, v[i], v[i ^ 3]) for i in range(8)] for v in vs]


def _swap_bit(v, block, bit):
    zero = (block & bit) == 0
    out = [None] * 8
    for i in range(8):
        if not i & bit:
            x, y = v[i], v[i | bit]
            out[i] = _pick(zero, x, _turn(y, 16 * bit))
            out[i | bit] = _pick(zero, _turn(x, -16 * bit), y)
    return out


def _refold(groups):
    half, block = _lanes()
    vs = [[_pick(half, rows[i], rows[i ^ 3]) for i in range(8)] for rows in groups]
    for bit in (1, 2):
        vs = [_swap_bit(v, block, bit) for v in vs]
    turned = [{p: _turn(v[p | 4], 64) for p in (1, 2)} for v in vs]
    return [
        ([_pick(half, v[p], u[p]) for p in (1, 2)], [_pick(half, u[p], v[p]) for p in (1, 2)])
        for v, u in zip(vs, turned)
    ]


class _Own:
    def __init__(self, ref):
        self.ref = ref

    def tile(self, at):
        return self.ref[at : at + 8, :]

    def core(self, q, p, s):
        return self.tile((q - 1) * 64 + 16 * p + 8 * s)

    def outer(self, i, s):
        return self.tile(OWN_EY + 16 * i + 8 * s)

    def quads(self, i, s):
        return self.tile(OWN_COLS + 16 * i + 8 * s)


class _Sent(_Own):
    def __init__(self, ref, from_below):
        self.ref, self.first = ref, 6 if from_below else 0

    def core(self, q, p, s):
        if 2 <= q <= 7:
            return self.tile((q - 2) * 64 + 16 * p + 8 * s)
        at = OUTER + (0 if q == 1 else 48) + 8 * s
        if p in (1, 2):
            return self.tile(at + 16 * (p - 1))
        shared = self.tile(at + 32)
        if p == 0:
            return shared
        near = _iota((8, LANES), 0) // 2 == self.first // 2
        return jnp.where(near, _roll(shared, -2 if self.first else 2, 0), shared)

    def short(self, i, s):
        return _roll(self.tile(TAIL + 8 * (i // 4 * 2 + s)), self.first - 2 * (i % 4), 0)

    def outer(self, i, s):
        return self.short(i, s)

    def quads(self, i, s):
        return self.short(4 + i, s)


def _pieces(at, q, s):
    if 1 <= q <= 8:
        return [at.core(q, p, s) for p in range(4)]
    slot = 2 if q == 0 else 3
    near = [_roll(at.quads(c, s), by, 1) for c, by in ((1, 4 * (3 - slot)), (3, -4 * slot))]
    return [near[0], *(at.outer((0 if q == 0 else 2) + h, s) for h in range(2)), near[1]]


def _far_pieces(at, q, s):
    c, slot = divmod(q - 2, 4)
    return [_roll(at.quads(c, s), -4 * slot, 1), None, None, _roll(at.quads(2 + c, s), 4 * (3 - slot), 1)]


def _unpack_brick(at, mask, mask_far, fold, store, store_far):
    for batch in ([(0, 0), (1, 0)], [(2, 0), (2, 1)], [(3, 0), (3, 1)], [(4, 0), (4, 1)]):
        tasks = [(q, far, s) for q, far in batch for s in range(2)]
        groups = [
            [(_far_pieces if far else _pieces)(at, o, s) for o in (q, 9 - q)] for q, far, s in tasks
        ]
        for (q, far, s), rows in zip(tasks, _unfold(groups)):
            m = _outer_mask(mask_far if far else mask, fold, q)
            for r in range(8):
                if far:
                    store_far(s, 8 * q + r - 15, rows[r] * m)
                else:
                    store(s, 8 * q + r, rows[r] * m)


def _outer_mask(mask, fold, q):
    return mask * fold if q < 3 else mask


def _far_mask(g, zb):
    row = _iota((24, LANES), 0) - 8
    lane = _iota((24, LANES), 1) % 64
    below, above = (zb > 0).astype(F32), (zb < 3).astype(F32)
    return _inside(row, g * 8, 64) * jnp.where(lane < 4, below, jnp.where(lane >= 60, above, 0.0))


def _brick_kernel(ref, tile, far, *, at, rows):
    g, yb, zb = _position()

    def store(s, i, v):
        tile[s, i] = v

    def put(s, i, v):
        far[s, i] = v

    mask_far = _far_mask(g, zb)[rows.start - 8 : rows.stop - 8]
    _unpack_brick(at(ref), _ring_mask(g, zb)[rows], mask_far, _fold_mask(yb), store, put)
    for s in range(2):
        tile[s, FINE] = _roll(tile[s, FINE - 1], 64, 1)
        far[s, FINE - 15] = _roll(far[s, FINE - 16], 64, 1)


def _beside(s, *tiles):
    return lambda i: jnp.concatenate([t[s, i] for t in tiles], axis=0)


def _coarse_kernel(t1, t2, t3, f1, f2, f3, xm2, xp2, Ae, Ao, Be, Bo, ahead_of, raw, beyond, cs, c0, c1):
    g, yb, zb = _position()
    ring, fold = _ring_mask(g, zb), _fold_mask(yb)
    De, Do = D = [_beside(s, t1, t2, t3) for s in range(2)]
    far_e, far_o = [_beside(s, f1, f2, f3) for s in range(2)]

    row = _iota((8, LANES), 0)

    def near(i, s):
        at, r = slice(8 * (i // 2), 8 * (i // 2) + 8), 4 * s + 2 * (i % 2)
        return jnp.where(row < 4, _roll(xp2[at, :], -r, 0), _roll(xm2[at, :], 6 - r, 0))

    def ahead(q, s):
        c, slot = divmod(q - 2, 4)
        lo = _roll(near(12 + c, s), 4 * (3 - slot), 1)
        hi = _roll(near(14 + c, s), -4 * slot, 1)
        return [lo, near(2 * (q - 2), s), near(2 * (q - 2) + 1, s), hi]

    tasks = [(q, s) for q in range(2, 5) for s in range(2)]
    for (q, s), rows in zip(tasks, _unfold([(ahead(q, s), ahead(9 - q, s)) for q, s in tasks])):
        m = _outer_mask(ring[:8], fold, q)
        for r in range(8):
            _store(ahead_of.at[s], 8 * q + r, rows[r] * m, FINE - 1)

    def patch(rows, pairs):
        lane = _iota((24, LANES), 1) % 64
        sums = []
        for i in rows:
            f = 2 * i - 15
            e, o = far_e(f) + far_e(f + 1), far_o(f) + far_o(f + 1)
            sums.append((e, o, e + o, (far_e(f - 1) + far_e(f + 2)) + (far_o(f - 1) + far_o(f + 2))))
        turned = [_roll(o, 1, 0) + _roll(e, -1, 0) for e, o, _, _ in sums]
        hs = [(1.0 - 3.0 * W) * fp + W * (outer + t) for (_, _, fp, outer), t in zip(sums, turned)]
        ends = [(_roll(fp, -3, 1), _roll(fp, 2, 1)) for _, _, fp, _ in sums]
        sides = []
        for (_, _, fp, _), h, pair in zip(sums, hs, pairs):
            lo = _roll(h, -2, 1) + _roll(h, -3, 1) + W * (_roll(fp, -1, 1) + pair)
            hi = _roll(h, 2, 1) + _roll(h, 3, 1) + W * (_roll(fp, 1, 1) + pair)
            sides.append((lo, hi))
        for i, (lo, hi) in zip(rows, sides):
            low = jnp.where(lane == 0, lo, _roll(lo, 1, 1))
            high = jnp.where(lane == 63, hi, _roll(hi, -1, 1))
            beyond[i - 10] = jnp.where(lane < 32, low, high) * 0.125
        return ends

    def put_source(i, c):
        raw[i] = c

    whole = [lambda y, s=s, v=v: jnp.concatenate([ahead_of[s, y], v(y)], axis=0) for s, v in enumerate(D)]
    args = (whole, 32, W, 1.0 - 5.0 * W, None)
    _restrict(*args, 3, 7, put_source, None, 4)
    _restrict(*args, 10, 10, put_source, patch, 4)
    _sweep_three(g, yb, zb, lambda i: raw[i], lambda i: beyond[i], cs, c0, c1)
    base = [lambda i, v=v: W * v(i) for v in D]
    step_masks = _step_masks(g, yb, zb)
    _correct_and_smooth(step_masks, base, D, lambda i: c0[i], Be, Bo, 7, 13, 4)
    _smooth(step_masks, (lambda i: Be[i], lambda i: Bo[i]), D, Ae, Ao, 15, 25, 9)


def _ones_kernel(Te, To, Be, Bo, cs, c0, c1):
    g, yb, zb = _position()
    one = jnp.ones((32, LANES), F32)
    _sweep_three(g, yb, zb, lambda i: one, lambda i: one[8:], cs, c0, c1)
    step_masks = _step_masks(g, yb, zb)
    _correct_and_smooth(step_masks, None, None, lambda i: c0[i], Be, Bo, 7, 13, 4)
    _smooth(step_masks, (lambda i: Be[i], lambda i: Bo[i]), None, Te, To, 15, 25, 9)


def _sweep_three(g, yb, zb, source, beyond, cs, c0, c1):
    ring, fold = BETA * _ring_mask(g, zb), _fold_mask(yb)
    outside = ring * _tall(fold, 32)
    lane = _iota((24, LANES), 1) % 64
    has_below, has_above = (zb > 0).astype(F32), (zb < 3).astype(F32)
    row = _iota((24, LANES), 0) - 8
    z_ends = jnp.where(lane < 2, has_below, jnp.where(lane >= 62, has_above, 0.0))
    beyond_mask = BETA * z_ends * _inside(row, g * 8, 64)
    beyond_outside = beyond_mask * _tall(fold, 24)
    mask = _ring_mask(g, zb)[8:]
    masks = (mask * _tall(fold, 24), mask)

    scaled = _lazily(lambda i: source(i) * (outside if i < 12 else ring))
    for i in range(4, COARSE):
        c = scaled(i)
        after = _roll(c, 64, 1) if i == COARSE - 1 else scaled(i + 1)
        near = (_roll(c, 1, 0) + _roll(c, -1, 0) + (scaled(i - 1) + after))[8:]
        c = c[8:]
        ends = None
        if i >= 10:
            ends = beyond(i - 10) * (beyond_outside if i < 12 else beyond_mask)
        cs[i] = c
        _store(c0, i, c + _sweep(c, near, lane, ends) * masks[i >= 12], COARSE - 1)
    _sweep_rows(c0, c1, cs, 5, masks)
    _sweep_rows(c1, c0, cs, 6, masks)


def _sweep(c, near, lane, ends):
    before, after = _roll(c, 2, 1), _roll(c, -2, 1)
    if ends is not None:
        before = jnp.where(lane < 2, ends, before)
        after = jnp.where(lane >= 62, ends, after)
    return 0.2 * c + W * (near + (before + after))


def _sweep_rows(src, dst, cs, first, masks):
    for i in range(first, COARSE):
        c = src[i]
        near = _roll(c, 1, 0) + _roll(c, -1, 0) + (src[i - 1] + src[i + 1])
        _store(dst, i, cs[i] + _sweep(c, near, None, None) * masks[i >= 12], COARSE - 1)


def _restrict(fields, rows, near, centre, more, first, count, store, patch, size):
    lane = _iota((rows, LANES), 1)
    even = lane % 2 == 0

    for start in range(first, first + count, size):
        even_at, odd_at = (_lazily(lambda u, v=v, start=start: v(2 * start + u)) for v in fields)
        sums = []
        us = range(min(size, first + count - start))
        for u in us:
            y = 2 * u
            ee, eo = even_at(y) + even_at(y + 1), odd_at(y) + odd_at(y + 1)
            outer = (even_at(y - 1) + even_at(y + 2)) + (odd_at(y - 1) + odd_at(y + 2))
            sums.append((ee, eo, ee + eo, outer))
        turned = [_roll(eo, 1, 0) + _roll(ee, -1, 0) for ee, eo, _, _ in sums]
        hs = []
        for u, ((_, _, pair, outer), t) in enumerate(zip(sums, turned)):
            h = (centre + 2.0 * near) * pair + near * (outer + t)
            hs.append(h if more is None else h + more(2 * (start + u)))
        sides = [(_roll(pair, 1, 1), _roll(pair, -2, 1)) for _, _, pair, _ in sums]
        if patch is not None:
            ends = patch([start + u for u in us], [pair[8:] for _, _, pair, _ in sums])
            for u, ((before, after), (low, high)) in enumerate(zip(sides, ends)):
                low = jnp.where(lane[8:] % 64 == 0, low, before[8:])
                high = jnp.where(lane[8:] % 64 == 62, high, after[8:])
                sides[u] = (
                    jnp.concatenate([before[:8], low], axis=0),
                    jnp.concatenate([after[:8], high], axis=0),
                )
        cs = [h + _roll(h, -1, 1) + near * (before + after) for h, (before, after) in zip(hs, sides)]
        cs = [jnp.where(even, c, _roll(c, 1, 1)) * 0.125 for c in cs]
        for u, c in enumerate(cs):
            store(start + u, c)


def _step_masks(g, yb, zb):
    mask = _ring_mask(g, zb)[8:]
    masks = (mask * _tall(_fold_mask(yb), 24), mask)
    return masks, [0.2 * m for m in masks], [W * m for m in masks]


def _of_row(pair, i, own_first):
    if isinstance(i, int):
        return pair[i >= own_first]
    return jnp.where(i < own_first, *pair)


def _relax(even, odd, i, n, store, batch=2):
    for first in range(0, n, batch):
        us = range(first, min(first + batch, n))
        turned = []
        for u in us:
            e, o = even(u), odd(u)
            turned.append((_roll(e, 1, 1), _roll(e, -1, 1), _roll(o, 1, 1), _roll(o, -1, 1), _roll(o, 1, 0), _roll(e, -1, 0)))
        for u, (e1, e2, o1, o2, before, after) in zip(us, turned):
            e, o = even(u), odd(u)
            ye = ((even(u - 1) + even(u + 1)) + (e1 + e2)) + (o + before)
            yo = ((odd(u - 1) + odd(u + 1)) + (o1 + o2)) + (e + after)
            store(i + u, e, o, ye, yo)


def _smooth_to(step_masks, D, dst_e, dst_o):
    def store(i, e, o, ye, yo):
        m, n = _of_row(step_masks[1], i, 24), _of_row(step_masks[2], i, 24)
        if D is not None:
            ye, yo = ye + D[0](i), yo + D[1](i)
        _store(dst_e, i, e * m + ye * n, FINE - 1)
        _store(dst_o, i, o * m + yo * n, FINE - 1)

    return store


def _smooth(step_masks, src, D, dst_e, dst_o, first, count, size):
    def fn(i, n):
        even, odd = (_lazily(lambda u, v=v: v(i + u)) for v in src)
        _relax(even, odd, i, n, _smooth_to(step_masks, D, dst_e, dst_o))

    _blocks(first, count, size, fn)


def _correct_and_smooth(step_masks, base, D, correction, dst_e, dst_o, first, count, size):
    def fn(start, n):
        i = 2 * start
        c = _lazily(lambda u: correction(start + u))
        if base is None:
            even = odd = lambda u: c(u // 2)
        else:
            even, odd = (_lazily(lambda u, v=v: v(i + u) + c(u // 2)) for v in base)
        _relax(even, odd, i, 2 * n, _smooth_to(step_masks, D, dst_e, dst_o))

    _blocks(first, count, size, fn)


def _cycle_kernel(
    order, t1, t2, t3, Re, Ro, Te, To, part, across, pot, res, Be, Bo, cs, c0, c1, boxes, place, sem
):
    g, yb, zb = _position()
    fetch = pltpu.make_async_copy(order, place, sem.at[0])
    fetch.start()
    totals = part[...] + across[...]
    mean1 = jnp.sum(totals[0:1]) * (1.0 / CELLS)
    mean2 = jnp.sum(totals[1:2]) * (1.0 / CELLS)
    step_masks = _step_masks(g, yb, zb)
    masks = step_masks[0]

    all_of = lambda ref: lambda i: ref[i]

    De, Do = D = [_beside(s, t1, t2, t3) for s in range(2)]
    A = (lambda i: Re[i] - mean1 * Te[i], lambda i: Ro[i] - mean1 * To[i])

    def again(i, c):
        _store(cs, i, (c - mean2) * (_of_row(masks, i, 12) * BETA), COARSE - 1)

    pair_of = lambda i: (De(i) + De(i + 1)) + (Do(i) + Do(i + 1))
    _restrict(A, 24, 1.0, -5.0, pair_of, 8, 12, again, None, 4)
    _sweep_rows(cs, c0, cs, 9, masks)
    _sweep_rows(c0, c1, cs, 10, masks)
    _sweep_rows(c1, c0, cs, 11, masks)
    _correct_and_smooth(step_masks, A, D, all_of(c0), Be, Bo, 11, 9, 5)

    fetch.wait()
    box_of = [place[h, 0] for h in range(4)]
    for q in (3, 4):
        i0 = 8 * q
        even = _lazily(lambda u: Be[i0 + u])
        odd = _lazily(lambda u: Bo[i0 + u])
        left = ([], [])

        def store(i, e, o, ye, yo):
            left[0].append(t2[0, i] - (6.0 * e - ye)[8:16])
            left[1].append(t2[1, i] - (6.0 * o - yo)[8:16])

        _relax(even, odd, i0, 8, store)
        tasks = [(f, s) for f in range(2) for s in range(2)]
        done = [[v(u)[8:16] for u in range(8)] for v in (even, odd)]
        groups = [(done, left)[f][s] for f, s in tasks]
        for (f, s), sides in zip(tasks, _refold(groups)):
            for o, pieces in zip((q - 3, 6 - q), sides):
                for h in range(2):
                    at = BLOCK * ((f * 4 + o) * 2 + h) + s
                    boxes[pl.ds(at, 8, stride=2), :] = pieces[h]
    for f, out in enumerate((pot, res)):
        for o in range(4):
            for h in range(2):
                v = _blk(boxes, (f * 4 + o) * 2 + h)
                out[box_of[(o // 2) * 2 + h], :, (o % 2) * LANES : (o % 2 + 1) * LANES] = v


def _lazily(fn):
    made = {}

    def get(u):
        if u not in made:
            made[u] = fn(u)
        return made[u]

    return get


def _shape(*dims):
    return jax.ShapeDtypeStruct(dims, F32)


def _rows(n):
    return _shape(n, LANES)


VMEM = pl.BlockSpec(memory_space=pltpu.VMEM)
HBM = pl.BlockSpec(memory_space=pltpu.HBM)


def _call(kernel, specs, outs, scratch=(), us=0.1, grant=40.0):
    return pl.pallas_call(
        kernel,
        out_shape=outs,
        in_specs=specs,
        out_specs=[VMEM] * len(outs),
        scratch_shapes=scratch,
        cost_estimate=pl.CostEstimate(flops=0, transcendentals=0, bytes_accessed=int(us * 3.5e6)),
        compiler_params=pltpu.CompilerParams(vmem_limit_bytes=int(grant * 2**20)),
    )


def _y_shift(n):
    return [(4 * y + z, 4 * ((y + n) % 4) + z) for y in range(4) for z in range(4)]


def _z_shift(n):
    return [(4 * y + z, 4 * y + (z + n) % 4) for y in range(4) for z in range(4)]


def _x_shift(n):
    return [(x, (x + n) % 8) for x in range(8)]


def _body(weights, divergence, box_coords, neighbors):
    coords = box_coords.T
    raw, weight = _call(
        _fetch_kernel,
        [HBM, HBM],
        [_shape(*divergence.shape), _shape(*weights.shape[1:])],
        [pltpu.SemaphoreType.DMA((2,))],
        us=1.0,
        grant=53.79,
    )(divergence, weights)
    own, sums, order = _call(
        _sort_kernel,
        [VMEM] * 3,
        [_rows(128), _rows(8), jax.ShapeDtypeStruct((8, LANES), jnp.int32)],
        [pltpu.VMEM((128, LANES), F32)],
    )(coords, raw, weight)
    across = lax.ppermute(sums, "dev", _y_shift(2))
    up, down = _call(_y_kernel, [VMEM] * 2, [_rows(Y_MESSAGE), _rows(Y_MESSAGE)])(own, sums)
    below = lax.ppermute(up, "dev", _y_shift(1))
    above = lax.ppermute(down, "dev", _y_shift(-1))

    plane = pltpu.VMEM((COARSE + 1, 24, LANES), F32)
    fine = _shape(FINE + 1, 24, LANES)
    inner = pltpu.VMEM((FINE + 1, 24, LANES), F32)
    ones = _call(_ones_kernel, [], [fine, fine], [inner, inner, plane, plane, plane], us=1.0)()
    sums, ones = lax.optimization_barrier((sums, ones))
    total = _call(_total_kernel, [VMEM] * 4, [_rows(8)])(sums, below, above, across)[0]
    zacross = lax.ppermute(total, "dev", _z_shift(2))
    up, down = _call(_z_kernel, [VMEM] * 4, [_rows(168), _rows(168)])(own, below, above, total)
    zbelow = lax.ppermute(up, "dev", _z_shift(1))
    zabove = lax.ppermute(down, "dev", _z_shift(-1))

    mine, up, down, high, low, part = _call(
        _x_kernel,
        [VMEM] * 7,
        [_rows(640), _rows(MESSAGE), _rows(MESSAGE), _rows(72), _rows(72), _rows(8)],
    )(own, below, above, zbelow, zabove, total, zacross)
    xm1 = lax.ppermute(up, "grp", _x_shift(1))
    xp1 = lax.ppermute(down, "grp", _x_shift(-1))
    xm2 = lax.ppermute(high, "grp", _x_shift(2))
    xp2 = lax.ppermute(low, "grp", _x_shift(-2))
    bricks = []
    for ref, at, rows in (
        (xm1, functools.partial(_Sent, from_below=True), slice(8, 16)),
        (mine, _Own, slice(16, 24)),
        (xp1, functools.partial(_Sent, from_below=False), slice(24, 32)),
    ):
        kernel = functools.partial(_brick_kernel, at=at, rows=rows)
        outs = [_shape(2, FINE + 1, 8, LANES), _shape(2, 26, 8, LANES)]
        bricks.append(_call(kernel, [VMEM], outs, us=0.8)(ref))
    part, bricks = lax.optimization_barrier((part, bricks))
    tiles, fars = zip(*bricks)
    part, send = _call(_window_kernel, [VMEM] * 5, [_rows(8), _rows(8)])(part, xm1, xp1, xm2, xp2)
    xacross = lax.ppermute(send, "grp", [(x, (x + 3 - 6 * (x % 2)) % 8) for x in range(8)])

    start = _call(
        _coarse_kernel,
        [VMEM] * 8,
        [fine, fine],
        [
            inner,
            inner,
            pltpu.VMEM((2, FINE + 1, 8, LANES), F32),
            pltpu.VMEM((COARSE, 32, LANES), F32),
            pltpu.VMEM((12, 24, LANES), F32),
            plane,
            plane,
            plane,
        ],
        us=3,
    )(*tiles, *fars, xm2, xp2)

    boxes = pltpu.VMEM((16 * BLOCK, LANES), F32)
    pot, res = _call(
        _cycle_kernel,
        [VMEM] * 10,
        [_shape(4, 16, 256), _shape(4, 16, 256)],
        [inner, inner, plane, plane, plane, boxes, pltpu.SMEM((8, LANES), jnp.int32), pltpu.SemaphoreType.DMA((1,))],
    )(order, *tiles, *start, *ones, part, xacross)
    return pot, res


def solution(mesh):
    table = _mean_weights()

    def body(divergence, box_coords, neighbors):
        return _body(jnp.asarray(table), divergence, box_coords, neighbors)

    split = P(("grp", "dev"), None, None)
    return jax.shard_map(
        body, mesh=mesh, in_specs=(split, P(), P()), out_specs=(split, split), check_vma=False
    )
```

```python
import functools

import numpy as np

import jax
import jax.numpy as jnp
from jax import lax
from jax.experimental import pallas as pl
from jax.experimental.pallas import tpu as pltpu
from jax.sharding import PartitionSpec as P

KC = 4
CYCLES = 2
W = 0.8 / 6.0
BETA = 0.8 / 1.5
CELLS = 128**3
BLOCK = 16
LANES = 128
F32 = jnp.float32


def _apply(v):
    total = 6.0 * v
    for axis in range(3):
        lo = [slice(None)] * 3
        hi = [slice(None)] * 3
        lo[axis], hi[axis] = slice(None, -1), slice(1, None)
        total[tuple(lo)] -= v[tuple(hi)]
        total[tuple(hi)] -= v[tuple(lo)]
    return total


def _mean_weights():
    ones = np.ones((128, 128, 128))
    relax = lambda v: v - W * _apply(v)
    k0 = _apply(ones)
    k1 = relax(k0)
    k2 = relax(k1)
    q = k2.reshape(64, 2, 64, 2, 64, 2).sum(axis=(1, 3, 5))
    s = np.zeros_like(q)
    for _ in range(KC):
        s = s + BETA * (q - 0.25 * _apply(s))
    back = np.repeat(np.repeat(np.repeat(s, 2, 0), 2, 1), 2, 2) / 8.0
    full = ones - W * (k0 + k1 + k2) - relax(back) + (s.sum() / CELLS) * relax(ones)
    blocks = []
    for x in (0, 3, 7):
        for y in (0, 1, 3):
            for z in (0, 1, 3):
                b = full[16 * x : 16 * x + 16, 32 * y : 32 * y + 32, 32 * z : 32 * z + 32]
                b = b.reshape(16, 4, 8, 2, 16).transpose(1, 3, 0, 2, 4)
                blocks.append(b.reshape(8, 16, LANES))
    return np.stack(blocks).astype(np.float32)


def _iota(shape, dim):
    return lax.broadcasted_iota(jnp.int32, shape, dim)


def _roll(v, shift, axis):
    shift = shift % v.shape[axis]
    return v if shift == 0 else pltpu.roll(v, shift, axis)


def _position():
    d = lax.axis_index("dev")
    return lax.axis_index("grp"), d // 4, d % 4


def _blk(ref, i):
    return ref[BLOCK * i : BLOCK * (i + 1), :]


def _put(ref, i, v):
    ref[BLOCK * i : BLOCK * (i + 1), :] = v


def _fetch_kernel(div, w2, raw, weight, sem):
    g, yb, zb = _position()
    kind = lambda i, n: jnp.where(i == 0, 0, jnp.where(i == n - 1, 2, 1))
    which = kind(g, 8) * 9 + kind(yb, 4) * 3 + kind(zb, 4)
    copies = (
        pltpu.make_async_copy(div, raw, sem.at[0]),
        pltpu.make_async_copy(w2.at[which], weight, sem.at[1]),
    )
    for copy in copies:
        copy.start()
    for copy in copies:
        copy.wait()


def _sort_kernel(coords, raw, weight, own, sums, order, plain):
    g, yb, zb = _position()
    row = _iota((16, LANES), 0)
    lane = _iota((16, LANES), 1)
    j, k = lane // 16, lane % 16
    edge_x = ((row == 0) & (g == 0)).astype(F32) + ((row == 15) & (g == 7)).astype(F32)
    s1 = jnp.zeros((16, LANES), F32)
    s2 = jnp.zeros((16, LANES), F32)
    box_of = _box_of(coords, g, yb, zb)
    row8 = _iota((8, LANES), 0)
    order[...] = sum(jnp.where(row8 == h, box_of[h], 0) for h in range(4))
    for o in range(4):
        for h in range(2):
            v = raw[box_of[(o // 2) * 2 + h], :, (o % 2) * LANES : (o % 2 + 1) * LANES]
            at = BLOCK * (o * 2 + h)
            plain[at : at + BLOCK, :] = v
            edge = edge_x
            if o == 0:
                edge += ((j == 0) & (yb == 0)).astype(F32)
            if o == 3:
                edge += ((j == 7) & (yb == 3)).astype(F32)
            if h == 0:
                edge += ((k == 0) & (zb == 0)).astype(F32)
            else:
                edge += ((k == 15) & (zb == 3)).astype(F32)
            s1 += (1.0 - W * edge) * v
            s2 += weight[o * 2 + h] * v
    for i in range(16):
        own[8 * i : 8 * i + 8, :] = plain[pl.ds(BLOCK * (i // 2) + i % 2, 8, stride=2), :]
    s1, s2 = (jnp.sum(v, axis=0, keepdims=True) for v in (s1, s2))
    sums[...] = jnp.where(row8 == 0, s1, jnp.where(row8 == 1, s2, 0.0))


def _box_of(coords, g, yb, zb):
    mine = (g * 4 + yb) * 4 + zb
    at = pl.ds(pl.multiple_of(mine // 32 * LANES, LANES), LANES)
    slot = coords[1:2, at] % 2 * 2 + coords[2:3, at] % 2
    box = _iota((1, LANES), 1) - mine % 32 * 4
    inside = (box >= 0) & (box < 4)
    return [jnp.sum(jnp.where(inside & (slot == h), box, 0)) for h in range(4)]


def _ext(own, below, above, q, h):
    if q == 0:
        return _roll(_blk(below, 4), 64 * h, 1)
    if q < 3:
        return _blk(below, (q - 1) * 2 + h)
    if q < 7:
        return _blk(own, (q - 3) * 2 + h)
    if q < 9:
        return _blk(above, (q - 7) * 2 + h)
    return _roll(_blk(above, 4), 64 * h, 1)


def _pack_quads(pieces, src_quad):
    quad = _iota(pieces[0].shape, 1) % 16 // 4
    out = _roll(pieces[0], 4 * (0 - src_quad), 1)
    for s in range(1, len(pieces)):
        out = jnp.where(quad == s, _roll(pieces[s], 4 * (s - src_quad), 1), out)
    return out


Y_FAR, Y_SUMS, Y_MESSAGE = 64, 80, 88


def _y_kernel(own, sums, up, down):
    half = _iota((BLOCK, LANES), 1) < 64
    for i in range(4):
        _put(up, i, _blk(own, i + 4))
        _put(down, i, _blk(own, i))
    _put(up, 4, jnp.where(half, _roll(_blk(own, 3), 64, 1), _blk(own, 2)))
    _put(down, 4, jnp.where(half, _blk(own, 4), _roll(_blk(own, 5), 64, 1)))
    for ref in (up, down):
        ref[Y_SUMS:Y_MESSAGE, :] = sums[...]


def _total_kernel(sums, below, above, across, total):
    total[...] = sums[...] + below[Y_SUMS:Y_MESSAGE, :] + above[Y_SUMS:Y_MESSAGE, :] + across[...]


def _z_kernel(own, below, above, total, up, down):
    ext = lambda q, h: _ext(own, below, above, q, h)
    for q in range(1, 9):
        _put(up, q - 1, ext(q, 1))
        _put(down, q - 1, ext(q, 0))
    for ref, near, quad in ((up, 1, 3), (down, 0, 0)):
        far = [ext(q, 1 - near) for q in range(2, 8)]
        _put(ref, 8, _pack_quads(far[:4], quad))
        _put(ref, 9, _pack_quads([*far[4:], ext(0, near), ext(9, near)], quad))
        ref[160:168, :] = total[...]


OUTER, SUMS, MESSAGE = 384, 480, 488
OWN_EY, OWN_COLS = 512, 576


def _rows_to(pieces):
    row = _iota((8, LANES), 0)
    out = None
    for i, (v, r) in enumerate(pieces):
        v = _roll(v, 2 * i - r, 0)
        out = v if out is None else jnp.where(row < 2 * i, out, v)
    return out


def _rows_far(near):
    return _iota((8, LANES), 0) // 2 == (0 if near else 3)


def _lower_lanes():
    return _iota((8, LANES), 1) % 16 < 8


def _hide(v, tile, near):
    return jnp.where(_rows_far(near), _roll(v, 2 if near else -2, 0), tile)


def _share(lo, hi, near):
    row, lane = _iota((8, LANES), 0), _iota((8, LANES), 1)
    middle = jnp.where(lane % 16 < 8, hi, lo)
    edge = jnp.where((row // 2) == near // 2, lo, _roll(hi, 2 if near else -2, 0))
    return jnp.where((row >= 2) & (row < 6), middle, edge)


def _x_kernel(own, below, above, zbelow, zabove, total, across, mine, up, down, high, low, part):
    ext = lambda q, h: _ext(own, below, above, q, h)
    extra = [ext(q, h) for q in (0, 9) for h in range(2)]
    extra += [_blk(zbelow, 8), _blk(zbelow, 9), _blk(zabove, 8), _blk(zabove, 9)]
    for i, v in enumerate(extra):
        _put(mine, 32 + i, v)
    two_away = []
    for q in range(1, 9):
        pieces = (_blk(zbelow, q - 1), ext(q, 0), ext(q, 1), _blk(zabove, q - 1))
        for p in range(4):
            _put(mine, (q - 1) * 4 + p, pieces[p])
        if 2 <= q <= 7:
            two_away += pieces[1:3]
            for ref, near in ((up, 6), (down, 0)):
                for p in (1, 2):
                    _put(ref, (q - 2) * 4 + p, pieces[p])
                for s in (0, 8):
                    lo, hi = (pieces[p][s : s + 8] for p in (0, 3))
                    far = _rows_far(near)
                    at = (q - 2) * 64 + s
                    ref[at : at + 8, :] = jnp.where(far & _lower_lanes(), hi, lo)
                    ref[at + 48 : at + 56, :] = _hide(extra[q - 2][s : s + 8], hi, near)
            continue
        at = OUTER + (0 if q == 1 else 48)
        for ref, near in ((up, 6), (down, 0)):
            for s in (0, 8):
                hidden = extra[6 if q == 1 else 7][s : s + 8]
                ref[at + s : at + s + 8, :] = _hide(hidden, pieces[1][s : s + 8], near)
            ref[at + 16 : at + 32, :] = pieces[2]
            for s in (0, 8):
                ref[at + 32 + s : at + 40 + s, :] = _share(pieces[0][s : s + 8], pieces[3][s : s + 8], near)
    for src, quad in ((zbelow, 3), (zabove, 0)):
        near = [_blk(src, q - 1) for q in range(2, 8)]
        two_away += [_pack_quads(near[:4], quad), _pack_quads(near[4:], quad)]
    for ref, r in ((high, 6), (low, 0)):
        for i in range(0, 16, 2):
            a, b = two_away[i : i + 2]
            ref[4 * i : 4 * i + 8, :] = _rows_to([(a[:8], r), (b[:8], r), (a[8:], r), (b[8:], r)])
    t = total[...] + zbelow[160:168, :] + zabove[160:168, :] + across[...]
    part[...] = t
    for ref, at in ((up, SUMS), (down, SUMS), (high, 64), (low, 64)):
        ref[at : at + 8, :] = t


def _window_kernel(mine, xm1, xp1, xm2, xp2, out, send):
    odd = _position()[0] % 2 == 1
    low = xm1[SUMS:MESSAGE, :] + xm2[64:72, :]
    high = xp1[SUMS:MESSAGE, :] + xp2[64:72, :]
    out[...] = mine[...] + (low + high)
    send[...] = mine[...] + jnp.where(odd, high, low)


FINE, COARSE = 40, 20


def _inside(pos, start, limit):
    return ((pos + start >= 0) & (pos + start < limit)).astype(F32)


def _ring_mask(g, zb):
    row = _iota((32, LANES), 0)
    offset = jnp.where(row < 4, row + 16, row - 16)
    return _inside(offset, g * 8, 64) * _inside(_iota((32, LANES), 1) % 64 - 16, zb * 32, 128)


def _fold_mask(yb):
    below, above = (yb > 0).astype(F32), (yb < 3).astype(F32)
    return jnp.where(_iota((8, LANES), 1) < 64, below, above)


def _tall(mask, n):
    return jnp.concatenate([mask] * (n // 8), axis=0)


def _blocks(first, count, size, fn):
    n = (count - 1) // size
    if n:

        def step(i, _):
            fn(first + i * size, size)
            return 0

        lax.fori_loop(0, n, step, 0)
    fn(first + n * size, count - n * size)


def _store(ref, i, v, last):
    ref[i] = v
    if isinstance(i, int) and i == last:
        ref[i + 1] = _roll(v, 64, 1)


def _lanes():
    lane = _iota((8, LANES), 1)
    return lane < 64, lane // 16


def _pick(cond, a, b):
    if a is None and b is None:
        return None
    return jnp.where(cond, 0.0 if a is None else a, 0.0 if b is None else b)


def _turn(v, shift):
    return None if v is None else _roll(v, shift, 1)


def _unfold(groups):
    half, block = _lanes()
    vs = [
        [_pick(half, a, c) for a, c in zip(low, high)] + [_turn(_pick(half, c, a), 64) for a, c in zip(low, high)]
        for low, high in groups
    ]
    for bit in (2, 1):
        vs = [_swap_bit(v, block, bit) for v in vs]
    return [[_pick(half, v[i], v[i ^ 3]) for i in range(8)] for v in vs]


def _swap_bit(v, block, bit):
    zero = (block & bit) == 0
    out = [None] * 8
    for i in range(8):
        if not i & bit:
            x, y = v[i], v[i | bit]
            out[i] = _pick(zero, x, _turn(y, 16 * bit))
            out[i | bit] = _pick(zero, _turn(x, -16 * bit), y)
    return out


def _refold(groups):
    half, block = _lanes()
    vs = [[_pick(half, rows[i], rows[i ^ 3]) for i in range(8)] for rows in groups]
    for bit in (1, 2):
        vs = [_swap_bit(v, block, bit) for v in vs]
    turned = [{p: _turn(v[p | 4], 64) for p in (1, 2)} for v in vs]
    return [
        ([_pick(half, v[p], u[p]) for p in (1, 2)], [_pick(half, u[p], v[p]) for p in (1, 2)])
        for v, u in zip(vs, turned)
    ]


class _Own:
    def __init__(self, ref):
        self.ref = ref

    def tile(self, at):
        return self.ref[at : at + 8, :]

    def core(self, q, p, s):
        return self.tile((q - 1) * 64 + 16 * p + 8 * s)

    def outer(self, i, s):
        return self.tile(OWN_EY + 16 * i + 8 * s)

    def quads(self, i, s):
        return self.tile(OWN_COLS + 16 * i + 8 * s)


class _Sent(_Own):
    def __init__(self, ref, from_below):
        self.ref, self.first = ref, 6 if from_below else 0

    def core(self, q, p, s):
        if 2 <= q <= 7:
            v = self.tile((q - 2) * 64 + 16 * p + 8 * s)
            return jnp.where(_rows_far(self.first), self.core(q, 0, s), v) if p == 3 else v
        at = OUTER + (0 if q == 1 else 48) + 8 * s
        if p in (1, 2):
            return self.tile(at + 16 * (p - 1))
        shared = self.tile(at + 32)
        if p == 0:
            return shared
        near = _iota((8, LANES), 0) // 2 == self.first // 2
        return jnp.where(near, _roll(shared, -2 if self.first else 2, 0), shared)

    def short(self, i, s):
        at = i * 64 + 48 if i < 6 else OUTER + 48 * (i - 6)
        return _roll(self.tile(at + 8 * s), -2 if self.first else 2, 0)

    def outer(self, i, s):
        return self.short(i, s)

    def quads(self, i, s):
        return self.short(4 + i, s)


def _pieces(at, q, s):
    if 1 <= q <= 8:
        return [at.core(q, p, s) for p in range(4)]
    slot = 2 if q == 0 else 3
    near = [_roll(at.quads(c, s), by, 1) for c, by in ((1, 4 * (3 - slot)), (3, -4 * slot))]
    return [near[0], *(at.outer((0 if q == 0 else 2) + h, s) for h in range(2)), near[1]]


def _far_pieces(at, q, s):
    c, slot = divmod(q - 2, 4)
    return [_roll(at.quads(c, s), -4 * slot, 1), None, None, _roll(at.quads(2 + c, s), 4 * (3 - slot), 1)]


def _unpack_brick(at, mask, mask_far, fold, store, store_far):
    for batch in ([(0, 0), (1, 0), (2, 0)], [(3, 0), (4, 0), (2, 1)], [(3, 1), (4, 1)]):
        tasks = [(q, far, s) for q, far in batch for s in range(2)]
        groups = [
            [(_far_pieces if far else _pieces)(at, o, s) for o in (q, 9 - q)] for q, far, s in tasks
        ]
        for (q, far, s), rows in zip(tasks, _unfold(groups)):
            m = _outer_mask(mask_far if far else mask, fold, q)
            for r in range(8):
                if far:
                    store_far(s, 8 * q + r - 15, rows[r] * m)
                else:
                    store(s, 8 * q + r, rows[r] * m)


def _outer_mask(mask, fold, q):
    return mask * fold if q < 3 else mask


def _far_mask(g, zb):
    row = _iota((24, LANES), 0) - 8
    lane = _iota((24, LANES), 1) % 64
    below, above = (zb > 0).astype(F32), (zb < 3).astype(F32)
    return _inside(row, g * 8, 64) * jnp.where(lane < 4, below, jnp.where(lane >= 60, above, 0.0))


def _brick_kernel(ref, tile, far, *, at, rows):
    g, yb, zb = _position()

    def store(s, i, v):
        tile[s, i] = v

    def put(s, i, v):
        far[s, i] = v

    mask_far = _far_mask(g, zb)[rows.start - 8 : rows.stop - 8]
    _unpack_brick(at(ref), _ring_mask(g, zb)[rows], mask_far, _fold_mask(yb), store, put)
    for s in range(2):
        tile[s, FINE] = _roll(tile[s, FINE - 1], 64, 1)
        far[s, FINE - 15] = _roll(far[s, FINE - 16], 64, 1)


def _beside(s, *tiles):
    return lambda i: jnp.concatenate([t[s, i] for t in tiles], axis=0)


def _coarse_kernel(t1, t2, t3, f1, f2, f3, xm2, xp2, Ae, Ao, Be, Bo, ahead_of, raw, beyond, cs, c0, c1):
    g, yb, zb = _position()
    ring, fold = _ring_mask(g, zb), _fold_mask(yb)
    De, Do = D = [_beside(s, t1, t2, t3) for s in range(2)]
    far_e, far_o = [_beside(s, f1, f2, f3) for s in range(2)]

    row = _iota((8, LANES), 0)

    def near(i, s):
        at, r = slice(8 * (i // 2), 8 * (i // 2) + 8), 4 * s + 2 * (i % 2)
        return jnp.where(row < 4, _roll(xp2[at, :], -r, 0), _roll(xm2[at, :], 6 - r, 0))

    def ahead(q, s):
        c, slot = divmod(q - 2, 4)
        lo = _roll(near(12 + c, s), 4 * (3 - slot), 1)
        hi = _roll(near(14 + c, s), -4 * slot, 1)
        return [lo, near(2 * (q - 2), s), near(2 * (q - 2) + 1, s), hi]

    tasks = [(q, s) for q in range(2, 5) for s in range(2)]
    for (q, s), rows in zip(tasks, _unfold([(ahead(q, s), ahead(9 - q, s)) for q, s in tasks])):
        m = _outer_mask(ring[:8], fold, q)
        for r in range(8):
            _store(ahead_of.at[s], 8 * q + r, rows[r] * m, FINE - 1)

    def patch(rows, pairs):
        lane = _iota((24, LANES), 1) % 64
        sums = []
        for i in rows:
            f = 2 * i - 15
            e, o = far_e(f) + far_e(f + 1), far_o(f) + far_o(f + 1)
            sums.append((e, o, e + o, (far_e(f - 1) + far_e(f + 2)) + (far_o(f - 1) + far_o(f + 2))))
        turned = [_roll(o, 1, 0) + _roll(e, -1, 0) for e, o, _, _ in sums]
        hs = [(1.0 - 3.0 * W) * fp + W * (outer + t) for (_, _, fp, outer), t in zip(sums, turned)]
        ends = [(_roll(fp, -3, 1), _roll(fp, 2, 1)) for _, _, fp, _ in sums]
        sides = []
        for (_, _, fp, _), h, pair in zip(sums, hs, pairs):
            lo = _roll(h, -2, 1) + _roll(h, -3, 1) + W * (_roll(fp, -1, 1) + pair)
            hi = _roll(h, 2, 1) + _roll(h, 3, 1) + W * (_roll(fp, 1, 1) + pair)
            sides.append((lo, hi))
        for i, (lo, hi) in zip(rows, sides):
            low = jnp.where(lane == 0, lo, _roll(lo, 1, 1))
            high = jnp.where(lane == 63, hi, _roll(hi, -1, 1))
            beyond[i - 10] = jnp.where(lane < 32, low, high) * 0.125
        return ends

    def put_source(i, c):
        raw[i] = c

    whole = [lambda y, s=s, v=v: jnp.concatenate([ahead_of[s, y], v(y)], axis=0) for s, v in enumerate(D)]
    args = (whole, 32, W, 1.0 - 5.0 * W, None)
    _restrict(*args, 3, 7, put_source, None, 7)
    _restrict(*args, 10, 10, put_source, patch, 5)
    _sweep_three(g, yb, zb, lambda i: raw[i], lambda i: beyond[i], cs, c0, c1)
    base = [lambda i, v=v: W * v(i) for v in D]
    step_masks = _step_masks(g, yb, zb)
    _correct_and_smooth(step_masks, base, D, lambda i: c0[i], Be, Bo, 7, 13, 4)
    _smooth(step_masks, (lambda i: Be[i], lambda i: Bo[i]), D, Ae, Ao, 15, 25, 9)


def _ones_kernel(Te, To, Be, Bo, cs, c0, c1):
    g, yb, zb = _position()
    one = jnp.ones((32, LANES), F32)
    _sweep_three(g, yb, zb, lambda i: one, lambda i: one[8:], cs, c0, c1)
    step_masks = _step_masks(g, yb, zb)
    _correct_and_smooth(step_masks, None, None, lambda i: c0[i], Be, Bo, 7, 13, 4)
    _smooth(step_masks, (lambda i: Be[i], lambda i: Bo[i]), None, Te, To, 15, 25, 9)


def _sweep_three(g, yb, zb, source, beyond, cs, c0, c1):
    ring, fold = BETA * _ring_mask(g, zb), _fold_mask(yb)
    outside = ring * _tall(fold, 32)
    lane = _iota((24, LANES), 1) % 64
    has_below, has_above = (zb > 0).astype(F32), (zb < 3).astype(F32)
    row = _iota((24, LANES), 0) - 8
    z_ends = jnp.where(lane < 2, has_below, jnp.where(lane >= 62, has_above, 0.0))
    beyond_mask = BETA * z_ends * _inside(row, g * 8, 64)
    beyond_outside = beyond_mask * _tall(fold, 24)
    mask = _ring_mask(g, zb)[8:]
    masks = (mask * _tall(fold, 24), mask)

    scaled = _lazily(lambda i: source(i) * (outside if i < 12 else ring))
    for i in range(4, COARSE):
        c = scaled(i)
        after = _roll(c, 64, 1) if i == COARSE - 1 else scaled(i + 1)
        near = (_roll(c, 1, 0) + _roll(c, -1, 0) + (scaled(i - 1) + after))[8:]
        c = c[8:]
        ends = None
        if i >= 10:
            ends = beyond(i - 10) * (beyond_outside if i < 12 else beyond_mask)
        cs[i] = c
        _store(c0, i, c + _sweep(c, near, lane, ends) * masks[i >= 12], COARSE - 1)
    _sweep_rows(c0, c1, cs, 5, masks)
    _sweep_rows(c1, c0, cs, 6, masks)


def _sweep(c, near, lane, ends):
    before, after = _roll(c, 2, 1), _roll(c, -2, 1)
    if ends is not None:
        before = jnp.where(lane < 2, ends, before)
        after = jnp.where(lane >= 62, ends, after)
    return 0.2 * c + W * (near + (before + after))


def _sweep_rows(src, dst, cs, first, masks):
    for i in range(first, COARSE):
        c = src[i]
        near = _roll(c, 1, 0) + _roll(c, -1, 0) + (src[i - 1] + src[i + 1])
        _store(dst, i, cs[i] + _sweep(c, near, None, None) * masks[i >= 12], COARSE - 1)


def _restrict(fields, rows, near, centre, more, first, count, store, patch, size):
    lane = _iota((rows, LANES), 1)
    even = lane % 2 == 0

    for start in range(first, first + count, size):
        even_at, odd_at = (_lazily(lambda u, v=v, start=start: v(2 * start + u)) for v in fields)
        sums = []
        us = range(min(size, first + count - start))
        for u in us:
            y = 2 * u
            ee, eo = even_at(y) + even_at(y + 1), odd_at(y) + odd_at(y + 1)
            outer = (even_at(y - 1) + even_at(y + 2)) + (odd_at(y - 1) + odd_at(y + 2))
            sums.append((ee, eo, ee + eo, outer))
        turned = [_roll(eo, 1, 0) + _roll(ee, -1, 0) for ee, eo, _, _ in sums]
        hs = []
        for u, ((_, _, pair, outer), t) in enumerate(zip(sums, turned)):
            h = (centre + 2.0 * near) * pair + near * (outer + t)
            hs.append(h if more is None else h + more(2 * (start + u)))
        sides = [(_roll(pair, 1, 1), _roll(pair, -2, 1)) for _, _, pair, _ in sums]
        if patch is not None:
            ends = patch([start + u for u in us], [pair[8:] for _, _, pair, _ in sums])
            for u, ((before, after), (low, high)) in enumerate(zip(sides, ends)):
                low = jnp.where(lane[8:] % 64 == 0, low, before[8:])
                high = jnp.where(lane[8:] % 64 == 62, high, after[8:])
                sides[u] = (
                    jnp.concatenate([before[:8], low], axis=0),
                    jnp.concatenate([after[:8], high], axis=0),
                )
        cs = [h + _roll(h, -1, 1) + near * (before + after) for h, (before, after) in zip(hs, sides)]
        cs = [jnp.where(even, c, _roll(c, 1, 1)) * 0.125 for c in cs]
        for u, c in enumerate(cs):
            store(start + u, c)


def _step_masks(g, yb, zb):
    mask = _ring_mask(g, zb)[8:]
    masks = (mask * _tall(_fold_mask(yb), 24), mask)
    return masks, [0.2 * m for m in masks], [W * m for m in masks]


def _of_row(pair, i, own_first):
    if isinstance(i, int):
        return pair[i >= own_first]
    return jnp.where(i < own_first, *pair)


def _relax(even, odd, i, n, store, batch=3):
    for first in range(0, n, batch):
        us = range(first, min(first + batch, n))
        turned = []
        for u in us:
            e, o = even(u), odd(u)
            turned.append((_roll(e, 1, 1), _roll(e, -1, 1), _roll(o, 1, 1), _roll(o, -1, 1), _roll(o, 1, 0), _roll(e, -1, 0)))
        for u, (e1, e2, o1, o2, before, after) in zip(us, turned):
            e, o = even(u), odd(u)
            ye = ((even(u - 1) + even(u + 1)) + (e1 + e2)) + (o + before)
            yo = ((odd(u - 1) + odd(u + 1)) + (o1 + o2)) + (e + after)
            store(i + u, e, o, ye, yo)


def _smooth_to(step_masks, D, dst_e, dst_o):
    def store(i, e, o, ye, yo):
        m, n = _of_row(step_masks[1], i, 24), _of_row(step_masks[2], i, 24)
        if D is not None:
            ye, yo = ye + D[0](i), yo + D[1](i)
        _store(dst_e, i, e * m + ye * n, FINE - 1)
        _store(dst_o, i, o * m + yo * n, FINE - 1)

    return store


def _smooth(step_masks, src, D, dst_e, dst_o, first, count, size):
    def fn(i, n):
        even, odd = (_lazily(lambda u, v=v: v(i + u)) for v in src)
        _relax(even, odd, i, n, _smooth_to(step_masks, D, dst_e, dst_o))

    _blocks(first, count, size, fn)


def _correct_and_smooth(step_masks, base, D, correction, dst_e, dst_o, first, count, size):
    def fn(start, n):
        i = 2 * start
        c = _lazily(lambda u: correction(start + u))
        if base is None:
            even = odd = lambda u: c(u // 2)
        else:
            even, odd = (_lazily(lambda u, v=v: v(i + u) + c(u // 2)) for v in base)
        _relax(even, odd, i, 2 * n, _smooth_to(step_masks, D, dst_e, dst_o))

    _blocks(first, count, size, fn)


def _cycle_kernel(
    order, t1, t2, t3, Re, Ro, Te, To, part, across, pot, res, Be, Bo, cs, c0, c1, boxes, place, sem
):
    g, yb, zb = _position()
    fetch = pltpu.make_async_copy(order, place, sem.at[0])
    fetch.start()
    totals = part[...] + across[...]
    mean1 = jnp.sum(totals[0:1]) * (1.0 / CELLS)
    mean2 = jnp.sum(totals[1:2]) * (1.0 / CELLS)
    step_masks = _step_masks(g, yb, zb)
    masks = step_masks[0]

    all_of = lambda ref: lambda i: ref[i]

    De, Do = D = [_beside(s, t1, t2, t3) for s in range(2)]
    A = (lambda i: Re[i] - mean1 * Te[i], lambda i: Ro[i] - mean1 * To[i])

    def again(i, c):
        _store(cs, i, (c - mean2) * (_of_row(masks, i, 12) * BETA), COARSE - 1)

    pair_of = lambda i: (De(i) + De(i + 1)) + (Do(i) + Do(i + 1))
    _restrict(A, 24, 1.0, -5.0, pair_of, 8, 12, again, None, 6)
    _sweep_rows(cs, c0, cs, 9, masks)
    _sweep_rows(c0, c1, cs, 10, masks)
    _sweep_rows(c1, c0, cs, 11, masks)
    _correct_and_smooth(step_masks, A, D, all_of(c0), Be, Bo, 11, 9, 5)

    fetch.wait()
    box_of = [place[h, 0] for h in range(4)]
    for q in (3, 4):
        i0 = 8 * q
        even = _lazily(lambda u: Be[i0 + u])
        odd = _lazily(lambda u: Bo[i0 + u])
        left = ([], [])

        def store(i, e, o, ye, yo):
            left[0].append(t2[0, i] - (6.0 * e - ye)[8:16])
            left[1].append(t2[1, i] - (6.0 * o - yo)[8:16])

        _relax(even, odd, i0, 8, store)
        tasks = [(f, s) for f in range(2) for s in range(2)]
        done = [[v(u)[8:16] for u in range(8)] for v in (even, odd)]
        groups = [(done, left)[f][s] for f, s in tasks]
        for (f, s), sides in zip(tasks, _refold(groups)):
            for o, pieces in zip((q - 3, 6 - q), sides):
                for h in range(2):
                    at = BLOCK * ((f * 4 + o) * 2 + h) + s
                    boxes[pl.ds(at, 8, stride=2), :] = pieces[h]
    for f, out in enumerate((pot, res)):
        for o in range(4):
            for h in range(2):
                v = _blk(boxes, (f * 4 + o) * 2 + h)
                out[box_of[(o // 2) * 2 + h], :, (o % 2) * LANES : (o % 2 + 1) * LANES] = v


def _lazily(fn):
    made = {}

    def get(u):
        if u not in made:
            made[u] = fn(u)
        return made[u]

    return get


def _shape(*dims):
    return jax.ShapeDtypeStruct(dims, F32)


def _rows(n):
    return _shape(n, LANES)


VMEM = pl.BlockSpec(memory_space=pltpu.VMEM)
HBM = pl.BlockSpec(memory_space=pltpu.HBM)


def _call(kernel, specs, outs, scratch=(), us=0.1, grant=40.0):
    return pl.pallas_call(
        kernel,
        out_shape=outs,
        in_specs=specs,
        out_specs=[VMEM] * len(outs),
        scratch_shapes=scratch,
        cost_estimate=pl.CostEstimate(flops=0, transcendentals=0, bytes_accessed=int(us * 3.5e6)),
        compiler_params=pltpu.CompilerParams(vmem_limit_bytes=int(grant * 2**20)),
    )


def _y_shift(n):
    return [(4 * y + z, 4 * ((y + n) % 4) + z) for y in range(4) for z in range(4)]


def _z_shift(n):
    return [(4 * y + z, 4 * y + (z + n) % 4) for y in range(4) for z in range(4)]


def _x_shift(n):
    return [(x, (x + n) % 8) for x in range(8)]


def _body(weights, divergence, box_coords, neighbors):
    coords = box_coords.T
    raw, weight = _call(
        _fetch_kernel,
        [HBM, HBM],
        [_shape(*divergence.shape), _shape(*weights.shape[1:])],
        [pltpu.SemaphoreType.DMA((2,))],
        us=1.0,
        grant=53.79,
    )(divergence, weights)
    own, sums, order = _call(
        _sort_kernel,
        [VMEM] * 3,
        [_rows(128), _rows(8), jax.ShapeDtypeStruct((8, LANES), jnp.int32)],
        [pltpu.VMEM((128, LANES), F32)],
    )(coords, raw, weight)
    across = lax.ppermute(sums, "dev", _y_shift(2))
    up, down = _call(_y_kernel, [VMEM] * 2, [_rows(Y_MESSAGE), _rows(Y_MESSAGE)])(own, sums)
    below = lax.ppermute(up, "dev", _y_shift(1))
    above = lax.ppermute(down, "dev", _y_shift(-1))

    plane = pltpu.VMEM((COARSE + 1, 24, LANES), F32)
    fine = _shape(FINE + 1, 24, LANES)
    inner = pltpu.VMEM((FINE + 1, 24, LANES), F32)
    ones = _call(_ones_kernel, [], [fine, fine], [inner, inner, plane, plane, plane], us=1.0)()
    sums, ones = lax.optimization_barrier((sums, ones))
    total = _call(_total_kernel, [VMEM] * 4, [_rows(8)])(sums, below, above, across)[0]
    zacross = lax.ppermute(total, "dev", _z_shift(2))
    up, down = _call(_z_kernel, [VMEM] * 4, [_rows(168), _rows(168)])(own, below, above, total)
    zbelow = lax.ppermute(up, "dev", _z_shift(1))
    zabove = lax.ppermute(down, "dev", _z_shift(-1))

    mine, up, down, high, low, part = _call(
        _x_kernel,
        [VMEM] * 7,
        [_rows(640), _rows(MESSAGE), _rows(MESSAGE), _rows(72), _rows(72), _rows(8)],
    )(own, below, above, zbelow, zabove, total, zacross)
    xm1 = lax.ppermute(up, "grp", _x_shift(1))
    xp1 = lax.ppermute(down, "grp", _x_shift(-1))
    xm2 = lax.ppermute(high, "grp", _x_shift(2))
    xp2 = lax.ppermute(low, "grp", _x_shift(-2))
    bricks = []
    for ref, at, rows in (
        (xm1, functools.partial(_Sent, from_below=True), slice(8, 16)),
        (mine, _Own, slice(16, 24)),
        (xp1, functools.partial(_Sent, from_below=False), slice(24, 32)),
    ):
        kernel = functools.partial(_brick_kernel, at=at, rows=rows)
        outs = [_shape(2, FINE + 1, 8, LANES), _shape(2, 26, 8, LANES)]
        bricks.append(_call(kernel, [VMEM], outs, us=0.8)(ref))
    part, bricks = lax.optimization_barrier((part, bricks))
    tiles, fars = zip(*bricks)
    part, send = _call(_window_kernel, [VMEM] * 5, [_rows(8), _rows(8)])(part, xm1, xp1, xm2, xp2)
    xacross = lax.ppermute(send, "grp", [(x, (x + 3 - 6 * (x % 2)) % 8) for x in range(8)])

    start = _call(
        _coarse_kernel,
        [VMEM] * 8,
        [fine, fine],
        [
            inner,
            inner,
            pltpu.VMEM((2, FINE + 1, 8, LANES), F32),
            pltpu.VMEM((COARSE, 32, LANES), F32),
            pltpu.VMEM((12, 24, LANES), F32),
            plane,
            plane,
            plane,
        ],
        us=3,
    )(*tiles, *fars, xm2, xp2)

    boxes = pltpu.VMEM((16 * BLOCK, LANES), F32)
    pot, res = _call(
        _cycle_kernel,
        [VMEM] * 10,
        [_shape(4, 16, 256), _shape(4, 16, 256)],
        [inner, inner, plane, plane, plane, boxes, pltpu.SMEM((8, LANES), jnp.int32), pltpu.SemaphoreType.DMA((1,))],
    )(order, *tiles, *start, *ones, part, xacross)
    return pot, res


def solution(mesh):
    table = _mean_weights()

    def body(divergence, box_coords, neighbors):
        return _body(jnp.asarray(table), divergence, box_coords, neighbors)

    split = P(("grp", "dev"), None, None)
    return jax.shard_map(
        body, mesh=mesh, in_specs=(split, P(), P()), out_specs=(split, split), check_vma=False
    )
```

```python
import functools

import numpy as np

import jax
import jax.numpy as jnp
from jax import lax
from jax.experimental import pallas as pl
from jax.experimental.pallas import tpu as pltpu
from jax.sharding import PartitionSpec as P

KC = 4
CYCLES = 2
W = 0.8 / 6.0
BETA = 0.8 / 1.5
CELLS = 128**3
BLOCK = 16
LANES = 128
F32 = jnp.float32


def _apply(v):
    total = 6.0 * v
    for axis in range(3):
        lo = [slice(None)] * 3
        hi = [slice(None)] * 3
        lo[axis], hi[axis] = slice(None, -1), slice(1, None)
        total[tuple(lo)] -= v[tuple(hi)]
        total[tuple(hi)] -= v[tuple(lo)]
    return total


def _mean_weights():
    ones = np.ones((128, 128, 128))
    relax = lambda v: v - W * _apply(v)
    k0 = _apply(ones)
    k1 = relax(k0)
    k2 = relax(k1)
    q = k2.reshape(64, 2, 64, 2, 64, 2).sum(axis=(1, 3, 5))
    s = np.zeros_like(q)
    for _ in range(KC):
        s = s + BETA * (q - 0.25 * _apply(s))
    back = np.repeat(np.repeat(np.repeat(s, 2, 0), 2, 1), 2, 2) / 8.0
    full = ones - W * (k0 + k1 + k2) - relax(back) + (s.sum() / CELLS) * relax(ones)
    blocks = []
    for x in (0, 3, 7):
        for y in (0, 1, 3):
            for z in (0, 1, 3):
                b = full[16 * x : 16 * x + 16, 32 * y : 32 * y + 32, 32 * z : 32 * z + 32]
                b = b.reshape(16, 4, 8, 2, 16).transpose(1, 3, 0, 2, 4)
                blocks.append(b.reshape(8, 16, LANES))
    return np.stack(blocks).astype(np.float32)


def _iota(shape, dim):
    return lax.broadcasted_iota(jnp.int32, shape, dim)


def _roll(v, shift, axis):
    shift = shift % v.shape[axis]
    return v if shift == 0 else pltpu.roll(v, shift, axis)


def _position():
    d = lax.axis_index("dev")
    return lax.axis_index("grp"), d // 4, d % 4


def _blk(ref, i):
    return ref[BLOCK * i : BLOCK * (i + 1), :]


def _put(ref, i, v):
    ref[BLOCK * i : BLOCK * (i + 1), :] = v


def _fetch_kernel(div, w2, raw, weight, sem):
    g, yb, zb = _position()
    kind = lambda i, n: jnp.where(i == 0, 0, jnp.where(i == n - 1, 2, 1))
    which = kind(g, 8) * 9 + kind(yb, 4) * 3 + kind(zb, 4)
    copies = (
        pltpu.make_async_copy(div, raw, sem.at[0]),
        pltpu.make_async_copy(w2.at[which], weight, sem.at[1]),
    )
    for copy in copies:
        copy.start()
    for copy in copies:
        copy.wait()


def _sort_kernel(coords, raw, weight, own, sums, order, plain):
    g, yb, zb = _position()
    row = _iota((16, LANES), 0)
    lane = _iota((16, LANES), 1)
    j, k = lane // 16, lane % 16
    edge_x = ((row == 0) & (g == 0)).astype(F32) + ((row == 15) & (g == 7)).astype(F32)
    s1 = jnp.zeros((16, LANES), F32)
    s2 = jnp.zeros((16, LANES), F32)
    box_of = _box_of(coords, g, yb, zb)
    row8 = _iota((8, LANES), 0)
    order[...] = sum(jnp.where(row8 == h, box_of[h], 0) for h in range(4))
    for o in range(4):
        for h in range(2):
            v = raw[box_of[(o // 2) * 2 + h], :, (o % 2) * LANES : (o % 2 + 1) * LANES]
            at = BLOCK * (o * 2 + h)
            plain[at : at + BLOCK, :] = v
            edge = edge_x
            if o == 0:
                edge += ((j == 0) & (yb == 0)).astype(F32)
            if o == 3:
                edge += ((j == 7) & (yb == 3)).astype(F32)
            if h == 0:
                edge += ((k == 0) & (zb == 0)).astype(F32)
            else:
                edge += ((k == 15) & (zb == 3)).astype(F32)
            s1 += (1.0 - W * edge) * v
            s2 += weight[o * 2 + h] * v
    for i in range(16):
        own[8 * i : 8 * i + 8, :] = plain[pl.ds(BLOCK * (i // 2) + i % 2, 8, stride=2), :]
    s1, s2 = (jnp.sum(v, axis=0, keepdims=True) for v in (s1, s2))
    sums[...] = jnp.where(row8 == 0, s1, jnp.where(row8 == 1, s2, 0.0))


def _box_of(coords, g, yb, zb):
    mine = (g * 4 + yb) * 4 + zb
    at = pl.ds(pl.multiple_of(mine // 32 * LANES, LANES), LANES)
    slot = coords[1:2, at] % 2 * 2 + coords[2:3, at] % 2
    box = _iota((1, LANES), 1) - mine % 32 * 4
    inside = (box >= 0) & (box < 4)
    return [jnp.sum(jnp.where(inside & (slot == h), box, 0)) for h in range(4)]


def _ext(own, below, above, q, h):
    if q == 0:
        return _roll(_blk(below, 4), 64 * h, 1)
    if q < 3:
        return _blk(below, (q - 1) * 2 + h)
    if q < 7:
        return _blk(own, (q - 3) * 2 + h)
    if q < 9:
        return _blk(above, (q - 7) * 2 + h)
    return _roll(_blk(above, 4), 64 * h, 1)


def _pack_quads(pieces, src_quad):
    quad = _iota(pieces[0].shape, 1) % 16 // 4
    out = _roll(pieces[0], 4 * (0 - src_quad), 1)
    for s in range(1, len(pieces)):
        out = jnp.where(quad == s, _roll(pieces[s], 4 * (s - src_quad), 1), out)
    return out


Y_FAR, Y_SUMS, Y_MESSAGE = 64, 80, 88


def _y_kernel(own, sums, up, down):
    half = _iota((BLOCK, LANES), 1) < 64
    for i in range(4):
        _put(up, i, _blk(own, i + 4))
        _put(down, i, _blk(own, i))
    _put(up, 4, jnp.where(half, _roll(_blk(own, 3), 64, 1), _blk(own, 2)))
    _put(down, 4, jnp.where(half, _blk(own, 4), _roll(_blk(own, 5), 64, 1)))
    for ref in (up, down):
        ref[Y_SUMS:Y_MESSAGE, :] = sums[...]


def _total_kernel(sums, below, above, across, total):
    total[...] = sums[...] + below[Y_SUMS:Y_MESSAGE, :] + above[Y_SUMS:Y_MESSAGE, :] + across[...]


def _z_kernel(own, below, above, total, up, down):
    ext = lambda q, h: _ext(own, below, above, q, h)
    for q in range(1, 9):
        _put(up, q - 1, ext(q, 1))
        _put(down, q - 1, ext(q, 0))
    for ref, near, quad in ((up, 1, 3), (down, 0, 0)):
        far = [ext(q, 1 - near) for q in range(2, 8)]
        _put(ref, 8, _pack_quads(far[:4], quad))
        _put(ref, 9, _pack_quads([*far[4:], ext(0, near), ext(9, near)], quad))
        ref[160:168, :] = total[...]


OUTER, SUMS, MESSAGE = 384, 480, 488
OWN_EY, OWN_COLS = 512, 576


def _rows_to(pieces):
    row = _iota((8, LANES), 0)
    out = None
    for i, (v, r) in enumerate(pieces):
        v = _roll(v, 2 * i - r, 0)
        out = v if out is None else jnp.where(row < 2 * i, out, v)
    return out


def _rows_far(near):
    return _iota((8, LANES), 0) // 2 == (0 if near else 3)


def _lower_lanes():
    return _iota((8, LANES), 1) % 16 < 8


def _hide(v, tile, near):
    return jnp.where(_rows_far(near), _roll(v, 2 if near else -2, 0), tile)


def _share(lo, hi, near):
    row, lane = _iota((8, LANES), 0), _iota((8, LANES), 1)
    middle = jnp.where(lane % 16 < 8, hi, lo)
    edge = jnp.where((row // 2) == near // 2, lo, _roll(hi, 2 if near else -2, 0))
    return jnp.where((row >= 2) & (row < 6), middle, edge)


def _x_kernel(own, below, above, zbelow, zabove, total, across, mine, up, down, high, low, part):
    ext = lambda q, h: _ext(own, below, above, q, h)
    extra = [ext(q, h) for q in (0, 9) for h in range(2)]
    extra += [_blk(zbelow, 8), _blk(zbelow, 9), _blk(zabove, 8), _blk(zabove, 9)]
    for i, v in enumerate(extra):
        _put(mine, 32 + i, v)
    two_away = []
    for q in range(1, 9):
        pieces = (_blk(zbelow, q - 1), ext(q, 0), ext(q, 1), _blk(zabove, q - 1))
        for p in range(4):
            _put(mine, (q - 1) * 4 + p, pieces[p])
        if 2 <= q <= 7:
            two_away += pieces[1:3]
            for ref, near in ((up, 6), (down, 0)):
                for p in (1, 2):
                    _put(ref, (q - 2) * 4 + p, pieces[p])
                for s in (0, 8):
                    lo, hi = (pieces[p][s : s + 8] for p in (0, 3))
                    far = _rows_far(near)
                    at = (q - 2) * 64 + s
                    ref[at : at + 8, :] = jnp.where(far & _lower_lanes(), hi, lo)
                    ref[at + 48 : at + 56, :] = _hide(extra[q - 2][s : s + 8], hi, near)
            continue
        at = OUTER + (0 if q == 1 else 48)
        for ref, near in ((up, 6), (down, 0)):
            for s in (0, 8):
                hidden = extra[6 if q == 1 else 7][s : s + 8]
                ref[at + s : at + s + 8, :] = _hide(hidden, pieces[1][s : s + 8], near)
            ref[at + 16 : at + 32, :] = pieces[2]
            for s in (0, 8):
                ref[at + 32 + s : at + 40 + s, :] = _share(pieces[0][s : s + 8], pieces[3][s : s + 8], near)
    for src, quad in ((zbelow, 3), (zabove, 0)):
        near = [_blk(src, q - 1) for q in range(2, 8)]
        two_away += [_pack_quads(near[:4], quad), _pack_quads(near[4:], quad)]
    for ref, r in ((high, 6), (low, 0)):
        for i in range(0, 16, 2):
            a, b = two_away[i : i + 2]
            ref[4 * i : 4 * i + 8, :] = _rows_to([(a[:8], r), (b[:8], r), (a[8:], r), (b[8:], r)])
    t = total[...] + zbelow[160:168, :] + zabove[160:168, :] + across[...]
    part[...] = t
    for ref, at in ((up, SUMS), (down, SUMS), (high, 64), (low, 64)):
        ref[at : at + 8, :] = t


def _window_kernel(mine, xm1, xp1, xm2, xp2, out, send):
    odd = _position()[0] % 2 == 1
    low = xm1[SUMS:MESSAGE, :] + xm2[64:72, :]
    high = xp1[SUMS:MESSAGE, :] + xp2[64:72, :]
    out[...] = mine[...] + (low + high)
    send[...] = mine[...] + jnp.where(odd, high, low)


FINE, COARSE = 40, 20


def _inside(pos, start, limit):
    return ((pos + start >= 0) & (pos + start < limit)).astype(F32)


def _ring_mask(g, zb):
    row = _iota((32, LANES), 0)
    offset = jnp.where(row < 4, row + 16, row - 16)
    return _inside(offset, g * 8, 64) * _inside(_iota((32, LANES), 1) % 64 - 16, zb * 32, 128)


def _fold_mask(yb):
    below, above = (yb > 0).astype(F32), (yb < 3).astype(F32)
    return jnp.where(_iota((8, LANES), 1) < 64, below, above)


def _tall(mask, n):
    return jnp.concatenate([mask] * (n // 8), axis=0)


def _blocks(first, count, size, fn):
    n = (count - 1) // size
    if n:

        def step(i, _):
            fn(first + i * size, size)
            return 0

        lax.fori_loop(0, n, step, 0)
    fn(first + n * size, count - n * size)


def _store(ref, i, v, last):
    ref[i] = v
    if isinstance(i, int) and i == last:
        ref[i + 1] = _roll(v, 64, 1)


def _lanes():
    lane = _iota((8, LANES), 1)
    return lane < 64, lane // 16


def _pick(cond, a, b):
    if a is None and b is None:
        return None
    return jnp.where(cond, 0.0 if a is None else a, 0.0 if b is None else b)


def _turn(v, shift):
    return None if v is None else _roll(v, shift, 1)


def _unfold(groups):
    half, block = _lanes()
    vs = [
        [_pick(half, a, c) for a, c in zip(low, high)] + [_turn(_pick(half, c, a), 64) for a, c in zip(low, high)]
        for low, high in groups
    ]
    for bit in (2, 1):
        vs = [_swap_bit(v, block, bit) for v in vs]
    return [[_pick(half, v[i], v[i ^ 3]) for i in range(8)] for v in vs]


def _swap_bit(v, block, bit):
    zero = (block & bit) == 0
    out = [None] * 8
    for i in range(8):
        if not i & bit:
            x, y = v[i], v[i | bit]
            out[i] = _pick(zero, x, _turn(y, 16 * bit))
            out[i | bit] = _pick(zero, _turn(x, -16 * bit), y)
    return out


def _refold(groups):
    half, block = _lanes()
    vs = [[_pick(half, rows[i], rows[i ^ 3]) for i in range(8)] for rows in groups]
    for bit in (1, 2):
        vs = [_swap_bit(v, block, bit) for v in vs]
    turned = [{p: _turn(v[p | 4], 64) for p in (1, 2)} for v in vs]
    return [
        ([_pick(half, v[p], u[p]) for p in (1, 2)], [_pick(half, u[p], v[p]) for p in (1, 2)])
        for v, u in zip(vs, turned)
    ]


class _Own:
    def __init__(self, ref):
        self.ref = ref

    def tile(self, at):
        return self.ref[at : at + 8, :]

    def core(self, q, p, s):
        return self.tile((q - 1) * 64 + 16 * p + 8 * s)

    def outer(self, i, s):
        return self.tile(OWN_EY + 16 * i + 8 * s)

    def quads(self, i, s):
        return self.tile(OWN_COLS + 16 * i + 8 * s)


class _Sent(_Own):
    def __init__(self, ref, from_below):
        self.ref, self.first = ref, 6 if from_below else 0

    def core(self, q, p, s):
        if 2 <= q <= 7:
            v = self.tile((q - 2) * 64 + 16 * p + 8 * s)
            return jnp.where(_rows_far(self.first), self.core(q, 0, s), v) if p == 3 else v
        at = OUTER + (0 if q == 1 else 48) + 8 * s
        if p in (1, 2):
            return self.tile(at + 16 * (p - 1))
        shared = self.tile(at + 32)
        if p == 0:
            return shared
        near = _iota((8, LANES), 0) // 2 == self.first // 2
        return jnp.where(near, _roll(shared, -2 if self.first else 2, 0), shared)

    def short(self, i, s):
        at = i * 64 + 48 if i < 6 else OUTER + 48 * (i - 6)
        return _roll(self.tile(at + 8 * s), -2 if self.first else 2, 0)

    def outer(self, i, s):
        return self.short(i, s)

    def quads(self, i, s):
        return self.short(4 + i, s)


def _pieces(at, q, s):
    if 1 <= q <= 8:
        return [at.core(q, p, s) for p in range(4)]
    slot = 2 if q == 0 else 3
    near = [_roll(at.quads(c, s), by, 1) for c, by in ((1, 4 * (3 - slot)), (3, -4 * slot))]
    return [near[0], *(at.outer((0 if q == 0 else 2) + h, s) for h in range(2)), near[1]]


def _far_pieces(at, q, s):
    c, slot = divmod(q - 2, 4)
    return [_roll(at.quads(c, s), -4 * slot, 1), None, None, _roll(at.quads(2 + c, s), 4 * (3 - slot), 1)]


def _unpack_brick(at, mask, mask_far, fold, store, store_far):
    for batch in ([(0, 0), (1, 0), (2, 0)], [(3, 0), (4, 0), (2, 1)], [(3, 1), (4, 1)]):
        tasks = [(q, far, s) for q, far in batch for s in range(2)]
        groups = [
            [(_far_pieces if far else _pieces)(at, o, s) for o in (q, 9 - q)] for q, far, s in tasks
        ]
        for (q, far, s), rows in zip(tasks, _unfold(groups)):
            m = _outer_mask(mask_far if far else mask, fold, q)
            for r in range(8):
                if far:
                    store_far(s, 8 * q + r - 15, rows[r] * m)
                else:
                    store(s, 8 * q + r, rows[r] * m)


def _outer_mask(mask, fold, q):
    return mask * fold if q < 3 else mask


def _far_mask(g, zb):
    row = _iota((24, LANES), 0) - 8
    lane = _iota((24, LANES), 1) % 64
    below, above = (zb > 0).astype(F32), (zb < 3).astype(F32)
    return _inside(row, g * 8, 64) * jnp.where(lane < 4, below, jnp.where(lane >= 60, above, 0.0))


def _brick_kernel(ref, tile, far, *, at, rows):
    g, yb, zb = _position()

    def store(s, i, v):
        tile[s, i] = v

    def put(s, i, v):
        far[s, i] = v

    mask_far = _far_mask(g, zb)[rows.start - 8 : rows.stop - 8]
    _unpack_brick(at(ref), _ring_mask(g, zb)[rows], mask_far, _fold_mask(yb), store, put)
    for s in range(2):
        tile[s, FINE] = _roll(tile[s, FINE - 1], 64, 1)
        far[s, FINE - 15] = _roll(far[s, FINE - 16], 64, 1)


def _beside(s, *tiles):
    return lambda i: jnp.concatenate([t[s, i] for t in tiles], axis=0)


def _coarse_kernel(t1, t2, t3, f1, f2, f3, xm2, xp2, Ae, Ao, Be, Bo, ahead_of, raw, beyond, cs, c0, c1):
    g, yb, zb = _position()
    ring, fold = _ring_mask(g, zb), _fold_mask(yb)
    De, Do = D = [_beside(s, t1, t2, t3) for s in range(2)]
    far_e, far_o = [_beside(s, f1, f2, f3) for s in range(2)]

    row = _iota((8, LANES), 0)

    def near(i, s):
        at, r = slice(8 * (i // 2), 8 * (i // 2) + 8), 4 * s + 2 * (i % 2)
        return jnp.where(row < 4, _roll(xp2[at, :], -r, 0), _roll(xm2[at, :], 6 - r, 0))

    def ahead(q, s):
        c, slot = divmod(q - 2, 4)
        lo = _roll(near(12 + c, s), 4 * (3 - slot), 1)
        hi = _roll(near(14 + c, s), -4 * slot, 1)
        return [lo, near(2 * (q - 2), s), near(2 * (q - 2) + 1, s), hi]

    tasks = [(q, s) for q in range(2, 5) for s in range(2)]
    for (q, s), rows in zip(tasks, _unfold([(ahead(q, s), ahead(9 - q, s)) for q, s in tasks])):
        m = _outer_mask(ring[:8], fold, q)
        for r in range(8):
            _store(ahead_of.at[s], 8 * q + r, rows[r] * m, FINE - 1)

    def patch(rows, pairs):
        lane = _iota((24, LANES), 1) % 64
        sums = []
        for i in rows:
            f = 2 * i - 15
            e, o = far_e(f) + far_e(f + 1), far_o(f) + far_o(f + 1)
            sums.append((e, o, e + o, (far_e(f - 1) + far_e(f + 2)) + (far_o(f - 1) + far_o(f + 2))))
        turned = [_roll(o, 1, 0) + _roll(e, -1, 0) for e, o, _, _ in sums]
        hs = [(1.0 - 3.0 * W) * fp + W * (outer + t) for (_, _, fp, outer), t in zip(sums, turned)]
        ends = [(_roll(fp, -3, 1), _roll(fp, 2, 1)) for _, _, fp, _ in sums]
        sides = []
        for (_, _, fp, _), h, pair in zip(sums, hs, pairs):
            lo = _roll(h, -2, 1) + _roll(h, -3, 1) + W * (_roll(fp, -1, 1) + pair)
            hi = _roll(h, 2, 1) + _roll(h, 3, 1) + W * (_roll(fp, 1, 1) + pair)
            sides.append((lo, hi))
        for i, (lo, hi) in zip(rows, sides):
            low = jnp.where(lane == 0, lo, _roll(lo, 1, 1))
            high = jnp.where(lane == 63, hi, _roll(hi, -1, 1))
            beyond[i - 10] = jnp.where(lane < 32, low, high) * 0.125
        return ends

    def put_source(i, c):
        raw[i] = c

    whole = [lambda y, s=s, v=v: jnp.concatenate([ahead_of[s, y], v(y)], axis=0) for s, v in enumerate(D)]
    args = (whole, 32, W, 1.0 - 5.0 * W, None)
    _restrict(*args, 3, 7, put_source, None, 7)
    _restrict(*args, 10, 10, put_source, patch, 5)
    _sweep_three(g, yb, zb, lambda i: raw[i], lambda i: beyond[i], cs, c0, c1)
    base = [lambda i, v=v: W * v(i) for v in D]
    step_masks = _step_masks(g, yb, zb)
    _correct_and_smooth(step_masks, base, D, lambda i: c0[i], Be, Bo, 7, 13, 4)
    _smooth(step_masks, (lambda i: Be[i], lambda i: Bo[i]), D, Ae, Ao, 15, 25, 9)


def _ones_kernel(Te, To, Be, Bo, cs, c0, c1):
    g, yb, zb = _position()
    one = jnp.ones((32, LANES), F32)
    _sweep_three(g, yb, zb, lambda i: one, lambda i: one[8:], cs, c0, c1)
    step_masks = _step_masks(g, yb, zb)
    _correct_and_smooth(step_masks, None, None, lambda i: c0[i], Be, Bo, 7, 13, 4)
    _smooth(step_masks, (lambda i: Be[i], lambda i: Bo[i]), None, Te, To, 15, 25, 9)


def _sweep_three(g, yb, zb, source, beyond, cs, c0, c1):
    ring, fold = BETA * _ring_mask(g, zb), _fold_mask(yb)
    outside = ring * _tall(fold, 32)
    lane = _iota((24, LANES), 1) % 64
    has_below, has_above = (zb > 0).astype(F32), (zb < 3).astype(F32)
    row = _iota((24, LANES), 0) - 8
    z_ends = jnp.where(lane < 2, has_below, jnp.where(lane >= 62, has_above, 0.0))
    beyond_mask = BETA * z_ends * _inside(row, g * 8, 64)
    beyond_outside = beyond_mask * _tall(fold, 24)
    mask = _ring_mask(g, zb)[8:]
    masks = (mask * _tall(fold, 24), mask)

    scaled = _lazily(lambda i: source(i) * (outside if i < 12 else ring))
    for i in range(4, COARSE):
        c = scaled(i)
        after = _roll(c, 64, 1) if i == COARSE - 1 else scaled(i + 1)
        near = (_roll(c, 1, 0) + _roll(c, -1, 0) + (scaled(i - 1) + after))[8:]
        c = c[8:]
        ends = None
        if i >= 10:
            ends = beyond(i - 10) * (beyond_outside if i < 12 else beyond_mask)
        cs[i] = c
        turns = _roll(c, 2, 1), _roll(c, -2, 1)
        _store(c0, i, c + _sweep(c, near, turns, lane, ends) * masks[i >= 12], COARSE - 1)
    _sweep_rows(c0, c1, cs, 5, masks)
    _sweep_rows(c1, c0, cs, 6, masks)


def _sweep(c, near, turns, lane, ends):
    before, after = turns
    if ends is not None:
        before = jnp.where(lane < 2, ends, before)
        after = jnp.where(lane >= 62, ends, after)
    return 0.2 * c + W * (near + (before + after))


def _sweep_rows(src, dst, cs, first, masks, batch=4):
    for start in range(first, COARSE, batch):
        rows = range(start, min(start + batch, COARSE))
        turned = [
            (_roll(src[i], 1, 0), _roll(src[i], -1, 0), _roll(src[i], 2, 1), _roll(src[i], -2, 1)) for i in rows
        ]
        for i, (low, high, *turns) in zip(rows, turned):
            near = (low + high) + (src[i - 1] + src[i + 1])
            _store(dst, i, cs[i] + _sweep(src[i], near, turns, None, None) * masks[i >= 12], COARSE - 1)


def _restrict(fields, rows, near, centre, more, first, count, store, patch, size):
    lane = _iota((rows, LANES), 1)
    even = lane % 2 == 0

    for start in range(first, first + count, size):
        even_at, odd_at = (_lazily(lambda u, v=v, start=start: v(2 * start + u)) for v in fields)
        sums = []
        us = range(min(size, first + count - start))
        for u in us:
            y = 2 * u
            ee, eo = even_at(y) + even_at(y + 1), odd_at(y) + odd_at(y + 1)
            outer = (even_at(y - 1) + even_at(y + 2)) + (odd_at(y - 1) + odd_at(y + 2))
            sums.append((ee, eo, ee + eo, outer))
        turned = [_roll(eo, 1, 0) + _roll(ee, -1, 0) for ee, eo, _, _ in sums]
        hs = []
        for u, ((_, _, pair, outer), t) in enumerate(zip(sums, turned)):
            h = (centre + 2.0 * near) * pair + near * (outer + t)
            hs.append(h if more is None else h + more(2 * (start + u)))
        sides = [(_roll(pair, 1, 1), _roll(pair, -2, 1)) for _, _, pair, _ in sums]
        if patch is not None:
            ends = patch([start + u for u in us], [pair[8:] for _, _, pair, _ in sums])
            for u, ((before, after), (low, high)) in enumerate(zip(sides, ends)):
                low = jnp.where(lane[8:] % 64 == 0, low, before[8:])
                high = jnp.where(lane[8:] % 64 == 62, high, after[8:])
                sides[u] = (
                    jnp.concatenate([before[:8], low], axis=0),
                    jnp.concatenate([after[:8], high], axis=0),
                )
        cs = [h + _roll(h, -1, 1) + near * (before + after) for h, (before, after) in zip(hs, sides)]
        cs = [jnp.where(even, c, _roll(c, 1, 1)) * 0.125 for c in cs]
        for u, c in enumerate(cs):
            store(start + u, c)


def _step_masks(g, yb, zb):
    mask = _ring_mask(g, zb)[8:]
    masks = (mask * _tall(_fold_mask(yb), 24), mask)
    return masks, [0.2 * m for m in masks], [W * m for m in masks]


def _of_row(pair, i, own_first):
    if isinstance(i, int):
        return pair[i >= own_first]
    return jnp.where(i < own_first, *pair)


def _relax(even, odd, i, n, store, batch=3):
    for first in range(0, n, batch):
        us = range(first, min(first + batch, n))
        turned = []
        for u in us:
            e, o = even(u), odd(u)
            turned.append((_roll(e, 1, 1), _roll(e, -1, 1), _roll(o, 1, 1), _roll(o, -1, 1), _roll(o, 1, 0), _roll(e, -1, 0)))
        for u, (e1, e2, o1, o2, before, after) in zip(us, turned):
            e, o = even(u), odd(u)
            ye = ((even(u - 1) + even(u + 1)) + (e1 + e2)) + (o + before)
            yo = ((odd(u - 1) + odd(u + 1)) + (o1 + o2)) + (e + after)
            store(i + u, e, o, ye, yo)


def _smooth_to(step_masks, D, dst_e, dst_o):
    def store(i, e, o, ye, yo):
        m, n = _of_row(step_masks[1], i, 24), _of_row(step_masks[2], i, 24)
        if D is not None:
            ye, yo = ye + D[0](i), yo + D[1](i)
        _store(dst_e, i, e * m + ye * n, FINE - 1)
        _store(dst_o, i, o * m + yo * n, FINE - 1)

    return store


def _smooth(step_masks, src, D, dst_e, dst_o, first, count, size):
    def fn(i, n):
        even, odd = (_lazily(lambda u, v=v: v(i + u)) for v in src)
        _relax(even, odd, i, n, _smooth_to(step_masks, D, dst_e, dst_o))

    _blocks(first, count, size, fn)


def _correct_and_smooth(step_masks, base, D, correction, dst_e, dst_o, first, count, size):
    def fn(start, n):
        i = 2 * start
        c = _lazily(lambda u: correction(start + u))
        if base is None:
            even = odd = lambda u: c(u // 2)
        else:
            even, odd = (_lazily(lambda u, v=v: v(i + u) + c(u // 2)) for v in base)
        _relax(even, odd, i, 2 * n, _smooth_to(step_masks, D, dst_e, dst_o))

    _blocks(first, count, size, fn)


def _cycle_kernel(
    order, t1, t2, t3, Re, Ro, Te, To, part, across, pot, res, Be, Bo, cs, c0, c1, boxes, place, sem
):
    g, yb, zb = _position()
    fetch = pltpu.make_async_copy(order, place, sem.at[0])
    fetch.start()
    totals = part[...] + across[...]
    means = jnp.sum(totals, axis=1, keepdims=True) * (1.0 / CELLS)
    mean1 = jnp.broadcast_to(means[0:1], (24, LANES))
    mean2 = jnp.broadcast_to(means[1:2], (24, LANES))
    step_masks = _step_masks(g, yb, zb)
    masks = step_masks[0]

    all_of = lambda ref: lambda i: ref[i]

    De, Do = D = [_beside(s, t1, t2, t3) for s in range(2)]
    A = (lambda i: Re[i] - mean1 * Te[i], lambda i: Ro[i] - mean1 * To[i])

    def again(i, c):
        _store(cs, i, (c - mean2) * (_of_row(masks, i, 12) * BETA), COARSE - 1)

    pair_of = lambda i: (De(i) + De(i + 1)) + (Do(i) + Do(i + 1))
    _restrict(A, 24, 1.0, -5.0, pair_of, 8, 12, again, None, 6)
    _sweep_rows(cs, c0, cs, 9, masks)
    _sweep_rows(c0, c1, cs, 10, masks)
    _sweep_rows(c1, c0, cs, 11, masks)
    _correct_and_smooth(step_masks, A, D, all_of(c0), Be, Bo, 11, 9, 5)

    fetch.wait()
    box_of = [place[h, 0] for h in range(4)]
    for q in (3, 4):
        i0 = 8 * q
        even = _lazily(lambda u: Be[i0 + u])
        odd = _lazily(lambda u: Bo[i0 + u])
        left = ([], [])

        def store(i, e, o, ye, yo):
            left[0].append(t2[0, i] - (6.0 * e - ye)[8:16])
            left[1].append(t2[1, i] - (6.0 * o - yo)[8:16])

        _relax(even, odd, i0, 8, store)
        tasks = [(f, s) for f in range(2) for s in range(2)]
        done = [[v(u)[8:16] for u in range(8)] for v in (even, odd)]
        groups = [(done, left)[f][s] for f, s in tasks]
        for (f, s), sides in zip(tasks, _refold(groups)):
            for o, pieces in zip((q - 3, 6 - q), sides):
                for h in range(2):
                    at = BLOCK * ((f * 4 + o) * 2 + h) + s
                    boxes[pl.ds(at, 8, stride=2), :] = pieces[h]
    for f, out in enumerate((pot, res)):
        for o in range(4):
            for h in range(2):
                v = _blk(boxes, (f * 4 + o) * 2 + h)
                out[box_of[(o // 2) * 2 + h], :, (o % 2) * LANES : (o % 2 + 1) * LANES] = v


def _lazily(fn):
    made = {}

    def get(u):
        if u not in made:
            made[u] = fn(u)
        return made[u]

    return get


def _shape(*dims):
    return jax.ShapeDtypeStruct(dims, F32)


def _rows(n):
    return _shape(n, LANES)


VMEM = pl.BlockSpec(memory_space=pltpu.VMEM)
HBM = pl.BlockSpec(memory_space=pltpu.HBM)


def _call(kernel, specs, outs, scratch=(), us=0.1, grant=40.0):
    return pl.pallas_call(
        kernel,
        out_shape=outs,
        in_specs=specs,
        out_specs=[VMEM] * len(outs),
        scratch_shapes=scratch,
        cost_estimate=pl.CostEstimate(flops=0, transcendentals=0, bytes_accessed=int(us * 3.5e6)),
        compiler_params=pltpu.CompilerParams(vmem_limit_bytes=int(grant * 2**20)),
    )


def _y_shift(n):
    return [(4 * y + z, 4 * ((y + n) % 4) + z) for y in range(4) for z in range(4)]


def _z_shift(n):
    return [(4 * y + z, 4 * y + (z + n) % 4) for y in range(4) for z in range(4)]


def _x_shift(n):
    return [(x, (x + n) % 8) for x in range(8)]


def _body(weights, divergence, box_coords, neighbors):
    coords = box_coords.T
    raw, weight = _call(
        _fetch_kernel,
        [HBM, HBM],
        [_shape(*divergence.shape), _shape(*weights.shape[1:])],
        [pltpu.SemaphoreType.DMA((2,))],
        us=1.0,
        grant=53.79,
    )(divergence, weights)
    own, sums, order = _call(
        _sort_kernel,
        [VMEM] * 3,
        [_rows(128), _rows(8), jax.ShapeDtypeStruct((8, LANES), jnp.int32)],
        [pltpu.VMEM((128, LANES), F32)],
    )(coords, raw, weight)
    across = lax.ppermute(sums, "dev", _y_shift(2))
    up, down = _call(_y_kernel, [VMEM] * 2, [_rows(Y_MESSAGE), _rows(Y_MESSAGE)])(own, sums)
    below = lax.ppermute(up, "dev", _y_shift(1))
    above = lax.ppermute(down, "dev", _y_shift(-1))

    plane = pltpu.VMEM((COARSE + 1, 24, LANES), F32)
    fine = _shape(FINE + 1, 24, LANES)
    inner = pltpu.VMEM((FINE + 1, 24, LANES), F32)
    ones = _call(_ones_kernel, [], [fine, fine], [inner, inner, plane, plane, plane], us=1.0)()
    sums, ones = lax.optimization_barrier((sums, ones))
    total = _call(_total_kernel, [VMEM] * 4, [_rows(8)])(sums, below, above, across)[0]
    zacross = lax.ppermute(total, "dev", _z_shift(2))
    up, down = _call(_z_kernel, [VMEM] * 4, [_rows(168), _rows(168)])(own, below, above, total)
    zbelow = lax.ppermute(up, "dev", _z_shift(1))
    zabove = lax.ppermute(down, "dev", _z_shift(-1))

    mine, up, down, high, low, part = _call(
        _x_kernel,
        [VMEM] * 7,
        [_rows(640), _rows(MESSAGE), _rows(MESSAGE), _rows(72), _rows(72), _rows(8)],
    )(own, below, above, zbelow, zabove, total, zacross)
    xm1 = lax.ppermute(up, "grp", _x_shift(1))
    xp1 = lax.ppermute(down, "grp", _x_shift(-1))
    xm2 = lax.ppermute(high, "grp", _x_shift(2))
    xp2 = lax.ppermute(low, "grp", _x_shift(-2))
    bricks = []
    for ref, at, rows in (
        (xm1, functools.partial(_Sent, from_below=True), slice(8, 16)),
        (mine, _Own, slice(16, 24)),
        (xp1, functools.partial(_Sent, from_below=False), slice(24, 32)),
    ):
        kernel = functools.partial(_brick_kernel, at=at, rows=rows)
        outs = [_shape(2, FINE + 1, 8, LANES), _shape(2, 26, 8, LANES)]
        bricks.append(_call(kernel, [VMEM], outs, us=0.8)(ref))
    part, bricks = lax.optimization_barrier((part, bricks))
    tiles, fars = zip(*bricks)
    part, send = _call(_window_kernel, [VMEM] * 5, [_rows(8), _rows(8)])(part, xm1, xp1, xm2, xp2)
    xacross = lax.ppermute(send, "grp", [(x, (x + 3 - 6 * (x % 2)) % 8) for x in range(8)])

    start = _call(
        _coarse_kernel,
        [VMEM] * 8,
        [fine, fine],
        [
            inner,
            inner,
            pltpu.VMEM((2, FINE + 1, 8, LANES), F32),
            pltpu.VMEM((COARSE, 32, LANES), F32),
            pltpu.VMEM((12, 24, LANES), F32),
            plane,
            plane,
            plane,
        ],
        us=3,
    )(*tiles, *fars, xm2, xp2)

    boxes = pltpu.VMEM((16 * BLOCK, LANES), F32)
    pot, res = _call(
        _cycle_kernel,
        [VMEM] * 10,
        [_shape(4, 16, 256), _shape(4, 16, 256)],
        [inner, inner, plane, plane, plane, boxes, pltpu.SMEM((8, LANES), jnp.int32), pltpu.SemaphoreType.DMA((1,))],
    )(order, *tiles, *start, *ones, part, xacross)
    return pot, res


def solution(mesh):
    table = _mean_weights()

    def body(divergence, box_coords, neighbors):
        return _body(jnp.asarray(table), divergence, box_coords, neighbors)

    split = P(("grp", "dev"), None, None)
    return jax.shard_map(
        body, mesh=mesh, in_specs=(split, P(), P()), out_specs=(split, split), check_vma=False
    )
```

```python
import functools

import numpy as np

import jax
import jax.numpy as jnp
from jax import lax
from jax.experimental import pallas as pl
from jax.experimental.pallas import tpu as pltpu
from jax.sharding import PartitionSpec as P

KC = 4
CYCLES = 2
W = 0.8 / 6.0
BETA = 0.8 / 1.5
CELLS = 128**3
BLOCK = 16
LANES = 128
F32 = jnp.float32


def _apply(v):
    total = 6.0 * v
    for axis in range(3):
        lo = [slice(None)] * 3
        hi = [slice(None)] * 3
        lo[axis], hi[axis] = slice(None, -1), slice(1, None)
        total[tuple(lo)] -= v[tuple(hi)]
        total[tuple(hi)] -= v[tuple(lo)]
    return total


def _mean_weights():
    ones = np.ones((128, 128, 128))
    relax = lambda v: v - W * _apply(v)
    k0 = _apply(ones)
    k1 = relax(k0)
    k2 = relax(k1)
    q = k2.reshape(64, 2, 64, 2, 64, 2).sum(axis=(1, 3, 5))
    s = np.zeros_like(q)
    for _ in range(KC):
        s = s + BETA * (q - 0.25 * _apply(s))
    back = np.repeat(np.repeat(np.repeat(s, 2, 0), 2, 1), 2, 2) / 8.0
    full = ones - W * (k0 + k1 + k2) - relax(back) + (s.sum() / CELLS) * relax(ones)
    blocks = []
    for x in (0, 3, 7):
        for y in (0, 1, 3):
            for z in (0, 1, 3):
                b = full[16 * x : 16 * x + 16, 32 * y : 32 * y + 32, 32 * z : 32 * z + 32]
                b = b.reshape(16, 4, 8, 2, 16).transpose(1, 3, 0, 2, 4)
                blocks.append(b.reshape(8, 16, LANES))
    return np.stack(blocks).astype(np.float32)


def _iota(shape, dim):
    return lax.broadcasted_iota(jnp.int32, shape, dim)


def _roll(v, shift, axis):
    shift = shift % v.shape[axis]
    return v if shift == 0 else pltpu.roll(v, shift, axis)


def _position():
    d = lax.axis_index("dev")
    return lax.axis_index("grp"), d // 4, d % 4


def _blk(ref, i):
    return ref[BLOCK * i : BLOCK * (i + 1), :]


def _put(ref, i, v):
    ref[BLOCK * i : BLOCK * (i + 1), :] = v


def _fetch_kernel(div, w2, raw, weight, sem):
    g, yb, zb = _position()
    kind = lambda i, n: jnp.where(i == 0, 0, jnp.where(i == n - 1, 2, 1))
    which = kind(g, 8) * 9 + kind(yb, 4) * 3 + kind(zb, 4)
    copies = (
        pltpu.make_async_copy(div, raw, sem.at[0]),
        pltpu.make_async_copy(w2.at[which], weight, sem.at[1]),
    )
    for copy in copies:
        copy.start()
    for copy in copies:
        copy.wait()


def _sort_kernel(coords, raw, weight, own, sums, order, plain):
    g, yb, zb = _position()
    row = _iota((16, LANES), 0)
    lane = _iota((16, LANES), 1)
    j, k = lane // 16, lane % 16
    edge_x = ((row == 0) & (g == 0)).astype(F32) + ((row == 15) & (g == 7)).astype(F32)
    s1 = jnp.zeros((16, LANES), F32)
    s2 = jnp.zeros((16, LANES), F32)
    box_of = _box_of(coords, g, yb, zb)
    row8 = _iota((8, LANES), 0)
    order[...] = sum(jnp.where(row8 == h, box_of[h], 0) for h in range(4))
    for o in range(4):
        for h in range(2):
            v = raw[box_of[(o // 2) * 2 + h], :, (o % 2) * LANES : (o % 2 + 1) * LANES]
            at = BLOCK * (o * 2 + h)
            plain[at : at + BLOCK, :] = v
            edge = edge_x
            if o == 0:
                edge += ((j == 0) & (yb == 0)).astype(F32)
            if o == 3:
                edge += ((j == 7) & (yb == 3)).astype(F32)
            if h == 0:
                edge += ((k == 0) & (zb == 0)).astype(F32)
            else:
                edge += ((k == 15) & (zb == 3)).astype(F32)
            s1 += (1.0 - W * edge) * v
            s2 += weight[o * 2 + h] * v
    for i in range(16):
        own[8 * i : 8 * i + 8, :] = plain[pl.ds(BLOCK * (i // 2) + i % 2, 8, stride=2), :]
    s1, s2 = (jnp.sum(v, axis=0, keepdims=True) for v in (s1, s2))
    sums[...] = jnp.where(row8 == 0, s1, jnp.where(row8 == 1, s2, 0.0))


def _box_of(coords, g, yb, zb):
    mine = (g * 4 + yb) * 4 + zb
    at = pl.ds(pl.multiple_of(mine // 32 * LANES, LANES), LANES)
    slot = coords[1:2, at] % 2 * 2 + coords[2:3, at] % 2
    box = _iota((1, LANES), 1) - mine % 32 * 4
    inside = (box >= 0) & (box < 4)
    return [jnp.sum(jnp.where(inside & (slot == h), box, 0)) for h in range(4)]


def _ext(own, below, above, q, h):
    if q == 0:
        return _roll(_blk(below, 4), 64 * h, 1)
    if q < 3:
        return _blk(below, (q - 1) * 2 + h)
    if q < 7:
        return _blk(own, (q - 3) * 2 + h)
    if q < 9:
        return _blk(above, (q - 7) * 2 + h)
    return _roll(_blk(above, 4), 64 * h, 1)


def _pack_quads(pieces, src_quad):
    quad = _iota(pieces[0].shape, 1) % 16 // 4
    out = _roll(pieces[0], 4 * (0 - src_quad), 1)
    for s in range(1, len(pieces)):
        out = jnp.where(quad == s, _roll(pieces[s], 4 * (s - src_quad), 1), out)
    return out


Y_FAR, Y_SUMS, Y_MESSAGE = 64, 80, 88


def _y_kernel(own, sums, up, down):
    half = _iota((BLOCK, LANES), 1) < 64
    for i in range(4):
        _put(up, i, _blk(own, i + 4))
        _put(down, i, _blk(own, i))
    _put(up, 4, jnp.where(half, _roll(_blk(own, 3), 64, 1), _blk(own, 2)))
    _put(down, 4, jnp.where(half, _blk(own, 4), _roll(_blk(own, 5), 64, 1)))
    for ref in (up, down):
        ref[Y_SUMS:Y_MESSAGE, :] = sums[...]


def _total_kernel(sums, below, above, across, total):
    total[...] = sums[...] + below[Y_SUMS:Y_MESSAGE, :] + above[Y_SUMS:Y_MESSAGE, :] + across[...]


def _z_kernel(own, below, above, total, up, down):
    ext = lambda q, h: _ext(own, below, above, q, h)
    for q in range(1, 9):
        _put(up, q - 1, ext(q, 1))
        _put(down, q - 1, ext(q, 0))
    for ref, near, quad in ((up, 1, 3), (down, 0, 0)):
        far = [ext(q, 1 - near) for q in range(2, 8)]
        _put(ref, 8, _pack_quads(far[:4], quad))
        _put(ref, 9, _pack_quads([*far[4:], ext(0, near), ext(9, near)], quad))
        ref[160:168, :] = total[...]


OUTER, SUMS, MESSAGE = 384, 480, 488
OWN_EY, OWN_COLS = 512, 576


def _rows_to(pieces):
    row = _iota((8, LANES), 0)
    out = None
    for i, (v, r) in enumerate(pieces):
        v = _roll(v, 2 * i - r, 0)
        out = v if out is None else jnp.where(row < 2 * i, out, v)
    return out


def _rows_far(near):
    return _iota((8, LANES), 0) // 2 == (0 if near else 3)


def _lower_lanes():
    return _iota((8, LANES), 1) % 16 < 8


def _hide(v, tile, near):
    return jnp.where(_rows_far(near), _roll(v, 2 if near else -2, 0), tile)


def _share(lo, hi, near):
    row, lane = _iota((8, LANES), 0), _iota((8, LANES), 1)
    middle = jnp.where(lane % 16 < 8, hi, lo)
    edge = jnp.where((row // 2) == near // 2, lo, _roll(hi, 2 if near else -2, 0))
    return jnp.where((row >= 2) & (row < 6), middle, edge)


def _x_kernel(own, below, above, zbelow, zabove, total, across, mine, up, down, high, low, part):
    ext = lambda q, h: _ext(own, below, above, q, h)
    extra = [ext(q, h) for q in (0, 9) for h in range(2)]
    extra += [_blk(zbelow, 8), _blk(zbelow, 9), _blk(zabove, 8), _blk(zabove, 9)]
    for i, v in enumerate(extra):
        _put(mine, 32 + i, v)
    two_away = []
    for q in range(1, 9):
        pieces = (_blk(zbelow, q - 1), ext(q, 0), ext(q, 1), _blk(zabove, q - 1))
        for p in range(4):
            _put(mine, (q - 1) * 4 + p, pieces[p])
        if 2 <= q <= 7:
            two_away += pieces[1:3]
            for ref, near in ((up, 6), (down, 0)):
                for p in (1, 2):
                    _put(ref, (q - 2) * 4 + p, pieces[p])
                for s in (0, 8):
                    lo, hi = (pieces[p][s : s + 8] for p in (0, 3))
                    far = _rows_far(near)
                    at = (q - 2) * 64 + s
                    ref[at : at + 8, :] = jnp.where(far & _lower_lanes(), hi, lo)
                    ref[at + 48 : at + 56, :] = _hide(extra[q - 2][s : s + 8], hi, near)
            continue
        at = OUTER + (0 if q == 1 else 48)
        for ref, near in ((up, 6), (down, 0)):
            for s in (0, 8):
                hidden = extra[6 if q == 1 else 7][s : s + 8]
                ref[at + s : at + s + 8, :] = _hide(hidden, pieces[1][s : s + 8], near)
            ref[at + 16 : at + 32, :] = pieces[2]
            for s in (0, 8):
                ref[at + 32 + s : at + 40 + s, :] = _share(pieces[0][s : s + 8], pieces[3][s : s + 8], near)
    for src, quad in ((zbelow, 3), (zabove, 0)):
        near = [_blk(src, q - 1) for q in range(2, 8)]
        two_away += [_pack_quads(near[:4], quad), _pack_quads(near[4:], quad)]
    for ref, r in ((high, 6), (low, 0)):
        for i in range(0, 16, 2):
            a, b = two_away[i : i + 2]
            ref[4 * i : 4 * i + 8, :] = _rows_to([(a[:8], r), (b[:8], r), (a[8:], r), (b[8:], r)])
    t = total[...] + zbelow[160:168, :] + zabove[160:168, :] + across[...]
    part[...] = t
    for ref, at in ((up, SUMS), (down, SUMS), (high, 64), (low, 64)):
        ref[at : at + 8, :] = t


def _window_kernel(mine, xm1, xp1, xm2, xp2, out, send):
    odd = _position()[0] % 2 == 1
    low = xm1[SUMS:MESSAGE, :] + xm2[64:72, :]
    high = xp1[SUMS:MESSAGE, :] + xp2[64:72, :]
    out[...] = mine[...] + (low + high)
    send[...] = mine[...] + jnp.where(odd, high, low)


FINE, COARSE = 40, 20


def _inside(pos, start, limit):
    return ((pos + start >= 0) & (pos + start < limit)).astype(F32)


def _ring_mask(g, zb):
    row = _iota((32, LANES), 0)
    offset = jnp.where(row < 4, row + 16, row - 16)
    return _inside(offset, g * 8, 64) * _inside(_iota((32, LANES), 1) % 64 - 16, zb * 32, 128)


def _fold_mask(yb):
    below, above = (yb > 0).astype(F32), (yb < 3).astype(F32)
    return jnp.where(_iota((8, LANES), 1) < 64, below, above)


def _tall(mask, n):
    return jnp.concatenate([mask] * (n // 8), axis=0)


def _blocks(first, count, size, fn):
    n = (count - 1) // size
    if n:

        def step(i, _):
            fn(first + i * size, size)
            return 0

        lax.fori_loop(0, n, step, 0)
    fn(first + n * size, count - n * size)


def _store(ref, i, v, last):
    ref[i] = v
    if isinstance(i, int) and i == last:
        ref[i + 1] = _roll(v, 64, 1)


def _lanes():
    lane = _iota((8, LANES), 1)
    return lane < 64, lane // 16


def _pick(cond, a, b):
    if a is None and b is None:
        return None
    return jnp.where(cond, 0.0 if a is None else a, 0.0 if b is None else b)


def _turn(v, shift):
    return None if v is None else _roll(v, shift, 1)


def _unfold(groups):
    half, block = _lanes()
    vs = [
        [_pick(half, a, c) for a, c in zip(low, high)] + [_turn(_pick(half, c, a), 64) for a, c in zip(low, high)]
        for low, high in groups
    ]
    for bit in (2, 1):
        vs = [_swap_bit(v, block, bit) for v in vs]
    return [[_pick(half, v[i], v[i ^ 3]) for i in range(8)] for v in vs]


def _swap_bit(v, block, bit):
    zero = (block & bit) == 0
    out = [None] * 8
    for i in range(8):
        if not i & bit:
            x, y = v[i], v[i | bit]
            out[i] = _pick(zero, x, _turn(y, 16 * bit))
            out[i | bit] = _pick(zero, _turn(x, -16 * bit), y)
    return out


def _refold(groups):
    half, block = _lanes()
    vs = [[_pick(half, rows[i], rows[i ^ 3]) for i in range(8)] for rows in groups]
    for bit in (1, 2):
        vs = [_swap_bit(v, block, bit) for v in vs]
    turned = [{p: _turn(v[p | 4], 64) for p in (1, 2)} for v in vs]
    return [
        ([_pick(half, v[p], u[p]) for p in (1, 2)], [_pick(half, u[p], v[p]) for p in (1, 2)])
        for v, u in zip(vs, turned)
    ]


class _Own:
    def __init__(self, ref):
        self.ref = ref

    def tile(self, at):
        return self.ref[at : at + 8, :]

    def core(self, q, p, s):
        return self.tile((q - 1) * 64 + 16 * p + 8 * s)

    def outer(self, i, s):
        return self.tile(OWN_EY + 16 * i + 8 * s)

    def quads(self, i, s):
        return self.tile(OWN_COLS + 16 * i + 8 * s)


class _Sent(_Own):
    def __init__(self, ref, from_below):
        self.ref, self.first = ref, 6 if from_below else 0

    def core(self, q, p, s):
        if 2 <= q <= 7:
            v = self.tile((q - 2) * 64 + 16 * p + 8 * s)
            return jnp.where(_rows_far(self.first), self.core(q, 0, s), v) if p == 3 else v
        at = OUTER + (0 if q == 1 else 48) + 8 * s
        if p in (1, 2):
            return self.tile(at + 16 * (p - 1))
        shared = self.tile(at + 32)
        if p == 0:
            return shared
        near = _iota((8, LANES), 0) // 2 == self.first // 2
        return jnp.where(near, _roll(shared, -2 if self.first else 2, 0), shared)

    def short(self, i, s):
        at = i * 64 + 48 if i < 6 else OUTER + 48 * (i - 6)
        return _roll(self.tile(at + 8 * s), -2 if self.first else 2, 0)

    def outer(self, i, s):
        return self.short(i, s)

    def quads(self, i, s):
        return self.short(4 + i, s)


def _pieces(at, q, s):
    if 1 <= q <= 8:
        return [at.core(q, p, s) for p in range(4)]
    slot = 2 if q == 0 else 3
    near = [_roll(at.quads(c, s), by, 1) for c, by in ((1, 4 * (3 - slot)), (3, -4 * slot))]
    return [near[0], *(at.outer((0 if q == 0 else 2) + h, s) for h in range(2)), near[1]]


def _far_pieces(at, q, s):
    c, slot = divmod(q - 2, 4)
    return [_roll(at.quads(c, s), -4 * slot, 1), None, None, _roll(at.quads(2 + c, s), 4 * (3 - slot), 1)]


def _unpack_brick(at, mask, mask_far, fold, store, store_far):
    for batch in ([(0, 0), (1, 0), (2, 0)], [(3, 0), (4, 0), (2, 1)], [(3, 1), (4, 1)]):
        tasks = [(q, far, s) for q, far in batch for s in range(2)]
        groups = [
            [(_far_pieces if far else _pieces)(at, o, s) for o in (q, 9 - q)] for q, far, s in tasks
        ]
        for (q, far, s), rows in zip(tasks, _unfold(groups)):
            m = _outer_mask(mask_far if far else mask, fold, q)
            for r in range(8):
                if far:
                    store_far(s, 8 * q + r - 15, rows[r] * m)
                else:
                    store(s, 8 * q + r, rows[r] * m)


def _outer_mask(mask, fold, q):
    return mask * fold if q < 3 else mask


def _far_mask(g, zb):
    row = _iota((24, LANES), 0) - 8
    lane = _iota((24, LANES), 1) % 64
    below, above = (zb > 0).astype(F32), (zb < 3).astype(F32)
    return _inside(row, g * 8, 64) * jnp.where(lane < 4, below, jnp.where(lane >= 60, above, 0.0))


def _brick_kernel(ref, tile, far, *, at, rows):
    g, yb, zb = _position()

    def store(s, i, v):
        tile[s, i] = v

    def put(s, i, v):
        far[s, i] = v

    mask_far = _far_mask(g, zb)[rows.start - 8 : rows.stop - 8]
    _unpack_brick(at(ref), _ring_mask(g, zb)[rows], mask_far, _fold_mask(yb), store, put)
    for s in range(2):
        tile[s, FINE] = _roll(tile[s, FINE - 1], 64, 1)
        far[s, FINE - 15] = _roll(far[s, FINE - 16], 64, 1)


def _beside(s, *tiles):
    return lambda i: jnp.concatenate([t[s, i] for t in tiles], axis=0)


def _coarse_kernel(t1, t2, t3, f1, f2, f3, xm2, xp2, Ae, Ao, source, Be, Bo, ahead_of, raw, beyond, cs, c0, c1):
    g, yb, zb = _position()
    ring, fold = _ring_mask(g, zb), _fold_mask(yb)
    De, Do = D = [_beside(s, t1, t2, t3) for s in range(2)]
    far_e, far_o = [_beside(s, f1, f2, f3) for s in range(2)]

    row = _iota((8, LANES), 0)

    def near(i, s):
        at, r = slice(8 * (i // 2), 8 * (i // 2) + 8), 4 * s + 2 * (i % 2)
        return jnp.where(row < 4, _roll(xp2[at, :], -r, 0), _roll(xm2[at, :], 6 - r, 0))

    def ahead(q, s):
        c, slot = divmod(q - 2, 4)
        lo = _roll(near(12 + c, s), 4 * (3 - slot), 1)
        hi = _roll(near(14 + c, s), -4 * slot, 1)
        return [lo, near(2 * (q - 2), s), near(2 * (q - 2) + 1, s), hi]

    tasks = [(q, s) for q in range(2, 5) for s in range(2)]
    for (q, s), rows in zip(tasks, _unfold([(ahead(q, s), ahead(9 - q, s)) for q, s in tasks])):
        m = _outer_mask(ring[:8], fold, q)
        for r in range(8):
            _store(ahead_of.at[s], 8 * q + r, rows[r] * m, FINE - 1)

    def patch(rows, pairs):
        lane = _iota((24, LANES), 1) % 64
        sums = []
        for i in rows:
            f = 2 * i - 15
            e, o = far_e(f) + far_e(f + 1), far_o(f) + far_o(f + 1)
            sums.append((e, o, e + o, (far_e(f - 1) + far_e(f + 2)) + (far_o(f - 1) + far_o(f + 2))))
        turned = [_roll(o, 1, 0) + _roll(e, -1, 0) for e, o, _, _ in sums]
        hs = [(1.0 - 3.0 * W) * fp + W * (outer + t) for (_, _, fp, outer), t in zip(sums, turned)]
        ends = [(_roll(fp, -3, 1), _roll(fp, 2, 1)) for _, _, fp, _ in sums]
        sides = []
        for (_, _, fp, _), h, pair in zip(sums, hs, pairs):
            lo = _roll(h, -2, 1) + _roll(h, -3, 1) + W * (_roll(fp, -1, 1) + pair)
            hi = _roll(h, 2, 1) + _roll(h, 3, 1) + W * (_roll(fp, 1, 1) + pair)
            sides.append((lo, hi))
        for i, (lo, hi) in zip(rows, sides):
            low = jnp.where(lane == 0, lo, _roll(lo, 1, 1))
            high = jnp.where(lane == 63, hi, _roll(hi, -1, 1))
            beyond[i - 10] = jnp.where(lane < 32, low, high) * 0.125
        return ends

    def put_source(i, c):
        raw[i] = c

    whole = [lambda y, s=s, v=v: jnp.concatenate([ahead_of[s, y], v(y)], axis=0) for s, v in enumerate(D)]
    args = (whole, 32, W, 1.0 - 5.0 * W, None)
    _restrict(*args, 3, 7, put_source, None, 7)
    _restrict(*args, 10, 10, put_source, patch, 5)
    _sweep_three(g, yb, zb, lambda i: raw[i], lambda i: beyond[i], cs, c0, c1)
    base = [lambda i, v=v: W * v(i) for v in D]
    step_masks = _step_masks(g, yb, zb)
    _correct_and_smooth(step_masks, base, D, lambda i: c0[i], Be, Bo, 7, 13, 13)
    _smooth(step_masks, (lambda i: Be[i], lambda i: Bo[i]), D, Ae, Ao, 15, 25, 25)
    pair_of = lambda i: (De(i) + De(i + 1)) + (Do(i) + Do(i + 1))
    A = (lambda i: Ae[i], lambda i: Ao[i])
    _restrict(A, 24, 1.0, -5.0, pair_of, 8, 12, lambda i, c: _set(source, i, c), None, 6)


def _set(ref, i, v):
    ref[i] = v


def _ones_kernel(Te, To, source, Be, Bo, cs, c0, c1):
    g, yb, zb = _position()
    one = jnp.ones((32, LANES), F32)
    _sweep_three(g, yb, zb, lambda i: one, lambda i: one[8:], cs, c0, c1)
    step_masks = _step_masks(g, yb, zb)
    _correct_and_smooth(step_masks, None, None, lambda i: c0[i], Be, Bo, 7, 13, 13)
    _smooth(step_masks, (lambda i: Be[i], lambda i: Bo[i]), None, Te, To, 15, 25, 25)
    T = (lambda i: Te[i], lambda i: To[i])
    _restrict(T, 24, 1.0, -5.0, None, 8, 12, lambda i, c: _set(source, i, c), None, 6)


def _sweep_three(g, yb, zb, source, beyond, cs, c0, c1):
    ring, fold = BETA * _ring_mask(g, zb), _fold_mask(yb)
    outside = ring * _tall(fold, 32)
    lane = _iota((24, LANES), 1) % 64
    has_below, has_above = (zb > 0).astype(F32), (zb < 3).astype(F32)
    row = _iota((24, LANES), 0) - 8
    z_ends = jnp.where(lane < 2, has_below, jnp.where(lane >= 62, has_above, 0.0))
    beyond_mask = BETA * z_ends * _inside(row, g * 8, 64)
    beyond_outside = beyond_mask * _tall(fold, 24)
    mask = _ring_mask(g, zb)[8:]
    masks = (mask * _tall(fold, 24), mask)

    scaled = _lazily(lambda i: source(i) * (outside if i < 12 else ring))
    for i in range(4, COARSE):
        c = scaled(i)
        after = _roll(c, 64, 1) if i == COARSE - 1 else scaled(i + 1)
        near = (_roll(c, 1, 0) + _roll(c, -1, 0) + (scaled(i - 1) + after))[8:]
        c = c[8:]
        ends = None
        if i >= 10:
            ends = beyond(i - 10) * (beyond_outside if i < 12 else beyond_mask)
        cs[i] = c
        turns = _roll(c, 2, 1), _roll(c, -2, 1)
        _store(c0, i, c + _sweep(c, near, turns, lane, ends) * masks[i >= 12], COARSE - 1)
    _sweep_rows(c0, c1, cs, 5, masks)
    _sweep_rows(c1, c0, cs, 6, masks)


def _sweep(c, near, turns, lane, ends):
    before, after = turns
    if ends is not None:
        before = jnp.where(lane < 2, ends, before)
        after = jnp.where(lane >= 62, ends, after)
    return 0.2 * c + W * (near + (before + after))


def _sweep_rows(src, dst, cs, first, masks, batch=4):
    for start in range(first, COARSE, batch):
        rows = range(start, min(start + batch, COARSE))
        turned = [
            (_roll(src[i], 1, 0), _roll(src[i], -1, 0), _roll(src[i], 2, 1), _roll(src[i], -2, 1)) for i in rows
        ]
        for i, (low, high, *turns) in zip(rows, turned):
            near = (low + high) + (src[i - 1] + src[i + 1])
            _store(dst, i, cs[i] + _sweep(src[i], near, turns, None, None) * masks[i >= 12], COARSE - 1)


def _restrict(fields, rows, near, centre, more, first, count, store, patch, size):
    lane = _iota((rows, LANES), 1)
    even = lane % 2 == 0

    for start in range(first, first + count, size):
        even_at, odd_at = (_lazily(lambda u, v=v, start=start: v(2 * start + u)) for v in fields)
        sums = []
        us = range(min(size, first + count - start))
        for u in us:
            y = 2 * u
            ee, eo = even_at(y) + even_at(y + 1), odd_at(y) + odd_at(y + 1)
            outer = (even_at(y - 1) + even_at(y + 2)) + (odd_at(y - 1) + odd_at(y + 2))
            sums.append((ee, eo, ee + eo, outer))
        turned = [_roll(eo, 1, 0) + _roll(ee, -1, 0) for ee, eo, _, _ in sums]
        hs = []
        for u, ((_, _, pair, outer), t) in enumerate(zip(sums, turned)):
            h = (centre + 2.0 * near) * pair + near * (outer + t)
            hs.append(h if more is None else h + more(2 * (start + u)))
        sides = [(_roll(pair, 1, 1), _roll(pair, -2, 1)) for _, _, pair, _ in sums]
        if patch is not None:
            ends = patch([start + u for u in us], [pair[8:] for _, _, pair, _ in sums])
            for u, ((before, after), (low, high)) in enumerate(zip(sides, ends)):
                low = jnp.where(lane[8:] % 64 == 0, low, before[8:])
                high = jnp.where(lane[8:] % 64 == 62, high, after[8:])
                sides[u] = (
                    jnp.concatenate([before[:8], low], axis=0),
                    jnp.concatenate([after[:8], high], axis=0),
                )
        cs = [h + _roll(h, -1, 1) + near * (before + after) for h, (before, after) in zip(hs, sides)]
        cs = [jnp.where(even, c, _roll(c, 1, 1)) * 0.125 for c in cs]
        for u, c in enumerate(cs):
            store(start + u, c)


def _step_masks(g, yb, zb):
    mask = _ring_mask(g, zb)[8:]
    masks = (mask * _tall(_fold_mask(yb), 24), mask)
    return masks, [0.2 * m for m in masks], [W * m for m in masks]


def _of_row(pair, i, own_first):
    if isinstance(i, int):
        return pair[i >= own_first]
    return jnp.where(i < own_first, *pair)


def _relax(even, odd, i, n, store, batch=3):
    for first in range(0, n, batch):
        us = range(first, min(first + batch, n))
        turned = []
        for u in us:
            e, o = even(u), odd(u)
            turned.append((_roll(e, 1, 1), _roll(e, -1, 1), _roll(o, 1, 1), _roll(o, -1, 1), _roll(o, 1, 0), _roll(e, -1, 0)))
        for u, (e1, e2, o1, o2, before, after) in zip(us, turned):
            e, o = even(u), odd(u)
            ye = ((even(u - 1) + even(u + 1)) + (e1 + e2)) + (o + before)
            yo = ((odd(u - 1) + odd(u + 1)) + (o1 + o2)) + (e + after)
            store(i + u, e, o, ye, yo)


def _smooth_to(step_masks, D, dst_e, dst_o):
    def store(i, e, o, ye, yo):
        m, n = _of_row(step_masks[1], i, 24), _of_row(step_masks[2], i, 24)
        if D is not None:
            ye, yo = ye + D[0](i), yo + D[1](i)
        _store(dst_e, i, e * m + ye * n, FINE - 1)
        _store(dst_o, i, o * m + yo * n, FINE - 1)

    return store


def _smooth(step_masks, src, D, dst_e, dst_o, first, count, size):
    def fn(i, n):
        even, odd = (_lazily(lambda u, v=v: v(i + u)) for v in src)
        _relax(even, odd, i, n, _smooth_to(step_masks, D, dst_e, dst_o))

    _blocks(first, count, size, fn)


def _correct_and_smooth(step_masks, base, D, correction, dst_e, dst_o, first, count, size):
    def fn(start, n):
        i = 2 * start
        c = _lazily(lambda u: correction(start + u))
        if base is None:
            even = odd = lambda u: c(u // 2)
        else:
            even, odd = (_lazily(lambda u, v=v: v(i + u) + c(u // 2)) for v in base)
        _relax(even, odd, i, 2 * n, _smooth_to(step_masks, D, dst_e, dst_o))

    _blocks(first, count, size, fn)


def _cycle_kernel(
    order, t1, t2, t3, Re, Ro, raw, Te, To, raw_one, part, across, pot, res, Be, Bo, cs, c0, c1, boxes, place, sem
):
    g, yb, zb = _position()
    fetch = pltpu.make_async_copy(order, place, sem.at[0])
    fetch.start()
    totals = part[...] + across[...]
    means = jnp.sum(totals, axis=1, keepdims=True) * (1.0 / CELLS)
    mean1 = jnp.broadcast_to(means[0:1], (24, LANES))
    mean2 = jnp.broadcast_to(means[1:2], (24, LANES))
    step_masks = _step_masks(g, yb, zb)
    masks = step_masks[0]

    all_of = lambda ref: lambda i: ref[i]

    De, Do = D = [_beside(s, t1, t2, t3) for s in range(2)]
    A = (lambda i: Re[i] - mean1 * Te[i], lambda i: Ro[i] - mean1 * To[i])

    for i in range(8, COARSE):
        c = raw[i] - mean1 * raw_one[i] - mean2
        _store(cs, i, c * (masks[i >= 12] * BETA), COARSE - 1)
    _sweep_rows(cs, c0, cs, 9, masks)
    _sweep_rows(c0, c1, cs, 10, masks)
    _sweep_rows(c1, c0, cs, 11, masks)
    _correct_and_smooth(step_masks, A, D, all_of(c0), Be, Bo, 11, 9, 9)

    fetch.wait()
    box_of = [place[h, 0] for h in range(4)]
    for q in (3, 4):
        i0 = 8 * q
        even = _lazily(lambda u: Be[i0 + u])
        odd = _lazily(lambda u: Bo[i0 + u])
        left = ([], [])

        def store(i, e, o, ye, yo):
            left[0].append(t2[0, i] - (6.0 * e - ye)[8:16])
            left[1].append(t2[1, i] - (6.0 * o - yo)[8:16])

        _relax(even, odd, i0, 8, store)
        tasks = [(f, s) for f in range(2) for s in range(2)]
        done = [[v(u)[8:16] for u in range(8)] for v in (even, odd)]
        groups = [(done, left)[f][s] for f, s in tasks]
        for (f, s), sides in zip(tasks, _refold(groups)):
            for o, pieces in zip((q - 3, 6 - q), sides):
                for h in range(2):
                    at = BLOCK * ((f * 4 + o) * 2 + h) + s
                    boxes[pl.ds(at, 8, stride=2), :] = pieces[h]
    for f, out in enumerate((pot, res)):
        for o in range(4):
            for h in range(2):
                v = _blk(boxes, (f * 4 + o) * 2 + h)
                out[box_of[(o // 2) * 2 + h], :, (o % 2) * LANES : (o % 2 + 1) * LANES] = v


def _lazily(fn):
    made = {}

    def get(u):
        if u not in made:
            made[u] = fn(u)
        return made[u]

    return get


def _shape(*dims):
    return jax.ShapeDtypeStruct(dims, F32)


def _rows(n):
    return _shape(n, LANES)


VMEM = pl.BlockSpec(memory_space=pltpu.VMEM)
HBM = pl.BlockSpec(memory_space=pltpu.HBM)


def _call(kernel, specs, outs, scratch=(), us=0.1, grant=40.0):
    return pl.pallas_call(
        kernel,
        out_shape=outs,
        in_specs=specs,
        out_specs=[VMEM] * len(outs),
        scratch_shapes=scratch,
        cost_estimate=pl.CostEstimate(flops=0, transcendentals=0, bytes_accessed=int(us * 3.5e6)),
        compiler_params=pltpu.CompilerParams(vmem_limit_bytes=int(grant * 2**20)),
    )


def _y_shift(n):
    return [(4 * y + z, 4 * ((y + n) % 4) + z) for y in range(4) for z in range(4)]


def _z_shift(n):
    return [(4 * y + z, 4 * y + (z + n) % 4) for y in range(4) for z in range(4)]


def _x_shift(n):
    return [(x, (x + n) % 8) for x in range(8)]


def _body(weights, divergence, box_coords, neighbors):
    coords = box_coords.T
    raw, weight = _call(
        _fetch_kernel,
        [HBM, HBM],
        [_shape(*divergence.shape), _shape(*weights.shape[1:])],
        [pltpu.SemaphoreType.DMA((2,))],
        us=1.0,
        grant=53.79,
    )(divergence, weights)
    own, sums, order = _call(
        _sort_kernel,
        [VMEM] * 3,
        [_rows(128), _rows(8), jax.ShapeDtypeStruct((8, LANES), jnp.int32)],
        [pltpu.VMEM((128, LANES), F32)],
    )(coords, raw, weight)
    across = lax.ppermute(sums, "dev", _y_shift(2))
    up, down = _call(_y_kernel, [VMEM] * 2, [_rows(Y_MESSAGE), _rows(Y_MESSAGE)])(own, sums)
    below = lax.ppermute(up, "dev", _y_shift(1))
    above = lax.ppermute(down, "dev", _y_shift(-1))

    plane = pltpu.VMEM((COARSE + 1, 24, LANES), F32)
    fine = _shape(FINE + 1, 24, LANES)
    inner = pltpu.VMEM((FINE + 1, 24, LANES), F32)
    ones = _call(_ones_kernel, [], [fine, fine, _shape(COARSE, 24, LANES)], [inner, inner, plane, plane, plane], us=1.0)()
    sums, ones = lax.optimization_barrier((sums, ones))
    total = _call(_total_kernel, [VMEM] * 4, [_rows(8)])(sums, below, above, across)[0]
    zacross = lax.ppermute(total, "dev", _z_shift(2))
    up, down = _call(_z_kernel, [VMEM] * 4, [_rows(168), _rows(168)])(own, below, above, total)
    zbelow = lax.ppermute(up, "dev", _z_shift(1))
    zabove = lax.ppermute(down, "dev", _z_shift(-1))

    mine, up, down, high, low, part = _call(
        _x_kernel,
        [VMEM] * 7,
        [_rows(640), _rows(MESSAGE), _rows(MESSAGE), _rows(72), _rows(72), _rows(8)],
    )(own, below, above, zbelow, zabove, total, zacross)
    xm1 = lax.ppermute(up, "grp", _x_shift(1))
    xp1 = lax.ppermute(down, "grp", _x_shift(-1))
    xm2 = lax.ppermute(high, "grp", _x_shift(2))
    xp2 = lax.ppermute(low, "grp", _x_shift(-2))
    bricks = []
    for ref, at, rows in (
        (xm1, functools.partial(_Sent, from_below=True), slice(8, 16)),
        (mine, _Own, slice(16, 24)),
        (xp1, functools.partial(_Sent, from_below=False), slice(24, 32)),
    ):
        kernel = functools.partial(_brick_kernel, at=at, rows=rows)
        outs = [_shape(2, FINE + 1, 8, LANES), _shape(2, 26, 8, LANES)]
        bricks.append(_call(kernel, [VMEM], outs, us=0.8)(ref))
    part, bricks = lax.optimization_barrier((part, bricks))
    tiles, fars = zip(*bricks)
    part, send = _call(_window_kernel, [VMEM] * 5, [_rows(8), _rows(8)])(part, xm1, xp1, xm2, xp2)
    xacross = lax.ppermute(send, "grp", [(x, (x + 3 - 6 * (x % 2)) % 8) for x in range(8)])

    start = _call(
        _coarse_kernel,
        [VMEM] * 8,
        [fine, fine, _shape(COARSE, 24, LANES)],
        [
            inner,
            inner,
            pltpu.VMEM((2, FINE + 1, 8, LANES), F32),
            pltpu.VMEM((COARSE, 32, LANES), F32),
            pltpu.VMEM((12, 24, LANES), F32),
            plane,
            plane,
            plane,
        ],
        us=3,
    )(*tiles, *fars, xm2, xp2)

    boxes = pltpu.VMEM((16 * BLOCK, LANES), F32)
    pot, res = _call(
        _cycle_kernel,
        [VMEM] * 12,
        [_shape(4, 16, 256), _shape(4, 16, 256)],
        [inner, inner, plane, plane, plane, boxes, pltpu.SMEM((8, LANES), jnp.int32), pltpu.SemaphoreType.DMA((1,))],
    )(order, *tiles, *start, *ones, part, xacross)
    return pot, res


def solution(mesh):
    table = _mean_weights()

    def body(divergence, box_coords, neighbors):
        return _body(jnp.asarray(table), divergence, box_coords, neighbors)

    split = P(("grp", "dev"), None, None)
    return jax.shard_map(
        body, mesh=mesh, in_specs=(split, P(), P()), out_specs=(split, split), check_vma=False
    )
```

```python
import functools

import numpy as np

import jax
import jax.numpy as jnp
from jax import lax
from jax.experimental import pallas as pl
from jax.experimental.pallas import tpu as pltpu
from jax.sharding import PartitionSpec as P

KC = 4
CYCLES = 2
W = 0.8 / 6.0
BETA = 0.8 / 1.5
CELLS = 128**3
BLOCK = 16
LANES = 128
F32 = jnp.float32


def _apply(v):
    total = 6.0 * v
    for axis in range(3):
        lo = [slice(None)] * 3
        hi = [slice(None)] * 3
        lo[axis], hi[axis] = slice(None, -1), slice(1, None)
        total[tuple(lo)] -= v[tuple(hi)]
        total[tuple(hi)] -= v[tuple(lo)]
    return total


def _mean_weights():
    ones = np.ones((128, 128, 128))
    relax = lambda v: v - W * _apply(v)
    k0 = _apply(ones)
    k1 = relax(k0)
    k2 = relax(k1)
    q = k2.reshape(64, 2, 64, 2, 64, 2).sum(axis=(1, 3, 5))
    s = np.zeros_like(q)
    for _ in range(KC):
        s = s + BETA * (q - 0.25 * _apply(s))
    back = np.repeat(np.repeat(np.repeat(s, 2, 0), 2, 1), 2, 2) / 8.0
    full = ones - W * (k0 + k1 + k2) - relax(back) + (s.sum() / CELLS) * relax(ones)
    blocks = []
    for x in (0, 3, 7):
        for y in (0, 1, 3):
            for z in (0, 1, 3):
                b = full[16 * x : 16 * x + 16, 32 * y : 32 * y + 32, 32 * z : 32 * z + 32]
                b = b.reshape(16, 4, 8, 2, 16).transpose(1, 3, 0, 2, 4)
                blocks.append(b.reshape(8, 16, LANES))
    return np.stack(blocks).astype(np.float32)


def _iota(shape, dim):
    return lax.broadcasted_iota(jnp.int32, shape, dim)


def _roll(v, shift, axis):
    shift = shift % v.shape[axis]
    return v if shift == 0 else pltpu.roll(v, shift, axis)


def _position():
    d = lax.axis_index("dev")
    return lax.axis_index("grp"), d // 4, d % 4


def _blk(ref, i):
    return ref[BLOCK * i : BLOCK * (i + 1), :]


def _put(ref, i, v):
    ref[BLOCK * i : BLOCK * (i + 1), :] = v


def _fetch_kernel(div, w2, raw, weight, sem):
    g, yb, zb = _position()
    kind = lambda i, n: jnp.where(i == 0, 0, jnp.where(i == n - 1, 2, 1))
    which = kind(g, 8) * 9 + kind(yb, 4) * 3 + kind(zb, 4)
    copies = (
        pltpu.make_async_copy(div, raw, sem.at[0]),
        pltpu.make_async_copy(w2.at[which], weight, sem.at[1]),
    )
    for copy in copies:
        copy.start()
    for copy in copies:
        copy.wait()


def _sort_kernel(coords, raw, weight, own, sums, order, up, down, plain):
    g, yb, zb = _position()
    row = _iota((16, LANES), 0)
    lane = _iota((16, LANES), 1)
    j, k = lane // 16, lane % 16
    edge_x = ((row == 0) & (g == 0)).astype(F32) + ((row == 15) & (g == 7)).astype(F32)
    s1 = jnp.zeros((16, LANES), F32)
    s2 = jnp.zeros((16, LANES), F32)
    box_of = _box_of(coords, g, yb, zb)
    row8 = _iota((8, LANES), 0)
    order[...] = sum(jnp.where(row8 == h, box_of[h], 0) for h in range(4))
    for o in range(4):
        for h in range(2):
            v = raw[box_of[(o // 2) * 2 + h], :, (o % 2) * LANES : (o % 2 + 1) * LANES]
            at = BLOCK * (o * 2 + h)
            plain[at : at + BLOCK, :] = v
            edge = edge_x
            if o == 0:
                edge += ((j == 0) & (yb == 0)).astype(F32)
            if o == 3:
                edge += ((j == 7) & (yb == 3)).astype(F32)
            if h == 0:
                edge += ((k == 0) & (zb == 0)).astype(F32)
            else:
                edge += ((k == 15) & (zb == 3)).astype(F32)
            s1 += (1.0 - W * edge) * v
            s2 += weight[o * 2 + h] * v
    for i in range(16):
        own[8 * i : 8 * i + 8, :] = plain[pl.ds(BLOCK * (i // 2) + i % 2, 8, stride=2), :]
    s1, s2 = (jnp.sum(v, axis=0, keepdims=True) for v in (s1, s2))
    sums[...] = jnp.where(row8 == 0, s1, jnp.where(row8 == 1, s2, 0.0))
    _y_messages(own, sums, up, down)


def _box_of(coords, g, yb, zb):
    mine = (g * 4 + yb) * 4 + zb
    at = pl.ds(pl.multiple_of(mine // 32 * LANES, LANES), LANES)
    slot = coords[1:2, at] % 2 * 2 + coords[2:3, at] % 2
    box = _iota((1, LANES), 1) - mine % 32 * 4
    inside = (box >= 0) & (box < 4)
    return [jnp.sum(jnp.where(inside & (slot == h), box, 0)) for h in range(4)]


def _ext(own, below, above, q, h):
    if q == 0:
        return _roll(_blk(below, 4), 64 * h, 1)
    if q < 3:
        return _blk(below, (q - 1) * 2 + h)
    if q < 7:
        return _blk(own, (q - 3) * 2 + h)
    if q < 9:
        return _blk(above, (q - 7) * 2 + h)
    return _roll(_blk(above, 4), 64 * h, 1)


def _pack_quads(pieces, src_quad):
    quad = _iota(pieces[0].shape, 1) % 16 // 4
    out = _roll(pieces[0], 4 * (0 - src_quad), 1)
    for s in range(1, len(pieces)):
        out = jnp.where(quad == s, _roll(pieces[s], 4 * (s - src_quad), 1), out)
    return out


Y_FAR, Y_SUMS, Y_MESSAGE = 64, 80, 88


def _y_messages(own, sums, up, down):
    half = _iota((BLOCK, LANES), 1) < 64
    for i in range(4):
        _put(up, i, _blk(own, i + 4))
        _put(down, i, _blk(own, i))
    _put(up, 4, jnp.where(half, _roll(_blk(own, 3), 64, 1), _blk(own, 2)))
    _put(down, 4, jnp.where(half, _blk(own, 4), _roll(_blk(own, 5), 64, 1)))
    for ref in (up, down):
        ref[Y_SUMS:Y_MESSAGE, :] = sums[...]


def _total_kernel(sums, below, above, across, total):
    total[...] = sums[...] + below[Y_SUMS:Y_MESSAGE, :] + above[Y_SUMS:Y_MESSAGE, :] + across[...]


def _z_kernel(own, below, above, total, up, down):
    ext = lambda q, h: _ext(own, below, above, q, h)
    for q in range(1, 9):
        _put(up, q - 1, ext(q, 1))
        _put(down, q - 1, ext(q, 0))
    for ref, near, quad in ((up, 1, 3), (down, 0, 0)):
        far = [ext(q, 1 - near) for q in range(2, 8)]
        _put(ref, 8, _pack_quads(far[:4], quad))
        _put(ref, 9, _pack_quads([*far[4:], ext(0, near), ext(9, near)], quad))
        ref[160:168, :] = total[...]


OUTER, SUMS, MESSAGE = 384, 480, 488
OWN_EY, OWN_COLS = 512, 576


def _rows_to(pieces):
    row = _iota((8, LANES), 0)
    out = None
    for i, (v, r) in enumerate(pieces):
        v = _roll(v, 2 * i - r, 0)
        out = v if out is None else jnp.where(row < 2 * i, out, v)
    return out


def _rows_far(near):
    return _iota((8, LANES), 0) // 2 == (0 if near else 3)


def _lower_lanes():
    return _iota((8, LANES), 1) % 16 < 8


def _hide(v, tile, near):
    return jnp.where(_rows_far(near), _roll(v, 2 if near else -2, 0), tile)


def _share(lo, hi, near):
    row, lane = _iota((8, LANES), 0), _iota((8, LANES), 1)
    middle = jnp.where(lane % 16 < 8, hi, lo)
    edge = jnp.where((row // 2) == near // 2, lo, _roll(hi, 2 if near else -2, 0))
    return jnp.where((row >= 2) & (row < 6), middle, edge)


def _x_kernel(own, below, above, zbelow, zabove, total, across, mine, up, down, high, low, part):
    ext = lambda q, h: _ext(own, below, above, q, h)
    extra = [ext(q, h) for q in (0, 9) for h in range(2)]
    extra += [_blk(zbelow, 8), _blk(zbelow, 9), _blk(zabove, 8), _blk(zabove, 9)]
    for i, v in enumerate(extra):
        _put(mine, 32 + i, v)
    two_away = []
    for q in range(1, 9):
        pieces = (_blk(zbelow, q - 1), ext(q, 0), ext(q, 1), _blk(zabove, q - 1))
        for p in range(4):
            _put(mine, (q - 1) * 4 + p, pieces[p])
        if 2 <= q <= 7:
            if 3 <= q <= 6:
                two_away += pieces[1:3]
            for ref, near in ((up, 6), (down, 0)):
                for p in (1, 2):
                    _put(ref, (q - 2) * 4 + p, pieces[p])
                for s in (0, 8):
                    lo, hi = (pieces[p][s : s + 8] for p in (0, 3))
                    far = _rows_far(near)
                    at = (q - 2) * 64 + s
                    ref[at : at + 8, :] = jnp.where(far & _lower_lanes(), hi, lo)
                    ref[at + 48 : at + 56, :] = _hide(extra[q - 2][s : s + 8], hi, near)
            continue
        at = OUTER + (0 if q == 1 else 48)
        for ref, near in ((up, 6), (down, 0)):
            for s in (0, 8):
                hidden = extra[6 if q == 1 else 7][s : s + 8]
                ref[at + s : at + s + 8, :] = _hide(hidden, pieces[1][s : s + 8], near)
            ref[at + 16 : at + 32, :] = pieces[2]
            for s in (0, 8):
                ref[at + 32 + s : at + 40 + s, :] = _share(pieces[0][s : s + 8], pieces[3][s : s + 8], near)
    half = _iota((BLOCK, LANES), 1) < 64
    two_away += [jnp.where(half, ext(7, h), ext(2, h)) for h in range(2)]
    for src, quad in ((zbelow, 3), (zabove, 0)):
        near = [_blk(src, q - 1) for q in range(2, 8)]
        two_away += [_pack_quads(near[:4], quad), _pack_quads(near[4:], quad)]
    for ref, r in ((high, 6), (low, 0)):
        for i in range(0, 14, 2):
            a, b = two_away[i : i + 2]
            ref[4 * i : 4 * i + 8, :] = _rows_to([(a[:8], r), (b[:8], r), (a[8:], r), (b[8:], r)])
    t = total[...] + zbelow[160:168, :] + zabove[160:168, :] + across[...]
    part[...] = t
    for ref, at in ((up, SUMS), (down, SUMS), (high, 56), (low, 56)):
        ref[at : at + 8, :] = t


def _window_kernel(mine, xm1, xp1, xm2, xp2, out, send):
    odd = _position()[0] % 2 == 1
    low = xm1[SUMS:MESSAGE, :] + xm2[56:64, :]
    high = xp1[SUMS:MESSAGE, :] + xp2[56:64, :]
    out[...] = mine[...] + (low + high)
    send[...] = mine[...] + jnp.where(odd, high, low)


FINE, COARSE = 40, 20


def _inside(pos, start, limit):
    return ((pos + start >= 0) & (pos + start < limit)).astype(F32)


def _ring_mask(g, zb):
    row = _iota((32, LANES), 0)
    offset = jnp.where(row < 4, row + 16, row - 16)
    return _inside(offset, g * 8, 64) * _inside(_iota((32, LANES), 1) % 64 - 16, zb * 32, 128)


def _fold_mask(yb):
    below, above = (yb > 0).astype(F32), (yb < 3).astype(F32)
    return jnp.where(_iota((8, LANES), 1) < 64, below, above)


def _tall(mask, n):
    return jnp.concatenate([mask] * (n // 8), axis=0)


def _blocks(first, count, size, fn):
    n = (count - 1) // size
    if n:

        def step(i, _):
            fn(first + i * size, size)
            return 0

        lax.fori_loop(0, n, step, 0)
    fn(first + n * size, count - n * size)


def _store(ref, i, v, last):
    ref[i] = v
    if isinstance(i, int) and i == last:
        ref[i + 1] = _roll(v, 64, 1)


def _lanes():
    lane = _iota((8, LANES), 1)
    return lane < 64, lane // 16


def _pick(cond, a, b):
    if a is None and b is None:
        return None
    return jnp.where(cond, 0.0 if a is None else a, 0.0 if b is None else b)


def _turn(v, shift):
    return None if v is None else _roll(v, shift, 1)


def _unfold(groups):
    half, block = _lanes()
    vs = [
        [_pick(half, a, c) for a, c in zip(low, high)] + [_turn(_pick(half, c, a), 64) for a, c in zip(low, high)]
        for low, high in groups
    ]
    for bit in (2, 1):
        vs = [_swap_bit(v, block, bit) for v in vs]
    return [[_pick(half, v[i], v[i ^ 3]) for i in range(8)] for v in vs]


def _swap_bit(v, block, bit):
    zero = (block & bit) == 0
    out = [None] * 8
    for i in range(8):
        if not i & bit:
            x, y = v[i], v[i | bit]
            out[i] = _pick(zero, x, _turn(y, 16 * bit))
            out[i | bit] = _pick(zero, _turn(x, -16 * bit), y)
    return out


def _refold(groups):
    half, block = _lanes()
    vs = [[_pick(half, rows[i], rows[i ^ 3]) for i in range(8)] for rows in groups]
    for bit in (1, 2):
        vs = [_swap_bit(v, block, bit) for v in vs]
    turned = [{p: _turn(v[p | 4], 64) for p in (1, 2)} for v in vs]
    return [
        ([_pick(half, v[p], u[p]) for p in (1, 2)], [_pick(half, u[p], v[p]) for p in (1, 2)])
        for v, u in zip(vs, turned)
    ]


class _Own:
    def __init__(self, ref):
        self.ref = ref

    def tile(self, at):
        return self.ref[at : at + 8, :]

    def core(self, q, p, s):
        return self.tile((q - 1) * 64 + 16 * p + 8 * s)

    def outer(self, i, s):
        return self.tile(OWN_EY + 16 * i + 8 * s)

    def quads(self, i, s):
        return self.tile(OWN_COLS + 16 * i + 8 * s)


class _Sent(_Own):
    def __init__(self, ref, from_below):
        self.ref, self.first = ref, 6 if from_below else 0

    def core(self, q, p, s):
        if 2 <= q <= 7:
            v = self.tile((q - 2) * 64 + 16 * p + 8 * s)
            return jnp.where(_rows_far(self.first), self.core(q, 0, s), v) if p == 3 else v
        at = OUTER + (0 if q == 1 else 48) + 8 * s
        if p in (1, 2):
            return self.tile(at + 16 * (p - 1))
        shared = self.tile(at + 32)
        if p == 0:
            return shared
        near = _iota((8, LANES), 0) // 2 == self.first // 2
        return jnp.where(near, _roll(shared, -2 if self.first else 2, 0), shared)

    def short(self, i, s):
        at = i * 64 + 48 if i < 6 else OUTER + 48 * (i - 6)
        return _roll(self.tile(at + 8 * s), -2 if self.first else 2, 0)

    def outer(self, i, s):
        return self.short(i, s)

    def quads(self, i, s):
        return self.short(4 + i, s)


def _pieces(at, q, s):
    if 1 <= q <= 8:
        return [at.core(q, p, s) for p in range(4)]
    slot = 2 if q == 0 else 3
    near = [_roll(at.quads(c, s), by, 1) for c, by in ((1, 4 * (3 - slot)), (3, -4 * slot))]
    return [near[0], *(at.outer((0 if q == 0 else 2) + h, s) for h in range(2)), near[1]]


def _far_pieces(at, q, s):
    c, slot = divmod(q - 2, 4)
    return [_roll(at.quads(c, s), -4 * slot, 1), None, None, _roll(at.quads(2 + c, s), 4 * (3 - slot), 1)]


def _unpack_brick(at, mask, mask_far, fold, store, store_far):
    for batch in ([(0, 0), (1, 0), (2, 0)], [(3, 0), (4, 0), (2, 1)], [(3, 1), (4, 1)]):
        tasks = [(q, far, s) for q, far in batch for s in range(2)]
        groups = [
            [(_far_pieces if far else _pieces)(at, o, s) for o in (q, 9 - q)] for q, far, s in tasks
        ]
        for (q, far, s), rows in zip(tasks, _unfold(groups)):
            m = _outer_mask(mask_far if far else mask, fold, q)
            for r in range(8):
                if far:
                    store_far(s, 8 * q + r - 15, rows[r] * m)
                else:
                    store(s, 8 * q + r, rows[r] * m)


def _outer_mask(mask, fold, q):
    return mask * fold if q < 3 else mask


def _far_mask(g, zb):
    row = _iota((24, LANES), 0) - 8
    lane = _iota((24, LANES), 1) % 64
    below, above = (zb > 0).astype(F32), (zb < 3).astype(F32)
    return _inside(row, g * 8, 64) * jnp.where(lane < 4, below, jnp.where(lane >= 60, above, 0.0))


def _brick_kernel(ref, tile, far, *, at, rows):
    g, yb, zb = _position()

    def store(s, i, v):
        tile[s, i] = v

    def put(s, i, v):
        far[s, i] = v

    mask_far = _far_mask(g, zb)[rows.start - 8 : rows.stop - 8]
    _unpack_brick(at(ref), _ring_mask(g, zb)[rows], mask_far, _fold_mask(yb), store, put)
    for s in range(2):
        tile[s, FINE] = _roll(tile[s, FINE - 1], 64, 1)
        far[s, FINE - 15] = _roll(far[s, FINE - 16], 64, 1)


def _beside(s, *tiles):
    return lambda i: jnp.concatenate([t[s, i] for t in tiles], axis=0)


def _coarse_kernel(t1, t2, t3, f1, f2, f3, xm2, xp2, Ae, Ao, source, Be, Bo, ahead_of, raw, beyond, cs, c0, c1):
    g, yb, zb = _position()
    ring, fold = _ring_mask(g, zb), _fold_mask(yb)
    De, Do = D = [_beside(s, t1, t2, t3) for s in range(2)]
    far_e, far_o = [_beside(s, f1, f2, f3) for s in range(2)]

    row = _iota((8, LANES), 0)

    def near(i, s):
        at, r = slice(8 * (i // 2), 8 * (i // 2) + 8), 4 * s + 2 * (i % 2)
        return jnp.where(row < 4, _roll(xp2[at, :], -r, 0), _roll(xm2[at, :], 6 - r, 0))

    def ahead(q, s):
        c, slot = divmod(q - 2, 4)
        lo = _roll(near(10 + c, s), 4 * (3 - slot), 1)
        hi = _roll(near(12 + c, s), -4 * slot, 1)
        at = 2 * (q - 3) if 3 <= q <= 6 else 8
        return [lo, near(at, s), near(at + 1, s), hi]

    tasks = [(q, s) for q in range(2, 5) for s in range(2)]
    for (q, s), rows in zip(tasks, _unfold([(ahead(q, s), ahead(9 - q, s)) for q, s in tasks])):
        m = _outer_mask(ring[:8], fold, q)
        for r in range(8):
            _store(ahead_of.at[s], 8 * q + r, rows[r] * m, FINE - 1)

    def patch(rows, pairs):
        lane = _iota((24, LANES), 1) % 64
        sums = []
        for i in rows:
            f = 2 * i - 15
            e, o = far_e(f) + far_e(f + 1), far_o(f) + far_o(f + 1)
            sums.append((e, o, e + o, (far_e(f - 1) + far_e(f + 2)) + (far_o(f - 1) + far_o(f + 2))))
        turned = [_roll(o, 1, 0) + _roll(e, -1, 0) for e, o, _, _ in sums]
        hs = [(1.0 - 3.0 * W) * fp + W * (outer + t) for (_, _, fp, outer), t in zip(sums, turned)]
        ends = [(_roll(fp, -3, 1), _roll(fp, 2, 1)) for _, _, fp, _ in sums]
        sides = []
        for (_, _, fp, _), h, pair in zip(sums, hs, pairs):
            lo = _roll(h, -2, 1) + _roll(h, -3, 1) + W * (_roll(fp, -1, 1) + pair)
            hi = _roll(h, 2, 1) + _roll(h, 3, 1) + W * (_roll(fp, 1, 1) + pair)
            sides.append((lo, hi))
        for i, (lo, hi) in zip(rows, sides):
            low = jnp.where(lane == 0, lo, _roll(lo, 1, 1))
            high = jnp.where(lane == 63, hi, _roll(hi, -1, 1))
            beyond[i - 10] = jnp.where(lane < 32, low, high) * 0.125
        return ends

    def put_source(i, c):
        raw[i] = c

    whole = [lambda y, s=s, v=v: jnp.concatenate([ahead_of[s, y], v(y)], axis=0) for s, v in enumerate(D)]
    args = (whole, 32, W, 1.0 - 5.0 * W, None)
    _restrict(*args, 3, 7, put_source, None, 7)
    _restrict(*args, 10, 10, put_source, patch, 10)
    _sweep_three(g, yb, zb, lambda i: raw[i], lambda i: beyond[i], cs, c0, c1)
    base = [lambda i, v=v: W * v(i) for v in D]
    step_masks = _step_masks(g, yb, zb)
    _correct_and_smooth(step_masks, base, D, lambda i: c0[i], Be, Bo, 7, 13, 13)
    _smooth(step_masks, (lambda i: Be[i], lambda i: Bo[i]), D, Ae, Ao, 15, 25, 25)
    pair_of = lambda i: (De(i) + De(i + 1)) + (Do(i) + Do(i + 1))
    A = (lambda i: Ae[i], lambda i: Ao[i])
    _restrict(A, 24, 1.0, -5.0, pair_of, 8, 12, lambda i, c: _set(source, i, c), None, 6)


def _set(ref, i, v):
    ref[i] = v


def _ones_kernel(Te, To, source, Be, Bo, cs, c0, c1):
    g, yb, zb = _position()
    one = jnp.ones((32, LANES), F32)
    _sweep_three(g, yb, zb, lambda i: one, lambda i: one[8:], cs, c0, c1)
    step_masks = _step_masks(g, yb, zb)
    _correct_and_smooth(step_masks, None, None, lambda i: c0[i], Be, Bo, 7, 13, 13)
    _smooth(step_masks, (lambda i: Be[i], lambda i: Bo[i]), None, Te, To, 15, 25, 25)
    T = (lambda i: Te[i], lambda i: To[i])
    _restrict(T, 24, 1.0, -5.0, None, 8, 12, lambda i, c: _set(source, i, c), None, 6)


def _sweep_three(g, yb, zb, source, beyond, cs, c0, c1):
    ring, fold = BETA * _ring_mask(g, zb), _fold_mask(yb)
    outside = ring * _tall(fold, 32)
    lane = _iota((24, LANES), 1) % 64
    has_below, has_above = (zb > 0).astype(F32), (zb < 3).astype(F32)
    row = _iota((24, LANES), 0) - 8
    z_ends = jnp.where(lane < 2, has_below, jnp.where(lane >= 62, has_above, 0.0))
    beyond_mask = BETA * z_ends * _inside(row, g * 8, 64)
    beyond_outside = beyond_mask * _tall(fold, 24)
    mask = _ring_mask(g, zb)[8:]
    masks = (mask * _tall(fold, 24), mask)

    scaled = _lazily(lambda i: source(i) * (outside if i < 12 else ring))
    for i in range(4, COARSE):
        c = scaled(i)
        after = _roll(c, 64, 1) if i == COARSE - 1 else scaled(i + 1)
        near = (_roll(c, 1, 0) + _roll(c, -1, 0) + (scaled(i - 1) + after))[8:]
        c = c[8:]
        ends = None
        if i >= 10:
            ends = beyond(i - 10) * (beyond_outside if i < 12 else beyond_mask)
        cs[i] = c
        turns = _roll(c, 2, 1), _roll(c, -2, 1)
        _store(c0, i, c + _sweep(c, near, turns, lane, ends) * masks[i >= 12], COARSE - 1)
    _sweep_rows(c0, c1, cs, 5, masks)
    _sweep_rows(c1, c0, cs, 6, masks)


def _sweep(c, near, turns, lane, ends):
    before, after = turns
    if ends is not None:
        before = jnp.where(lane < 2, ends, before)
        after = jnp.where(lane >= 62, ends, after)
    return 0.2 * c + W * (near + (before + after))


def _sweep_rows(src, dst, cs, first, masks, batch=6):
    for start in range(first, COARSE, batch):
        rows = range(start, min(start + batch, COARSE))
        turned = [
            (_roll(src[i], 1, 0), _roll(src[i], -1, 0), _roll(src[i], 2, 1), _roll(src[i], -2, 1)) for i in rows
        ]
        for i, (low, high, *turns) in zip(rows, turned):
            near = (low + high) + (src[i - 1] + src[i + 1])
            _store(dst, i, cs[i] + _sweep(src[i], near, turns, None, None) * masks[i >= 12], COARSE - 1)


def _restrict(fields, rows, near, centre, more, first, count, store, patch, size):
    lane = _iota((rows, LANES), 1)
    even = lane % 2 == 0

    for start in range(first, first + count, size):
        even_at, odd_at = (_lazily(lambda u, v=v, start=start: v(2 * start + u)) for v in fields)
        sums = []
        us = range(min(size, first + count - start))
        for u in us:
            y = 2 * u
            ee, eo = even_at(y) + even_at(y + 1), odd_at(y) + odd_at(y + 1)
            outer = (even_at(y - 1) + even_at(y + 2)) + (odd_at(y - 1) + odd_at(y + 2))
            sums.append((ee, eo, ee + eo, outer))
        turned = [_roll(eo, 1, 0) + _roll(ee, -1, 0) for ee, eo, _, _ in sums]
        hs = []
        for u, ((_, _, pair, outer), t) in enumerate(zip(sums, turned)):
            h = (centre + 2.0 * near) * pair + near * (outer + t)
            hs.append(h if more is None else h + more(2 * (start + u)))
        sides = [(_roll(pair, 1, 1), _roll(pair, -2, 1)) for _, _, pair, _ in sums]
        if patch is not None:
            ends = patch([start + u for u in us], [pair[8:] for _, _, pair, _ in sums])
            for u, ((before, after), (low, high)) in enumerate(zip(sides, ends)):
                low = jnp.where(lane[8:] % 64 == 0, low, before[8:])
                high = jnp.where(lane[8:] % 64 == 62, high, after[8:])
                sides[u] = (
                    jnp.concatenate([before[:8], low], axis=0),
                    jnp.concatenate([after[:8], high], axis=0),
                )
        cs = [h + _roll(h, -1, 1) + near * (before + after) for h, (before, after) in zip(hs, sides)]
        cs = [jnp.where(even, c, _roll(c, 1, 1)) * 0.125 for c in cs]
        for u, c in enumerate(cs):
            store(start + u, c)


def _step_masks(g, yb, zb):
    mask = _ring_mask(g, zb)[8:]
    masks = (mask * _tall(_fold_mask(yb), 24), mask)
    return masks, [0.2 * m for m in masks], [W * m for m in masks]


def _of_row(pair, i, own_first):
    if isinstance(i, int):
        return pair[i >= own_first]
    return jnp.where(i < own_first, *pair)


def _relax(even, odd, i, n, store, batch=4):
    for first in range(0, n, batch):
        us = range(first, min(first + batch, n))
        turned = []
        for u in us:
            e, o = even(u), odd(u)
            turned.append((_roll(e, 1, 1), _roll(e, -1, 1), _roll(o, 1, 1), _roll(o, -1, 1), _roll(o, 1, 0), _roll(e, -1, 0)))
        for u, (e1, e2, o1, o2, before, after) in zip(us, turned):
            e, o = even(u), odd(u)
            ye = ((even(u - 1) + even(u + 1)) + (e1 + e2)) + (o + before)
            yo = ((odd(u - 1) + odd(u + 1)) + (o1 + o2)) + (e + after)
            store(i + u, e, o, ye, yo)


def _smooth_to(step_masks, D, dst_e, dst_o):
    def store(i, e, o, ye, yo):
        m, n = _of_row(step_masks[1], i, 24), _of_row(step_masks[2], i, 24)
        if D is not None:
            ye, yo = ye + D[0](i), yo + D[1](i)
        _store(dst_e, i, e * m + ye * n, FINE - 1)
        _store(dst_o, i, o * m + yo * n, FINE - 1)

    return store


def _smooth(step_masks, src, D, dst_e, dst_o, first, count, size):
    def fn(i, n):
        even, odd = (_lazily(lambda u, v=v: v(i + u)) for v in src)
        _relax(even, odd, i, n, _smooth_to(step_masks, D, dst_e, dst_o))

    _blocks(first, count, size, fn)


def _correct_and_smooth(step_masks, base, D, correction, dst_e, dst_o, first, count, size):
    def fn(start, n):
        i = 2 * start
        c = _lazily(lambda u: correction(start + u))
        if base is None:
            even = odd = lambda u: c(u // 2)
        else:
            even, odd = (_lazily(lambda u, v=v: v(i + u) + c(u // 2)) for v in base)
        _relax(even, odd, i, 2 * n, _smooth_to(step_masks, D, dst_e, dst_o))

    _blocks(first, count, size, fn)


def _cycle_kernel(
    order, t1, t2, t3, Re, Ro, raw, Te, To, raw_one, part, across, pot, res, Be, Bo, cs, c0, c1, boxes, place, sem
):
    g, yb, zb = _position()
    fetch = pltpu.make_async_copy(order, place, sem.at[0])
    fetch.start()
    totals = part[...] + across[...]
    means = jnp.sum(totals, axis=1, keepdims=True) * (1.0 / CELLS)
    mean1 = jnp.broadcast_to(means[0:1], (24, LANES))
    mean2 = jnp.broadcast_to(means[1:2], (24, LANES))
    step_masks = _step_masks(g, yb, zb)
    masks = step_masks[0]

    all_of = lambda ref: lambda i: ref[i]

    De, Do = D = [_beside(s, t1, t2, t3) for s in range(2)]
    A = (lambda i: Re[i] - mean1 * Te[i], lambda i: Ro[i] - mean1 * To[i])

    for i in range(8, COARSE):
        c = raw[i] - mean1 * raw_one[i] - mean2
        _store(cs, i, c * (masks[i >= 12] * BETA), COARSE - 1)
    _sweep_rows(cs, c0, cs, 9, masks)
    _sweep_rows(c0, c1, cs, 10, masks)
    _sweep_rows(c1, c0, cs, 11, masks)
    _correct_and_smooth(step_masks, A, D, all_of(c0), Be, Bo, 11, 9, 9)

    fetch.wait()
    box_of = [place[h, 0] for h in range(4)]
    for q in (3, 4):
        i0 = 8 * q
        even = _lazily(lambda u: Be[i0 + u])
        odd = _lazily(lambda u: Bo[i0 + u])
        left = ([], [])

        def store(i, e, o, ye, yo):
            left[0].append(t2[0, i] - (6.0 * e - ye)[8:16])
            left[1].append(t2[1, i] - (6.0 * o - yo)[8:16])

        _relax(even, odd, i0, 8, store)
        tasks = [(f, s) for f in range(2) for s in range(2)]
        done = [[v(u)[8:16] for u in range(8)] for v in (even, odd)]
        groups = [(done, left)[f][s] for f, s in tasks]
        for (f, s), sides in zip(tasks, _refold(groups)):
            for o, pieces in zip((q - 3, 6 - q), sides):
                for h in range(2):
                    at = BLOCK * ((f * 4 + o) * 2 + h) + s
                    boxes[pl.ds(at, 8, stride=2), :] = pieces[h]
    for f, out in enumerate((pot, res)):
        for o in range(4):
            for h in range(2):
                v = _blk(boxes, (f * 4 + o) * 2 + h)
                out[box_of[(o // 2) * 2 + h], :, (o % 2) * LANES : (o % 2 + 1) * LANES] = v


def _lazily(fn):
    made = {}

    def get(u):
        if u not in made:
            made[u] = fn(u)
        return made[u]

    return get


def _shape(*dims):
    return jax.ShapeDtypeStruct(dims, F32)


def _rows(n):
    return _shape(n, LANES)


VMEM = pl.BlockSpec(memory_space=pltpu.VMEM)
HBM = pl.BlockSpec(memory_space=pltpu.HBM)


def _call(kernel, specs, outs, scratch=(), us=0.1, grant=40.0):
    return pl.pallas_call(
        kernel,
        out_shape=outs,
        in_specs=specs,
        out_specs=[VMEM] * len(outs),
        scratch_shapes=scratch,
        cost_estimate=pl.CostEstimate(flops=0, transcendentals=0, bytes_accessed=int(us * 3.5e6)),
        compiler_params=pltpu.CompilerParams(vmem_limit_bytes=int(grant * 2**20)),
    )


def _y_shift(n):
    return [(4 * y + z, 4 * ((y + n) % 4) + z) for y in range(4) for z in range(4)]


def _z_shift(n):
    return [(4 * y + z, 4 * y + (z + n) % 4) for y in range(4) for z in range(4)]


def _x_shift(n):
    return [(x, (x + n) % 8) for x in range(8)]


def _body(weights, divergence, box_coords, neighbors):
    coords = box_coords.T
    raw, weight = _call(
        _fetch_kernel,
        [HBM, HBM],
        [_shape(*divergence.shape), _shape(*weights.shape[1:])],
        [pltpu.SemaphoreType.DMA((2,))],
        us=1.0,
        grant=53.79,
    )(divergence, weights)
    own, sums, order, up, down = _call(
        _sort_kernel,
        [VMEM] * 3,
        [
            *(_rows(128), _rows(8), jax.ShapeDtypeStruct((8, LANES), jnp.int32)),
            *(_rows(Y_MESSAGE), _rows(Y_MESSAGE)),
        ],
        [pltpu.VMEM((128, LANES), F32)],
    )(coords, raw, weight)
    across = lax.ppermute(sums, "dev", _y_shift(2))
    below = lax.ppermute(up, "dev", _y_shift(1))
    above = lax.ppermute(down, "dev", _y_shift(-1))

    plane = pltpu.VMEM((COARSE + 1, 24, LANES), F32)
    fine = _shape(FINE + 1, 24, LANES)
    inner = pltpu.VMEM((FINE + 1, 24, LANES), F32)
    ones = _call(_ones_kernel, [], [fine, fine, _shape(COARSE, 24, LANES)], [inner, inner, plane, plane, plane], us=1.0)()
    sums, ones = lax.optimization_barrier((sums, ones))
    total = _call(_total_kernel, [VMEM] * 4, [_rows(8)])(sums, below, above, across)[0]
    zacross = lax.ppermute(total, "dev", _z_shift(2))
    up, down = _call(_z_kernel, [VMEM] * 4, [_rows(168), _rows(168)])(own, below, above, total)
    zbelow = lax.ppermute(up, "dev", _z_shift(1))
    zabove = lax.ppermute(down, "dev", _z_shift(-1))

    mine, up, down, high, low, part = _call(
        _x_kernel,
        [VMEM] * 7,
        [_rows(640), _rows(MESSAGE), _rows(MESSAGE), _rows(64), _rows(64), _rows(8)],
    )(own, below, above, zbelow, zabove, total, zacross)
    xm1 = lax.ppermute(up, "grp", _x_shift(1))
    xp1 = lax.ppermute(down, "grp", _x_shift(-1))
    xm2 = lax.ppermute(high, "grp", _x_shift(2))
    xp2 = lax.ppermute(low, "grp", _x_shift(-2))
    bricks = []
    for ref, at, rows in (
        (xm1, functools.partial(_Sent, from_below=True), slice(8, 16)),
        (mine, _Own, slice(16, 24)),
        (xp1, functools.partial(_Sent, from_below=False), slice(24, 32)),
    ):
        kernel = functools.partial(_brick_kernel, at=at, rows=rows)
        outs = [_shape(2, FINE + 1, 8, LANES), _shape(2, 26, 8, LANES)]
        bricks.append(_call(kernel, [VMEM], outs, us=0.8)(ref))
    part, bricks = lax.optimization_barrier((part, bricks))
    tiles, fars = zip(*bricks)
    part, send = _call(_window_kernel, [VMEM] * 5, [_rows(8), _rows(8)])(part, xm1, xp1, xm2, xp2)
    xacross = lax.ppermute(send, "grp", [(x, (x + 3 - 6 * (x % 2)) % 8) for x in range(8)])

    start = _call(
        _coarse_kernel,
        [VMEM] * 8,
        [fine, fine, _shape(COARSE, 24, LANES)],
        [
            inner,
            inner,
            pltpu.VMEM((2, FINE + 1, 8, LANES), F32),
            pltpu.VMEM((COARSE, 32, LANES), F32),
            pltpu.VMEM((12, 24, LANES), F32),
            plane,
            plane,
            plane,
        ],
        us=3,
    )(*tiles, *fars, xm2, xp2)

    boxes = pltpu.VMEM((16 * BLOCK, LANES), F32)
    pot, res = _call(
        _cycle_kernel,
        [VMEM] * 12,
        [_shape(4, 16, 256), _shape(4, 16, 256)],
        [inner, inner, plane, plane, plane, boxes, pltpu.SMEM((8, LANES), jnp.int32), pltpu.SemaphoreType.DMA((1,))],
    )(order, *tiles, *start, *ones, part, xacross)
    return pot, res


def solution(mesh):
    table = _mean_weights()

    def body(divergence, box_coords, neighbors):
        return _body(jnp.asarray(table), divergence, box_coords, neighbors)

    split = P(("grp", "dev"), None, None)
    return jax.shard_map(
        body, mesh=mesh, in_specs=(split, P(), P()), out_specs=(split, split), check_vma=False
    )
```

```python
import functools

import numpy as np

import jax
import jax.numpy as jnp
from jax import lax
from jax.experimental import pallas as pl
from jax.experimental.pallas import tpu as pltpu
from jax.sharding import PartitionSpec as P

KC = 4
CYCLES = 2
W = 0.8 / 6.0
BETA = 0.8 / 1.5
CELLS = 128**3
BLOCK = 16
LANES = 128
F32 = jnp.float32


def _apply(v):
    total = 6.0 * v
    for axis in range(3):
        lo = [slice(None)] * 3
        hi = [slice(None)] * 3
        lo[axis], hi[axis] = slice(None, -1), slice(1, None)
        total[tuple(lo)] -= v[tuple(hi)]
        total[tuple(hi)] -= v[tuple(lo)]
    return total


def _mean_weights():
    ones = np.ones((128, 128, 128))
    relax = lambda v: v - W * _apply(v)
    k0 = _apply(ones)
    k1 = relax(k0)
    k2 = relax(k1)
    q = k2.reshape(64, 2, 64, 2, 64, 2).sum(axis=(1, 3, 5))
    s = np.zeros_like(q)
    for _ in range(KC):
        s = s + BETA * (q - 0.25 * _apply(s))
    back = np.repeat(np.repeat(np.repeat(s, 2, 0), 2, 1), 2, 2) / 8.0
    full = ones - W * (k0 + k1 + k2) - relax(back) + (s.sum() / CELLS) * relax(ones)
    blocks = []
    for x in (0, 3, 7):
        for y in (0, 1, 3):
            for z in (0, 1, 3):
                b = full[16 * x : 16 * x + 16, 32 * y : 32 * y + 32, 32 * z : 32 * z + 32]
                b = b.reshape(16, 4, 8, 2, 16).transpose(1, 3, 0, 2, 4)
                blocks.append(b.reshape(8, 16, LANES))
    return np.stack(blocks).astype(np.float32)


def _iota(shape, dim):
    return lax.broadcasted_iota(jnp.int32, shape, dim)


def _roll(v, shift, axis):
    shift = shift % v.shape[axis]
    return v if shift == 0 else pltpu.roll(v, shift, axis)


def _position():
    d = lax.axis_index("dev")
    return lax.axis_index("grp"), d // 4, d % 4


def _blk(ref, i):
    return ref[BLOCK * i : BLOCK * (i + 1), :]


def _put(ref, i, v):
    ref[BLOCK * i : BLOCK * (i + 1), :] = v


def _fetch_kernel(div, w2, raw, weight, sem):
    g, yb, zb = _position()
    kind = lambda i, n: jnp.where(i == 0, 0, jnp.where(i == n - 1, 2, 1))
    which = kind(g, 8) * 9 + kind(yb, 4) * 3 + kind(zb, 4)
    copies = (
        pltpu.make_async_copy(div, raw, sem.at[0]),
        pltpu.make_async_copy(w2.at[which], weight, sem.at[1]),
    )
    for copy in copies:
        copy.start()
    for copy in copies:
        copy.wait()


def _sort_kernel(coords, raw, weight, own, sums, order, up, down, plain):
    g, yb, zb = _position()
    row = _iota((16, LANES), 0)
    lane = _iota((16, LANES), 1)
    j, k = lane // 16, lane % 16
    edge_x = ((row == 0) & (g == 0)).astype(F32) + ((row == 15) & (g == 7)).astype(F32)
    s1 = jnp.zeros((16, LANES), F32)
    s2 = jnp.zeros((16, LANES), F32)
    box_of = _box_of(coords, g, yb, zb)
    row8 = _iota((8, LANES), 0)
    order[...] = sum(jnp.where(row8 == h, box_of[h], 0) for h in range(4))
    for o in range(4):
        for h in range(2):
            v = raw[box_of[(o // 2) * 2 + h], :, (o % 2) * LANES : (o % 2 + 1) * LANES]
            at = BLOCK * (o * 2 + h)
            plain[at : at + BLOCK, :] = v
            edge = edge_x
            if o == 0:
                edge += ((j == 0) & (yb == 0)).astype(F32)
            if o == 3:
                edge += ((j == 7) & (yb == 3)).astype(F32)
            if h == 0:
                edge += ((k == 0) & (zb == 0)).astype(F32)
            else:
                edge += ((k == 15) & (zb == 3)).astype(F32)
            s1 += (1.0 - W * edge) * v
            s2 += weight[o * 2 + h] * v
    for i in range(16):
        own[8 * i : 8 * i + 8, :] = plain[pl.ds(BLOCK * (i // 2) + i % 2, 8, stride=2), :]
    s1, s2 = (jnp.sum(v, axis=0, keepdims=True) for v in (s1, s2))
    sums[...] = jnp.where(row8 == 0, s1, jnp.where(row8 == 1, s2, 0.0))
    _y_messages(own, sums, up, down)


def _box_of(coords, g, yb, zb):
    mine = (g * 4 + yb) * 4 + zb
    at = pl.ds(pl.multiple_of(mine // 32 * LANES, LANES), LANES)
    slot = coords[1:2, at] % 2 * 2 + coords[2:3, at] % 2
    box = _iota((1, LANES), 1) - mine % 32 * 4
    inside = (box >= 0) & (box < 4)
    return [jnp.sum(jnp.where(inside & (slot == h), box, 0)) for h in range(4)]


def _ext(own, below, above, q, h):
    if q == 0:
        return _roll(_blk(below, 4), 64 * h, 1)
    if q < 3:
        return _blk(below, (q - 1) * 2 + h)
    if q < 7:
        return _blk(own, (q - 3) * 2 + h)
    if q < 9:
        return _blk(above, (q - 7) * 2 + h)
    return _roll(_blk(above, 4), 64 * h, 1)


def _pack_quads(pieces, src_quad):
    quad = _iota(pieces[0].shape, 1) % 16 // 4
    out = _roll(pieces[0], 4 * (0 - src_quad), 1)
    for s in range(1, len(pieces)):
        out = jnp.where(quad == s, _roll(pieces[s], 4 * (s - src_quad), 1), out)
    return out


Y_FAR, Y_SUMS, Y_MESSAGE = 64, 80, 88


def _y_messages(own, sums, up, down):
    half = _iota((BLOCK, LANES), 1) < 64
    for i in range(4):
        _put(up, i, _blk(own, i + 4))
        _put(down, i, _blk(own, i))
    _put(up, 4, jnp.where(half, _roll(_blk(own, 3), 64, 1), _blk(own, 2)))
    _put(down, 4, jnp.where(half, _blk(own, 4), _roll(_blk(own, 5), 64, 1)))
    for ref in (up, down):
        ref[Y_SUMS:Y_MESSAGE, :] = sums[...]


def _total_kernel(sums, below, above, across, total):
    total[...] = sums[...] + below[Y_SUMS:Y_MESSAGE, :] + above[Y_SUMS:Y_MESSAGE, :] + across[...]


def _z_kernel(own, below, above, total, up, down):
    ext = lambda q, h: _ext(own, below, above, q, h)
    for q in range(1, 9):
        _put(up, q - 1, ext(q, 1))
        _put(down, q - 1, ext(q, 0))
    for ref, near, quad in ((up, 1, 3), (down, 0, 0)):
        far = [ext(q, 1 - near) for q in range(2, 8)]
        _put(ref, 8, _pack_quads(far[:4], quad))
        _put(ref, 9, _pack_quads([*far[4:], ext(0, near), ext(9, near)], quad))
        ref[160:168, :] = total[...]


OUTER, SUMS, MESSAGE = 384, 480, 488
OWN_EY, OWN_COLS = 512, 576


def _rows_to(pieces):
    row = _iota((8, LANES), 0)
    out = None
    for i, (v, r) in enumerate(pieces):
        v = _roll(v, 2 * i - r, 0)
        out = v if out is None else jnp.where(row < 2 * i, out, v)
    return out


def _rows_far(near):
    return _iota((8, LANES), 0) // 2 == (0 if near else 3)


def _lower_lanes():
    return _iota((8, LANES), 1) % 16 < 8


def _hide(v, tile, near):
    return jnp.where(_rows_far(near), _roll(v, 2 if near else -2, 0), tile)


def _share(lo, hi, near):
    row, lane = _iota((8, LANES), 0), _iota((8, LANES), 1)
    middle = jnp.where(lane % 16 < 8, hi, lo)
    edge = jnp.where((row // 2) == near // 2, lo, _roll(hi, 2 if near else -2, 0))
    return jnp.where((row >= 2) & (row < 6), middle, edge)


def _x_kernel(own, below, above, zbelow, zabove, total, across, mine, up, down, high, low, part):
    ext = lambda q, h: _ext(own, below, above, q, h)
    extra = [ext(q, h) for q in (0, 9) for h in range(2)]
    extra += [_blk(zbelow, 8), _blk(zbelow, 9), _blk(zabove, 8), _blk(zabove, 9)]
    for i, v in enumerate(extra):
        _put(mine, 32 + i, v)
    two_away = []
    for q in range(1, 9):
        pieces = (_blk(zbelow, q - 1), ext(q, 0), ext(q, 1), _blk(zabove, q - 1))
        for p in range(4):
            _put(mine, (q - 1) * 4 + p, pieces[p])
        if 2 <= q <= 7:
            if 3 <= q <= 6:
                two_away += pieces[1:3]
            for ref, near in ((up, 6), (down, 0)):
                for p in (1, 2):
                    _put(ref, (q - 2) * 4 + p, pieces[p])
                for s in (0, 8):
                    lo, hi = (pieces[p][s : s + 8] for p in (0, 3))
                    far = _rows_far(near)
                    at = (q - 2) * 64 + s
                    ref[at : at + 8, :] = jnp.where(far & _lower_lanes(), hi, lo)
                    ref[at + 48 : at + 56, :] = _hide(extra[q - 2][s : s + 8], hi, near)
            continue
        at = OUTER + (0 if q == 1 else 48)
        for ref, near in ((up, 6), (down, 0)):
            for s in (0, 8):
                hidden = extra[6 if q == 1 else 7][s : s + 8]
                ref[at + s : at + s + 8, :] = _hide(hidden, pieces[1][s : s + 8], near)
            ref[at + 16 : at + 32, :] = pieces[2]
            for s in (0, 8):
                ref[at + 32 + s : at + 40 + s, :] = _share(pieces[0][s : s + 8], pieces[3][s : s + 8], near)
    half = _iota((BLOCK, LANES), 1) < 64
    two_away += [jnp.where(half, ext(7, h), ext(2, h)) for h in range(2)]
    for src, quad in ((zbelow, 3), (zabove, 0)):
        near = [_blk(src, q - 1) for q in range(2, 8)]
        two_away += [_pack_quads(near[:4], quad), _pack_quads(near[4:], quad)]
    for ref, r in ((high, 6), (low, 0)):
        for i in range(0, 14, 2):
            a, b = two_away[i : i + 2]
            ref[4 * i : 4 * i + 8, :] = _rows_to([(a[:8], r), (b[:8], r), (a[8:], r), (b[8:], r)])
    t = total[...] + zbelow[160:168, :] + zabove[160:168, :] + across[...]
    part[...] = t
    for ref, at in ((up, SUMS), (down, SUMS), (high, 56), (low, 56)):
        ref[at : at + 8, :] = t


def _window_kernel(mine, xm1, xp1, xm2, xp2, out, send):
    odd = _position()[0] % 2 == 1
    low = xm1[SUMS:MESSAGE, :] + xm2[56:64, :]
    high = xp1[SUMS:MESSAGE, :] + xp2[56:64, :]
    out[...] = mine[...] + (low + high)
    send[...] = mine[...] + jnp.where(odd, high, low)


FINE, COARSE = 40, 20


def _inside(pos, start, limit):
    return ((pos + start >= 0) & (pos + start < limit)).astype(F32)


def _ring_mask(g, zb):
    row = _iota((32, LANES), 0)
    offset = jnp.where(row < 4, row + 16, row - 16)
    return _inside(offset, g * 8, 64) * _inside(_iota((32, LANES), 1) % 64 - 16, zb * 32, 128)


def _fold_mask(yb):
    below, above = (yb > 0).astype(F32), (yb < 3).astype(F32)
    return jnp.where(_iota((8, LANES), 1) < 64, below, above)


def _tall(mask, n):
    return jnp.concatenate([mask] * (n // 8), axis=0)


def _blocks(first, count, size, fn):
    n = (count - 1) // size
    if n:

        def step(i, _):
            fn(first + i * size, size)
            return 0

        lax.fori_loop(0, n, step, 0)
    fn(first + n * size, count - n * size)


def _store(ref, i, v, last):
    ref[i] = v
    if isinstance(i, int) and i == last:
        ref[i + 1] = _roll(v, 64, 1)


def _lanes():
    lane = _iota((8, LANES), 1)
    return lane < 64, lane // 16


def _pick(cond, a, b):
    if a is None and b is None:
        return None
    return jnp.where(cond, 0.0 if a is None else a, 0.0 if b is None else b)


def _turn(v, shift):
    return None if v is None else _roll(v, shift, 1)


def _unfold(groups):
    half, block = _lanes()
    vs = [
        [_pick(half, a, c) for a, c in zip(low, high)] + [_turn(_pick(half, c, a), 64) for a, c in zip(low, high)]
        for low, high in groups
    ]
    for bit in (2, 1):
        vs = [_swap_bit(v, block, bit) for v in vs]
    return [[_pick(half, v[i], v[i ^ 3]) for i in range(8)] for v in vs]


def _swap_bit(v, block, bit):
    zero = (block & bit) == 0
    out = [None] * 8
    for i in range(8):
        if not i & bit:
            x, y = v[i], v[i | bit]
            out[i] = _pick(zero, x, _turn(y, 16 * bit))
            out[i | bit] = _pick(zero, _turn(x, -16 * bit), y)
    return out


def _refold(groups):
    half, block = _lanes()
    vs = [[_pick(half, rows[i], rows[i ^ 3]) for i in range(8)] for rows in groups]
    for bit in (1, 2):
        vs = [_swap_bit(v, block, bit) for v in vs]
    turned = [{p: _turn(v[p | 4], 64) for p in (1, 2)} for v in vs]
    return [
        ([_pick(half, v[p], u[p]) for p in (1, 2)], [_pick(half, u[p], v[p]) for p in (1, 2)])
        for v, u in zip(vs, turned)
    ]


class _Own:
    def __init__(self, ref):
        self.ref = ref

    def tile(self, at):
        return self.ref[at : at + 8, :]

    def core(self, q, p, s):
        return self.tile((q - 1) * 64 + 16 * p + 8 * s)

    def outer(self, i, s):
        return self.tile(OWN_EY + 16 * i + 8 * s)

    def quads(self, i, s):
        return self.tile(OWN_COLS + 16 * i + 8 * s)


class _Sent(_Own):
    def __init__(self, ref, from_below):
        self.ref, self.first = ref, 6 if from_below else 0

    def core(self, q, p, s):
        if 2 <= q <= 7:
            v = self.tile((q - 2) * 64 + 16 * p + 8 * s)
            return jnp.where(_rows_far(self.first), self.core(q, 0, s), v) if p == 3 else v
        at = OUTER + (0 if q == 1 else 48) + 8 * s
        if p in (1, 2):
            return self.tile(at + 16 * (p - 1))
        shared = self.tile(at + 32)
        if p == 0:
            return shared
        near = _iota((8, LANES), 0) // 2 == self.first // 2
        return jnp.where(near, _roll(shared, -2 if self.first else 2, 0), shared)

    def short(self, i, s):
        at = i * 64 + 48 if i < 6 else OUTER + 48 * (i - 6)
        return _roll(self.tile(at + 8 * s), -2 if self.first else 2, 0)

    def outer(self, i, s):
        return self.short(i, s)

    def quads(self, i, s):
        return self.short(4 + i, s)


def _pieces(at, q, s):
    if 1 <= q <= 8:
        return [at.core(q, p, s) for p in range(4)]
    slot = 2 if q == 0 else 3
    near = [_roll(at.quads(c, s), by, 1) for c, by in ((1, 4 * (3 - slot)), (3, -4 * slot))]
    return [near[0], *(at.outer((0 if q == 0 else 2) + h, s) for h in range(2)), near[1]]


def _far_pieces(at, q, s):
    c, slot = divmod(q - 2, 4)
    return [_roll(at.quads(c, s), -4 * slot, 1), None, None, _roll(at.quads(2 + c, s), 4 * (3 - slot), 1)]


def _unpack_brick(at, mask, mask_far, fold, store, store_far):
    for batch in ([(0, 0), (1, 0), (2, 0)], [(3, 0), (4, 0), (2, 1)], [(3, 1), (4, 1)]):
        tasks = [(q, far, s) for q, far in batch for s in range(2)]
        groups = [
            [(_far_pieces if far else _pieces)(at, o, s) for o in (q, 9 - q)] for q, far, s in tasks
        ]
        for (q, far, s), rows in zip(tasks, _unfold(groups)):
            m = _outer_mask(mask_far if far else mask, fold, q)
            for r in range(8):
                if far:
                    store_far(s, 8 * q + r - 15, rows[r] * m)
                else:
                    store(s, 8 * q + r, rows[r] * m)


def _outer_mask(mask, fold, q):
    return mask * fold if q < 3 else mask


def _far_mask(g, zb):
    row = _iota((24, LANES), 0) - 8
    lane = _iota((24, LANES), 1) % 64
    below, above = (zb > 0).astype(F32), (zb < 3).astype(F32)
    return _inside(row, g * 8, 64) * jnp.where(lane < 4, below, jnp.where(lane >= 60, above, 0.0))


def _brick_kernel(ref, tile, far, *, at, rows):
    g, yb, zb = _position()

    def store(s, i, v):
        tile[s, i] = v

    def put(s, i, v):
        far[s, i] = v

    mask_far = _far_mask(g, zb)[rows.start - 8 : rows.stop - 8]
    _unpack_brick(at(ref), _ring_mask(g, zb)[rows], mask_far, _fold_mask(yb), store, put)
    for s in range(2):
        tile[s, FINE] = _roll(tile[s, FINE - 1], 64, 1)
        far[s, FINE - 15] = _roll(far[s, FINE - 16], 64, 1)


def _beside(s, *tiles):
    return lambda i: jnp.concatenate([t[s, i] for t in tiles], axis=0)


def _coarse_kernel(t1, t2, t3, f1, f2, f3, xm2, xp2, Ae, Ao, source, Be, Bo, ahead_of, raw, beyond, cs, c0, c1):
    g, yb, zb = _position()
    ring, fold = _ring_mask(g, zb), _fold_mask(yb)
    De, Do = D = [_beside(s, t1, t2, t3) for s in range(2)]
    far_e, far_o = [_beside(s, f1, f2, f3) for s in range(2)]

    row = _iota((8, LANES), 0)

    def near(i, s):
        at, r = slice(8 * (i // 2), 8 * (i // 2) + 8), 4 * s + 2 * (i % 2)
        return jnp.where(row < 4, _roll(xp2[at, :], -r, 0), _roll(xm2[at, :], 6 - r, 0))

    def ahead(q, s):
        c, slot = divmod(q - 2, 4)
        lo = _roll(near(10 + c, s), 4 * (3 - slot), 1)
        hi = _roll(near(12 + c, s), -4 * slot, 1)
        at = 2 * (q - 3) if 3 <= q <= 6 else 8
        return [lo, near(at, s), near(at + 1, s), hi]

    tasks = [(q, s) for q in range(2, 5) for s in range(2)]
    for (q, s), rows in zip(tasks, _unfold([(ahead(q, s), ahead(9 - q, s)) for q, s in tasks])):
        m = _outer_mask(ring[:8], fold, q)
        for r in range(8):
            _store(ahead_of.at[s], 8 * q + r, rows[r] * m, FINE - 1)

    def patch(rows, pairs):
        lane = _iota((24, LANES), 1) % 64
        sums = []
        for i in rows:
            f = 2 * i - 15
            e, o = far_e(f) + far_e(f + 1), far_o(f) + far_o(f + 1)
            sums.append((e, o, e + o, (far_e(f - 1) + far_e(f + 2)) + (far_o(f - 1) + far_o(f + 2))))
        turned = [_roll(o, 1, 0) + _roll(e, -1, 0) for e, o, _, _ in sums]
        hs = [(1.0 - 3.0 * W) * fp + W * (outer + t) for (_, _, fp, outer), t in zip(sums, turned)]
        ends = [(_roll(fp, -3, 1), _roll(fp, 2, 1)) for _, _, fp, _ in sums]
        sides = []
        for (_, _, fp, _), h, pair in zip(sums, hs, pairs):
            lo = _roll(h, -2, 1) + _roll(h, -3, 1) + W * (_roll(fp, -1, 1) + pair)
            hi = _roll(h, 2, 1) + _roll(h, 3, 1) + W * (_roll(fp, 1, 1) + pair)
            sides.append((lo, hi))
        for i, (lo, hi) in zip(rows, sides):
            low = jnp.where(lane == 0, lo, _roll(lo, 1, 1))
            high = jnp.where(lane == 63, hi, _roll(hi, -1, 1))
            beyond[i - 10] = jnp.where(lane < 32, low, high) * 0.125
        return ends

    def put_source(i, c):
        raw[i] = c

    whole = [lambda y, s=s, v=v: jnp.concatenate([ahead_of[s, y], v(y)], axis=0) for s, v in enumerate(D)]
    args = (whole, 32, W, 1.0 - 5.0 * W, None)
    _restrict(*args, 3, 7, put_source, None, 7)
    _restrict(*args, 10, 10, put_source, patch, 10)
    _sweep_three(g, yb, zb, lambda i: raw[i], lambda i: beyond[i], cs, c0, c1)
    base = [lambda i, v=v: W * v(i) for v in D]
    step_masks = _step_masks(g, yb, zb)
    _correct_and_smooth(step_masks, base, D, lambda i: c0[i], Be, Bo, 7, 13, 13)
    _smooth(step_masks, (lambda i: Be[i], lambda i: Bo[i]), D, Ae, Ao, 15, 25, 25)
    pair_of = lambda i: (De(i) + De(i + 1)) + (Do(i) + Do(i + 1))
    A = (lambda i: Ae[i], lambda i: Ao[i])
    _restrict(A, 24, 1.0, -5.0, pair_of, 8, 12, lambda i, c: _set(source, i, c), None, 6)


def _set(ref, i, v):
    ref[i] = v


def _ones_kernel(Te, To, source, Be, Bo, cs, c0, c1):
    g, yb, zb = _position()
    one = jnp.ones((32, LANES), F32)
    _sweep_three(g, yb, zb, lambda i: one, lambda i: one[8:], cs, c0, c1)
    step_masks = _step_masks(g, yb, zb)
    _correct_and_smooth(step_masks, None, None, lambda i: c0[i], Be, Bo, 7, 13, 13)
    _smooth(step_masks, (lambda i: Be[i], lambda i: Bo[i]), None, Te, To, 15, 25, 25)
    T = (lambda i: Te[i], lambda i: To[i])
    _restrict(T, 24, 1.0, -5.0, None, 8, 12, lambda i, c: _set(source, i, c), None, 6)


def _sweep_three(g, yb, zb, source, beyond, cs, c0, c1):
    ring, fold = BETA * _ring_mask(g, zb), _fold_mask(yb)
    outside = ring * _tall(fold, 32)
    lane = _iota((24, LANES), 1) % 64
    has_below, has_above = (zb > 0).astype(F32), (zb < 3).astype(F32)
    row = _iota((24, LANES), 0) - 8
    z_ends = jnp.where(lane < 2, has_below, jnp.where(lane >= 62, has_above, 0.0))
    beyond_mask = BETA * z_ends * _inside(row, g * 8, 64)
    beyond_outside = beyond_mask * _tall(fold, 24)
    mask = _ring_mask(g, zb)[8:]
    masks = (mask * _tall(fold, 24), mask)

    scaled = _lazily(lambda i: source(i) * (outside if i < 12 else ring))
    for i in range(4, COARSE):
        c = scaled(i)
        after = _roll(c, 64, 1) if i == COARSE - 1 else scaled(i + 1)
        near = (_roll(c, 1, 0) + _roll(c, -1, 0) + (scaled(i - 1) + after))[8:]
        c = c[8:]
        ends = None
        if i >= 10:
            ends = beyond(i - 10) * (beyond_outside if i < 12 else beyond_mask)
        cs[i] = c
        turns = _roll(c, 2, 1), _roll(c, -2, 1)
        _store(c0, i, c + _sweep(c, near, turns, lane, ends) * masks[i >= 12], COARSE - 1)
    _sweep_rows(c0, c1, cs, 5, masks)
    _sweep_rows(c1, c0, cs, 6, masks)


def _sweep(c, near, turns, lane, ends):
    before, after = turns
    if ends is not None:
        before = jnp.where(lane < 2, ends, before)
        after = jnp.where(lane >= 62, ends, after)
    return 0.2 * c + W * (near + (before + after))


def _sweep_rows(src, dst, cs, first, masks, batch=6):
    for start in range(first, COARSE, batch):
        rows = range(start, min(start + batch, COARSE))
        turned = [
            (_roll(src[i], 1, 0), _roll(src[i], -1, 0), _roll(src[i], 2, 1), _roll(src[i], -2, 1)) for i in rows
        ]
        for i, (low, high, *turns) in zip(rows, turned):
            near = (low + high) + (src[i - 1] + src[i + 1])
            _store(dst, i, cs[i] + _sweep(src[i], near, turns, None, None) * masks[i >= 12], COARSE - 1)


def _restrict(fields, rows, near, centre, more, first, count, store, patch, size):
    lane = _iota((rows, LANES), 1)
    even = lane % 2 == 0

    for start in range(first, first + count, size):
        even_at, odd_at = (_lazily(lambda u, v=v, start=start: v(2 * start + u)) for v in fields)
        sums = []
        us = range(min(size, first + count - start))
        for u in us:
            y = 2 * u
            ee, eo = even_at(y) + even_at(y + 1), odd_at(y) + odd_at(y + 1)
            outer = (even_at(y - 1) + even_at(y + 2)) + (odd_at(y - 1) + odd_at(y + 2))
            sums.append((ee, eo, ee + eo, outer))
        turned = [_roll(eo, 1, 0) + _roll(ee, -1, 0) for ee, eo, _, _ in sums]
        hs = []
        for u, ((_, _, pair, outer), t) in enumerate(zip(sums, turned)):
            h = (centre + 2.0 * near) * pair + near * (outer + t)
            hs.append(h if more is None else h + more(2 * (start + u)))
        sides = [(_roll(pair, 1, 1), _roll(pair, -2, 1)) for _, _, pair, _ in sums]
        if patch is not None:
            ends = patch([start + u for u in us], [pair[8:] for _, _, pair, _ in sums])
            for u, ((before, after), (low, high)) in enumerate(zip(sides, ends)):
                low = jnp.where(lane[8:] % 64 == 0, low, before[8:])
                high = jnp.where(lane[8:] % 64 == 62, high, after[8:])
                sides[u] = (
                    jnp.concatenate([before[:8], low], axis=0),
                    jnp.concatenate([after[:8], high], axis=0),
                )
        cs = [h + _roll(h, -1, 1) + near * (before + after) for h, (before, after) in zip(hs, sides)]
        cs = [jnp.where(even, c, _roll(c, 1, 1)) * 0.125 for c in cs]
        for u, c in enumerate(cs):
            store(start + u, c)


def _step_masks(g, yb, zb):
    mask = _ring_mask(g, zb)[8:]
    masks = (mask * _tall(_fold_mask(yb), 24), mask)
    return masks, [0.2 * m for m in masks], [W * m for m in masks]


def _of_row(pair, i, own_first):
    if isinstance(i, int):
        return pair[i >= own_first]
    return jnp.where(i < own_first, *pair)


def _relax(even, odd, i, n, store, batch=4):
    for first in range(0, n, batch):
        us = range(first, min(first + batch, n))
        turned = []
        for u in us:
            e, o = even(u), odd(u)
            turned.append((_roll(e, 1, 1), _roll(e, -1, 1), _roll(o, 1, 1), _roll(o, -1, 1), _roll(o, 1, 0), _roll(e, -1, 0)))
        for u, (e1, e2, o1, o2, before, after) in zip(us, turned):
            e, o = even(u), odd(u)
            ye = ((even(u - 1) + even(u + 1)) + (e1 + e2)) + (o + before)
            yo = ((odd(u - 1) + odd(u + 1)) + (o1 + o2)) + (e + after)
            store(i + u, e, o, ye, yo)


def _smooth_to(step_masks, D, dst_e, dst_o):
    def store(i, e, o, ye, yo):
        m, n = _of_row(step_masks[1], i, 24), _of_row(step_masks[2], i, 24)
        if D is not None:
            ye, yo = ye + D[0](i), yo + D[1](i)
        _store(dst_e, i, e * m + ye * n, FINE - 1)
        _store(dst_o, i, o * m + yo * n, FINE - 1)

    return store


def _smooth(step_masks, src, D, dst_e, dst_o, first, count, size):
    def fn(i, n):
        even, odd = (_lazily(lambda u, v=v: v(i + u)) for v in src)
        _relax(even, odd, i, n, _smooth_to(step_masks, D, dst_e, dst_o))

    _blocks(first, count, size, fn)


def _correct_and_smooth(step_masks, base, D, correction, dst_e, dst_o, first, count, size):
    def fn(start, n):
        i = 2 * start
        c = _lazily(lambda u: correction(start + u))
        if base is None:
            even = odd = lambda u: c(u // 2)
        else:
            even, odd = (_lazily(lambda u, v=v: v(i + u) + c(u // 2)) for v in base)
        _relax(even, odd, i, 2 * n, _smooth_to(step_masks, D, dst_e, dst_o))

    _blocks(first, count, size, fn)


def _cycle_kernel(
    order, t1, t2, t3, Re, Ro, raw, Te, To, raw_one, part, across, pot, res, Be, Bo, cs, c0, c1, boxes, stage, place, sem
):
    g, yb, zb = _position()
    fetch = pltpu.make_async_copy(order, place, sem.at[0])
    fetch.start()
    totals = part[...] + across[...]
    means = jnp.sum(totals, axis=1, keepdims=True) * (1.0 / CELLS)
    mean1 = jnp.broadcast_to(means[0:1], (24, LANES))
    mean2 = jnp.broadcast_to(means[1:2], (24, LANES))
    step_masks = _step_masks(g, yb, zb)
    masks = step_masks[0]

    all_of = lambda ref: lambda i: ref[i]

    De, Do = D = [_beside(s, t1, t2, t3) for s in range(2)]
    A = (lambda i: Re[i] - mean1 * Te[i], lambda i: Ro[i] - mean1 * To[i])

    for i in range(8, COARSE):
        c = raw[i] - mean1 * raw_one[i] - mean2
        _store(cs, i, c * (masks[i >= 12] * BETA), COARSE - 1)
    _sweep_rows(cs, c0, cs, 9, masks)
    _sweep_rows(c0, c1, cs, 10, masks)
    _sweep_rows(c1, c0, cs, 11, masks)
    _correct_and_smooth(step_masks, A, D, all_of(c0), Be, Bo, 11, 9, 9)

    fetch.wait()
    box_of = [place[h, 0] for h in range(4)]

    def send(f, groups, out):
        for q in (3, 4):
            for s, sides in enumerate(_refold(groups(q))):
                for o, pieces in zip((q - 3, 6 - q), sides):
                    for h in range(2):
                        at = BLOCK * ((f * 4 + o) * 2 + h) + s
                        boxes[pl.ds(at, 8, stride=2), :] = pieces[h]
        for o in range(4):
            for h in range(2):
                v = _blk(boxes, (f * 4 + o) * 2 + h)
                stage[f, box_of[(o // 2) * 2 + h], :, (o % 2) * LANES : (o % 2 + 1) * LANES] = v
        copy = pltpu.make_async_copy(stage.at[f], out, sem.at[1 + f])
        copy.start()
        return copy

    sent = [send(0, lambda q: [[v[8 * q + u, 8:16, :] for u in range(8)] for v in (Be, Bo)], pot)]

    def residual(q):
        left = ([], [])

        def store(i, e, o, ye, yo):
            left[0].append(t2[0, i] - (6.0 * e - ye)[8:16])
            left[1].append(t2[1, i] - (6.0 * o - yo)[8:16])

        even, odd = (_lazily(lambda u, v=v: v[8 * q + u]) for v in (Be, Bo))
        _relax(even, odd, 8 * q, 8, store)
        return left

    sent.append(send(1, residual, res))
    for copy in sent:
        copy.wait()


def _lazily(fn):
    made = {}

    def get(u):
        if u not in made:
            made[u] = fn(u)
        return made[u]

    return get


def _shape(*dims):
    return jax.ShapeDtypeStruct(dims, F32)


def _rows(n):
    return _shape(n, LANES)


VMEM = pl.BlockSpec(memory_space=pltpu.VMEM)
HBM = pl.BlockSpec(memory_space=pltpu.HBM)


def _call(kernel, specs, outs, scratch=(), us=0.1, grant=40.0, to=VMEM):
    return pl.pallas_call(
        kernel,
        out_shape=outs,
        in_specs=specs,
        out_specs=[to] * len(outs),
        scratch_shapes=scratch,
        cost_estimate=pl.CostEstimate(flops=0, transcendentals=0, bytes_accessed=int(us * 3.5e6)),
        compiler_params=pltpu.CompilerParams(vmem_limit_bytes=int(grant * 2**20)),
    )


def _y_shift(n):
    return [(4 * y + z, 4 * ((y + n) % 4) + z) for y in range(4) for z in range(4)]


def _z_shift(n):
    return [(4 * y + z, 4 * y + (z + n) % 4) for y in range(4) for z in range(4)]


def _x_shift(n):
    return [(x, (x + n) % 8) for x in range(8)]


def _body(weights, divergence, box_coords, neighbors):
    coords = box_coords.T
    raw, weight = _call(
        _fetch_kernel,
        [HBM, HBM],
        [_shape(*divergence.shape), _shape(*weights.shape[1:])],
        [pltpu.SemaphoreType.DMA((2,))],
        us=1.0,
        grant=53.79,
    )(divergence, weights)
    own, sums, order, up, down = _call(
        _sort_kernel,
        [VMEM] * 3,
        [
            *(_rows(128), _rows(8), jax.ShapeDtypeStruct((8, LANES), jnp.int32)),
            *(_rows(Y_MESSAGE), _rows(Y_MESSAGE)),
        ],
        [pltpu.VMEM((128, LANES), F32)],
    )(coords, raw, weight)
    across = lax.ppermute(sums, "dev", _y_shift(2))
    below = lax.ppermute(up, "dev", _y_shift(1))
    above = lax.ppermute(down, "dev", _y_shift(-1))

    plane = pltpu.VMEM((COARSE + 1, 24, LANES), F32)
    fine = _shape(FINE + 1, 24, LANES)
    inner = pltpu.VMEM((FINE + 1, 24, LANES), F32)
    ones = _call(_ones_kernel, [], [fine, fine, _shape(COARSE, 24, LANES)], [inner, inner, plane, plane, plane], us=1.0)()
    sums, ones = lax.optimization_barrier((sums, ones))
    total = _call(_total_kernel, [VMEM] * 4, [_rows(8)])(sums, below, above, across)[0]
    zacross = lax.ppermute(total, "dev", _z_shift(2))
    up, down = _call(_z_kernel, [VMEM] * 4, [_rows(168), _rows(168)])(own, below, above, total)
    zbelow = lax.ppermute(up, "dev", _z_shift(1))
    zabove = lax.ppermute(down, "dev", _z_shift(-1))

    mine, up, down, high, low, part = _call(
        _x_kernel,
        [VMEM] * 7,
        [_rows(640), _rows(MESSAGE), _rows(MESSAGE), _rows(64), _rows(64), _rows(8)],
    )(own, below, above, zbelow, zabove, total, zacross)
    xm1 = lax.ppermute(up, "grp", _x_shift(1))
    xp1 = lax.ppermute(down, "grp", _x_shift(-1))
    xm2 = lax.ppermute(high, "grp", _x_shift(2))
    xp2 = lax.ppermute(low, "grp", _x_shift(-2))
    bricks = []
    for ref, at, rows in (
        (xm1, functools.partial(_Sent, from_below=True), slice(8, 16)),
        (mine, _Own, slice(16, 24)),
        (xp1, functools.partial(_Sent, from_below=False), slice(24, 32)),
    ):
        kernel = functools.partial(_brick_kernel, at=at, rows=rows)
        outs = [_shape(2, FINE + 1, 8, LANES), _shape(2, 26, 8, LANES)]
        bricks.append(_call(kernel, [VMEM], outs, us=0.8)(ref))
    part, bricks = lax.optimization_barrier((part, bricks))
    tiles, fars = zip(*bricks)
    part, send = _call(_window_kernel, [VMEM] * 5, [_rows(8), _rows(8)])(part, xm1, xp1, xm2, xp2)
    xacross = lax.ppermute(send, "grp", [(x, (x + 3 - 6 * (x % 2)) % 8) for x in range(8)])

    start = _call(
        _coarse_kernel,
        [VMEM] * 8,
        [fine, fine, _shape(COARSE, 24, LANES)],
        [
            inner,
            inner,
            pltpu.VMEM((2, FINE + 1, 8, LANES), F32),
            pltpu.VMEM((COARSE, 32, LANES), F32),
            pltpu.VMEM((12, 24, LANES), F32),
            plane,
            plane,
            plane,
        ],
        us=3,
    )(*tiles, *fars, xm2, xp2)

    boxes = pltpu.VMEM((16 * BLOCK, LANES), F32)
    pot, res = _call(
        _cycle_kernel,
        [VMEM] * 12,
        [_shape(4, 16, 256), _shape(4, 16, 256)],
        [inner, inner, plane, plane, plane, boxes, pltpu.VMEM((2, 4, 16, 256), F32), pltpu.SMEM((8, LANES), jnp.int32), pltpu.SemaphoreType.DMA((3,))],
        to=HBM,
    )(order, *tiles, *start, *ones, part, xacross)
    return pot, res


def solution(mesh):
    table = _mean_weights()

    def body(divergence, box_coords, neighbors):
        return _body(jnp.asarray(table), divergence, box_coords, neighbors)

    split = P(("grp", "dev"), None, None)
    return jax.shard_map(
        body, mesh=mesh, in_specs=(split, P(), P()), out_specs=(split, split), check_vma=False
    )
```

```python
import functools

import numpy as np

import jax
import jax.numpy as jnp
from jax import lax
from jax.experimental import pallas as pl
from jax.experimental.pallas import tpu as pltpu
from jax.sharding import PartitionSpec as P

KC = 4
CYCLES = 2
W = 0.8 / 6.0
BETA = 0.8 / 1.5
CELLS = 128**3
BLOCK = 16
LANES = 128
F32 = jnp.float32


def _apply(v):
    total = 6.0 * v
    for axis in range(3):
        lo = [slice(None)] * 3
        hi = [slice(None)] * 3
        lo[axis], hi[axis] = slice(None, -1), slice(1, None)
        total[tuple(lo)] -= v[tuple(hi)]
        total[tuple(hi)] -= v[tuple(lo)]
    return total


def _mean_weights():
    ones = np.ones((128, 128, 128))
    relax = lambda v: v - W * _apply(v)
    k0 = _apply(ones)
    k1 = relax(k0)
    k2 = relax(k1)
    q = k2.reshape(64, 2, 64, 2, 64, 2).sum(axis=(1, 3, 5))
    s = np.zeros_like(q)
    for _ in range(KC):
        s = s + BETA * (q - 0.25 * _apply(s))
    back = np.repeat(np.repeat(np.repeat(s, 2, 0), 2, 1), 2, 2) / 8.0
    full = ones - W * (k0 + k1 + k2) - relax(back) + (s.sum() / CELLS) * relax(ones)
    blocks = []
    for x in (0, 3, 7):
        for y in (0, 1, 3):
            for z in (0, 1, 3):
                b = full[16 * x : 16 * x + 16, 32 * y : 32 * y + 32, 32 * z : 32 * z + 32]
                b = b.reshape(16, 4, 8, 2, 16).transpose(1, 3, 0, 2, 4)
                blocks.append(b.reshape(8, 16, LANES))
    return np.stack(blocks).astype(np.float32)


def _iota(shape, dim):
    return lax.broadcasted_iota(jnp.int32, shape, dim)


def _roll(v, shift, axis):
    shift = shift % v.shape[axis]
    return v if shift == 0 else pltpu.roll(v, shift, axis)


def _position():
    d = lax.axis_index("dev")
    return lax.axis_index("grp"), d // 4, d % 4


def _blk(ref, i):
    return ref[BLOCK * i : BLOCK * (i + 1), :]


def _put(ref, i, v):
    ref[BLOCK * i : BLOCK * (i + 1), :] = v


def _fetch_kernel(div, w2, raw, weight, sem):
    g, yb, zb = _position()
    kind = lambda i, n: jnp.where(i == 0, 0, jnp.where(i == n - 1, 2, 1))
    which = kind(g, 8) * 9 + kind(yb, 4) * 3 + kind(zb, 4)
    copies = (
        pltpu.make_async_copy(div, raw, sem.at[0]),
        pltpu.make_async_copy(w2.at[which], weight, sem.at[1]),
    )
    for copy in copies:
        copy.start()
    for copy in copies:
        copy.wait()


def _sort_kernel(coords, raw, weight, own, sums, order, up, down, plain):
    g, yb, zb = _position()
    row = _iota((16, LANES), 0)
    lane = _iota((16, LANES), 1)
    j, k = lane // 16, lane % 16
    edge_x = ((row == 0) & (g == 0)).astype(F32) + ((row == 15) & (g == 7)).astype(F32)
    s1 = jnp.zeros((16, LANES), F32)
    s2 = jnp.zeros((16, LANES), F32)
    box_of = _box_of(coords, g, yb, zb)
    row8 = _iota((8, LANES), 0)
    order[...] = sum(jnp.where(row8 == h, box_of[h], 0) for h in range(4))
    for o in range(4):
        for h in range(2):
            v = raw[box_of[(o // 2) * 2 + h], :, (o % 2) * LANES : (o % 2 + 1) * LANES]
            at = BLOCK * (o * 2 + h)
            plain[at : at + BLOCK, :] = v
            edge = edge_x
            if o == 0:
                edge += ((j == 0) & (yb == 0)).astype(F32)
            if o == 3:
                edge += ((j == 7) & (yb == 3)).astype(F32)
            if h == 0:
                edge += ((k == 0) & (zb == 0)).astype(F32)
            else:
                edge += ((k == 15) & (zb == 3)).astype(F32)
            s1 += (1.0 - W * edge) * v
            s2 += weight[o * 2 + h] * v
    for i in range(16):
        own[8 * i : 8 * i + 8, :] = plain[pl.ds(BLOCK * (i // 2) + i % 2, 8, stride=2), :]
    s1, s2 = (jnp.sum(v, axis=0, keepdims=True) for v in (s1, s2))
    sums[...] = jnp.where(row8 == 0, s1, jnp.where(row8 == 1, s2, 0.0))
    _y_messages(own, sums, up, down)


def _box_of(coords, g, yb, zb):
    mine = (g * 4 + yb) * 4 + zb
    at = pl.ds(pl.multiple_of(mine // 32 * LANES, LANES), LANES)
    slot = coords[1:2, at] % 2 * 2 + coords[2:3, at] % 2
    box = _iota((1, LANES), 1) - mine % 32 * 4
    inside = (box >= 0) & (box < 4)
    return [jnp.sum(jnp.where(inside & (slot == h), box, 0)) for h in range(4)]


def _ext(own, below, above, q, h):
    if q == 0:
        return _roll(_blk(below, 4), 64 * h, 1)
    if q < 3:
        return _blk(below, (q - 1) * 2 + h)
    if q < 7:
        return _blk(own, (q - 3) * 2 + h)
    if q < 9:
        return _blk(above, (q - 7) * 2 + h)
    return _roll(_blk(above, 4), 64 * h, 1)


def _pack_quads(pieces, src_quad):
    quad = _iota(pieces[0].shape, 1) % 16 // 4
    out = _roll(pieces[0], 4 * (0 - src_quad), 1)
    for s in range(1, len(pieces)):
        out = jnp.where(quad == s, _roll(pieces[s], 4 * (s - src_quad), 1), out)
    return out


Y_FAR, Y_SUMS, Y_MESSAGE = 64, 80, 88


def _y_messages(own, sums, up, down):
    half = _iota((BLOCK, LANES), 1) < 64
    for i in range(4):
        _put(up, i, _blk(own, i + 4))
        _put(down, i, _blk(own, i))
    _put(up, 4, jnp.where(half, _roll(_blk(own, 3), 64, 1), _blk(own, 2)))
    _put(down, 4, jnp.where(half, _blk(own, 4), _roll(_blk(own, 5), 64, 1)))
    for ref in (up, down):
        ref[Y_SUMS:Y_MESSAGE, :] = sums[...]


def _total_kernel(sums, below, above, across, total):
    total[...] = sums[...] + below[Y_SUMS:Y_MESSAGE, :] + above[Y_SUMS:Y_MESSAGE, :] + across[...]


def _z_kernel(own, below, above, total, up, down):
    ext = lambda q, h: _ext(own, below, above, q, h)
    for q in range(1, 9):
        _put(up, q - 1, ext(q, 1))
        _put(down, q - 1, ext(q, 0))
    for ref, near, quad in ((up, 1, 3), (down, 0, 0)):
        far = [ext(q, 1 - near) for q in range(2, 8)]
        _put(ref, 8, _pack_quads(far[:4], quad))
        _put(ref, 9, _pack_quads([*far[4:], ext(0, near), ext(9, near)], quad))
        ref[160:168, :] = total[...]


OUTER, SUMS, MESSAGE = 384, 480, 488
OWN_EY, OWN_COLS = 512, 576


def _rows_to(pieces):
    row = _iota((8, LANES), 0)
    out = None
    for i, (v, r) in enumerate(pieces):
        v = _roll(v, 2 * i - r, 0)
        out = v if out is None else jnp.where(row < 2 * i, out, v)
    return out


def _rows_far(near):
    return _iota((8, LANES), 0) // 2 == (0 if near else 3)


def _lower_lanes():
    return _iota((8, LANES), 1) % 16 < 8


def _hide(v, tile, near):
    return jnp.where(_rows_far(near), _roll(v, 2 if near else -2, 0), tile)


def _share(lo, hi, near):
    row, lane = _iota((8, LANES), 0), _iota((8, LANES), 1)
    middle = jnp.where(lane % 16 < 8, hi, lo)
    edge = jnp.where((row // 2) == near // 2, lo, _roll(hi, 2 if near else -2, 0))
    return jnp.where((row >= 2) & (row < 6), middle, edge)


def _x_kernel(own, below, above, zbelow, zabove, total, across, mine, up, down, high, low, part):
    ext = lambda q, h: _ext(own, below, above, q, h)
    extra = [ext(q, h) for q in (0, 9) for h in range(2)]
    extra += [_blk(zbelow, 8), _blk(zbelow, 9), _blk(zabove, 8), _blk(zabove, 9)]
    for i, v in enumerate(extra):
        _put(mine, 32 + i, v)
    two_away = []
    for q in range(1, 9):
        pieces = (_blk(zbelow, q - 1), ext(q, 0), ext(q, 1), _blk(zabove, q - 1))
        for p in range(4):
            _put(mine, (q - 1) * 4 + p, pieces[p])
        if 2 <= q <= 7:
            if 3 <= q <= 6:
                two_away += pieces[1:3]
            for ref, near in ((up, 6), (down, 0)):
                for p in (1, 2):
                    _put(ref, (q - 2) * 4 + p, pieces[p])
                for s in (0, 8):
                    lo, hi = (pieces[p][s : s + 8] for p in (0, 3))
                    far = _rows_far(near)
                    at = (q - 2) * 64 + s
                    ref[at : at + 8, :] = jnp.where(far & _lower_lanes(), hi, lo)
                    ref[at + 48 : at + 56, :] = _hide(extra[q - 2][s : s + 8], hi, near)
            continue
        at = OUTER + (0 if q == 1 else 48)
        for ref, near in ((up, 6), (down, 0)):
            for s in (0, 8):
                hidden = extra[6 if q == 1 else 7][s : s + 8]
                ref[at + s : at + s + 8, :] = _hide(hidden, pieces[1][s : s + 8], near)
            ref[at + 16 : at + 32, :] = pieces[2]
            for s in (0, 8):
                ref[at + 32 + s : at + 40 + s, :] = _share(pieces[0][s : s + 8], pieces[3][s : s + 8], near)
    half = _iota((BLOCK, LANES), 1) < 64
    two_away += [jnp.where(half, ext(7, h), ext(2, h)) for h in range(2)]
    for src, quad in ((zbelow, 3), (zabove, 0)):
        near = [_blk(src, q - 1) for q in range(2, 8)]
        two_away += [_pack_quads(near[:4], quad), _pack_quads(near[4:], quad)]
    for ref, r in ((high, 6), (low, 0)):
        for i in range(0, 14, 2):
            a, b = two_away[i : i + 2]
            ref[4 * i : 4 * i + 8, :] = _rows_to([(a[:8], r), (b[:8], r), (a[8:], r), (b[8:], r)])
    t = total[...] + zbelow[160:168, :] + zabove[160:168, :] + across[...]
    part[...] = t
    for ref, at in ((up, SUMS), (down, SUMS), (high, 56), (low, 56)):
        ref[at : at + 8, :] = t


def _window_kernel(mine, xm1, xp1, xm2, xp2, out, send):
    odd = _position()[0] % 2 == 1
    low = xm1[SUMS:MESSAGE, :] + xm2[56:64, :]
    high = xp1[SUMS:MESSAGE, :] + xp2[56:64, :]
    out[...] = mine[...] + (low + high)
    send[...] = mine[...] + jnp.where(odd, high, low)


FINE, COARSE = 40, 20


def _inside(pos, start, limit):
    return ((pos + start >= 0) & (pos + start < limit)).astype(F32)


def _ring_mask(g, zb):
    row = _iota((32, LANES), 0)
    offset = jnp.where(row < 4, row + 16, row - 16)
    return _inside(offset, g * 8, 64) * _inside(_iota((32, LANES), 1) % 64 - 16, zb * 32, 128)


def _fold_mask(yb):
    below, above = (yb > 0).astype(F32), (yb < 3).astype(F32)
    return jnp.where(_iota((8, LANES), 1) < 64, below, above)


def _tall(mask, n):
    return jnp.concatenate([mask] * (n // 8), axis=0)


def _blocks(first, count, size, fn):
    n = (count - 1) // size
    if n:

        def step(i, _):
            fn(first + i * size, size)
            return 0

        lax.fori_loop(0, n, step, 0)
    fn(first + n * size, count - n * size)


def _store(ref, i, v, last):
    ref[i] = v
    if isinstance(i, int) and i == last:
        ref[i + 1] = _roll(v, 64, 1)


def _lanes():
    lane = _iota((8, LANES), 1)
    return lane < 64, lane // 16


def _pick(cond, a, b):
    if a is None and b is None:
        return None
    return jnp.where(cond, 0.0 if a is None else a, 0.0 if b is None else b)


def _turn(v, shift):
    return None if v is None else _roll(v, shift, 1)


def _unfold(groups):
    half, block = _lanes()
    vs = [
        [_pick(half, a, c) for a, c in zip(low, high)] + [_turn(_pick(half, c, a), 64) for a, c in zip(low, high)]
        for low, high in groups
    ]
    for bit in (2, 1):
        vs = [_swap_bit(v, block, bit) for v in vs]
    return [[_pick(half, v[i], v[i ^ 3]) for i in range(8)] for v in vs]


def _swap_bit(v, block, bit):
    zero = (block & bit) == 0
    out = [None] * 8
    for i in range(8):
        if not i & bit:
            x, y = v[i], v[i | bit]
            out[i] = _pick(zero, x, _turn(y, 16 * bit))
            out[i | bit] = _pick(zero, _turn(x, -16 * bit), y)
    return out


def _refold(groups):
    half, block = _lanes()
    vs = [[_pick(half, rows[i], rows[i ^ 3]) for i in range(8)] for rows in groups]
    for bit in (1, 2):
        vs = [_swap_bit(v, block, bit) for v in vs]
    turned = [{p: _turn(v[p | 4], 64) for p in (1, 2)} for v in vs]
    return [
        ([_pick(half, v[p], u[p]) for p in (1, 2)], [_pick(half, u[p], v[p]) for p in (1, 2)])
        for v, u in zip(vs, turned)
    ]


class _Own:
    def __init__(self, ref):
        self.ref = ref

    def tile(self, at):
        return self.ref[at : at + 8, :]

    def core(self, q, p, s):
        return self.tile((q - 1) * 64 + 16 * p + 8 * s)

    def outer(self, i, s):
        return self.tile(OWN_EY + 16 * i + 8 * s)

    def quads(self, i, s):
        return self.tile(OWN_COLS + 16 * i + 8 * s)


class _Sent(_Own):
    def __init__(self, ref, from_below):
        self.ref, self.first = ref, 6 if from_below else 0

    def core(self, q, p, s):
        if 2 <= q <= 7:
            v = self.tile((q - 2) * 64 + 16 * p + 8 * s)
            return jnp.where(_rows_far(self.first), self.core(q, 0, s), v) if p == 3 else v
        at = OUTER + (0 if q == 1 else 48) + 8 * s
        if p in (1, 2):
            return self.tile(at + 16 * (p - 1))
        shared = self.tile(at + 32)
        if p == 0:
            return shared
        near = _iota((8, LANES), 0) // 2 == self.first // 2
        return jnp.where(near, _roll(shared, -2 if self.first else 2, 0), shared)

    def short(self, i, s):
        at = i * 64 + 48 if i < 6 else OUTER + 48 * (i - 6)
        return _roll(self.tile(at + 8 * s), -2 if self.first else 2, 0)

    def outer(self, i, s):
        return self.short(i, s)

    def quads(self, i, s):
        return self.short(4 + i, s)


def _pieces(at, q, s):
    if 1 <= q <= 8:
        return [at.core(q, p, s) for p in range(4)]
    slot = 2 if q == 0 else 3
    near = [_roll(at.quads(c, s), by, 1) for c, by in ((1, 4 * (3 - slot)), (3, -4 * slot))]
    return [near[0], *(at.outer((0 if q == 0 else 2) + h, s) for h in range(2)), near[1]]


def _far_pieces(at, q, s):
    c, slot = divmod(q - 2, 4)
    return [_roll(at.quads(c, s), -4 * slot, 1), None, None, _roll(at.quads(2 + c, s), 4 * (3 - slot), 1)]


def _unpack_brick(at, mask, mask_far, fold, store, store_far):
    for batch in ([(0, 0), (1, 0), (2, 0), (3, 0)], [(4, 0), (2, 1), (3, 1), (4, 1)]):
        tasks = [(q, far, s) for q, far in batch for s in range(2)]
        groups = [
            [(_far_pieces if far else _pieces)(at, o, s) for o in (q, 9 - q)] for q, far, s in tasks
        ]
        for (q, far, s), rows in zip(tasks, _unfold(groups)):
            m = _outer_mask(mask_far if far else mask, fold, q)
            for r in range(8):
                if far:
                    store_far(s, 8 * q + r - 15, rows[r] * m)
                else:
                    store(s, 8 * q + r, rows[r] * m)


def _outer_mask(mask, fold, q):
    return mask * fold if q < 3 else mask


def _far_mask(g, zb):
    row = _iota((24, LANES), 0) - 8
    lane = _iota((24, LANES), 1) % 64
    below, above = (zb > 0).astype(F32), (zb < 3).astype(F32)
    return _inside(row, g * 8, 64) * jnp.where(lane < 4, below, jnp.where(lane >= 60, above, 0.0))


def _brick_kernel(ref, tile, far, *, at, rows):
    g, yb, zb = _position()

    def store(s, i, v):
        tile[s, i] = v

    def put(s, i, v):
        far[s, i] = v

    mask_far = _far_mask(g, zb)[rows.start - 8 : rows.stop - 8]
    _unpack_brick(at(ref), _ring_mask(g, zb)[rows], mask_far, _fold_mask(yb), store, put)
    for s in range(2):
        tile[s, FINE] = _roll(tile[s, FINE - 1], 64, 1)
        far[s, FINE - 15] = _roll(far[s, FINE - 16], 64, 1)


def _beside(s, *tiles):
    return lambda i: jnp.concatenate([t[s, i] for t in tiles], axis=0)


def _coarse_kernel(t1, t2, t3, f1, f2, f3, xm2, xp2, Ae, Ao, source, Be, Bo, ahead_of, raw, beyond, cs, c0, c1):
    g, yb, zb = _position()
    ring, fold = _ring_mask(g, zb), _fold_mask(yb)
    De, Do = D = [_beside(s, t1, t2, t3) for s in range(2)]
    far_e, far_o = [_beside(s, f1, f2, f3) for s in range(2)]

    row = _iota((8, LANES), 0)

    def near(i, s):
        at, r = slice(8 * (i // 2), 8 * (i // 2) + 8), 4 * s + 2 * (i % 2)
        return jnp.where(row < 4, _roll(xp2[at, :], -r, 0), _roll(xm2[at, :], 6 - r, 0))

    def ahead(q, s):
        c, slot = divmod(q - 2, 4)
        lo = _roll(near(10 + c, s), 4 * (3 - slot), 1)
        hi = _roll(near(12 + c, s), -4 * slot, 1)
        at = 2 * (q - 3) if 3 <= q <= 6 else 8
        return [lo, near(at, s), near(at + 1, s), hi]

    tasks = [(q, s) for q in range(2, 5) for s in range(2)]
    for (q, s), rows in zip(tasks, _unfold([(ahead(q, s), ahead(9 - q, s)) for q, s in tasks])):
        m = _outer_mask(ring[:8], fold, q)
        for r in range(8):
            _store(ahead_of.at[s], 8 * q + r, rows[r] * m, FINE - 1)

    def patch(rows, pairs):
        lane = _iota((24, LANES), 1) % 64
        sums = []
        for i in rows:
            f = 2 * i - 15
            e, o = far_e(f) + far_e(f + 1), far_o(f) + far_o(f + 1)
            sums.append((e, o, e + o, (far_e(f - 1) + far_e(f + 2)) + (far_o(f - 1) + far_o(f + 2))))
        turned = [_roll(o, 1, 0) + _roll(e, -1, 0) for e, o, _, _ in sums]
        hs = [(1.0 - 3.0 * W) * fp + W * (outer + t) for (_, _, fp, outer), t in zip(sums, turned)]
        ends = [(_roll(fp, -3, 1), _roll(fp, 2, 1)) for _, _, fp, _ in sums]
        sides = []
        for (_, _, fp, _), h, pair in zip(sums, hs, pairs):
            lo = _roll(h, -2, 1) + _roll(h, -3, 1) + W * (_roll(fp, -1, 1) + pair)
            hi = _roll(h, 2, 1) + _roll(h, 3, 1) + W * (_roll(fp, 1, 1) + pair)
            sides.append((lo, hi))
        for i, (lo, hi) in zip(rows, sides):
            low = jnp.where(lane == 0, lo, _roll(lo, 1, 1))
            high = jnp.where(lane == 63, hi, _roll(hi, -1, 1))
            beyond[i - 10] = jnp.where(lane < 32, low, high) * 0.125
        return ends

    def put_source(i, c):
        raw[i] = c

    whole = [lambda y, s=s, v=v: jnp.concatenate([ahead_of[s, y], v(y)], axis=0) for s, v in enumerate(D)]
    args = (whole, 32, W, 1.0 - 5.0 * W, None)
    _restrict(*args, 3, 7, put_source, None, 7)
    _restrict(*args, 10, 10, put_source, patch, 10)
    _sweep_three(g, yb, zb, lambda i: raw[i], lambda i: beyond[i], cs, c0, c1)
    base = [lambda i, v=v: W * v(i) for v in D]
    step_masks = _step_masks(g, yb, zb)
    _correct_and_smooth(step_masks, base, D, lambda i: c0[i], Be, Bo, 7, 13, 13)
    _smooth(step_masks, (lambda i: Be[i], lambda i: Bo[i]), D, Ae, Ao, 15, 25, 25)
    pair_of = lambda i: (De(i) + De(i + 1)) + (Do(i) + Do(i + 1))
    A = (lambda i: Ae[i], lambda i: Ao[i])
    _restrict(A, 24, 1.0, -5.0, pair_of, 8, 12, lambda i, c: _set(source, i, c), None, 6)


def _set(ref, i, v):
    ref[i] = v


def _ones_kernel(Te, To, source, Be, Bo, cs, c0, c1):
    g, yb, zb = _position()
    one = jnp.ones((32, LANES), F32)
    _sweep_three(g, yb, zb, lambda i: one, lambda i: one[8:], cs, c0, c1)
    step_masks = _step_masks(g, yb, zb)
    _correct_and_smooth(step_masks, None, None, lambda i: c0[i], Be, Bo, 7, 13, 13)
    _smooth(step_masks, (lambda i: Be[i], lambda i: Bo[i]), None, Te, To, 15, 25, 25)
    T = (lambda i: Te[i], lambda i: To[i])
    _restrict(T, 24, 1.0, -5.0, None, 8, 12, lambda i, c: _set(source, i, c), None, 6)


def _sweep_three(g, yb, zb, source, beyond, cs, c0, c1):
    ring, fold = BETA * _ring_mask(g, zb), _fold_mask(yb)
    outside = ring * _tall(fold, 32)
    lane = _iota((24, LANES), 1) % 64
    has_below, has_above = (zb > 0).astype(F32), (zb < 3).astype(F32)
    row = _iota((24, LANES), 0) - 8
    z_ends = jnp.where(lane < 2, has_below, jnp.where(lane >= 62, has_above, 0.0))
    beyond_mask = BETA * z_ends * _inside(row, g * 8, 64)
    beyond_outside = beyond_mask * _tall(fold, 24)
    mask = _ring_mask(g, zb)[8:]
    masks = (mask * _tall(fold, 24), mask)

    scaled = _lazily(lambda i: source(i) * (outside if i < 12 else ring))
    for i in range(4, COARSE):
        c = scaled(i)
        after = _roll(c, 64, 1) if i == COARSE - 1 else scaled(i + 1)
        near = (_roll(c, 1, 0) + _roll(c, -1, 0) + (scaled(i - 1) + after))[8:]
        c = c[8:]
        ends = None
        if i >= 10:
            ends = beyond(i - 10) * (beyond_outside if i < 12 else beyond_mask)
        cs[i] = c
        turns = _roll(c, 2, 1), _roll(c, -2, 1)
        _store(c0, i, c + _sweep(c, near, turns, lane, ends) * masks[i >= 12], COARSE - 1)
    _sweep_rows(c0, c1, cs, 5, masks)
    _sweep_rows(c1, c0, cs, 6, masks)


def _sweep(c, near, turns, lane, ends):
    before, after = turns
    if ends is not None:
        before = jnp.where(lane < 2, ends, before)
        after = jnp.where(lane >= 62, ends, after)
    return 0.2 * c + W * (near + (before + after))


def _sweep_rows(src, dst, cs, first, masks, batch=6):
    for start in range(first, COARSE, batch):
        rows = range(start, min(start + batch, COARSE))
        turned = [
            (_roll(src[i], 1, 0), _roll(src[i], -1, 0), _roll(src[i], 2, 1), _roll(src[i], -2, 1)) for i in rows
        ]
        for i, (low, high, *turns) in zip(rows, turned):
            near = (low + high) + (src[i - 1] + src[i + 1])
            _store(dst, i, cs[i] + _sweep(src[i], near, turns, None, None) * masks[i >= 12], COARSE - 1)


def _restrict(fields, rows, near, centre, more, first, count, store, patch, size):
    lane = _iota((rows, LANES), 1)
    even = lane % 2 == 0

    for start in range(first, first + count, size):
        even_at, odd_at = (_lazily(lambda u, v=v, start=start: v(2 * start + u)) for v in fields)
        sums = []
        us = range(min(size, first + count - start))
        for u in us:
            y = 2 * u
            ee, eo = even_at(y) + even_at(y + 1), odd_at(y) + odd_at(y + 1)
            outer = (even_at(y - 1) + even_at(y + 2)) + (odd_at(y - 1) + odd_at(y + 2))
            sums.append((ee, eo, ee + eo, outer))
        turned = [_roll(eo, 1, 0) + _roll(ee, -1, 0) for ee, eo, _, _ in sums]
        hs = []
        for u, ((_, _, pair, outer), t) in enumerate(zip(sums, turned)):
            h = (centre + 2.0 * near) * pair + near * (outer + t)
            hs.append(h if more is None else h + more(2 * (start + u)))
        sides = [(_roll(pair, 1, 1), _roll(pair, -2, 1)) for _, _, pair, _ in sums]
        if patch is not None:
            ends = patch([start + u for u in us], [pair[8:] for _, _, pair, _ in sums])
            for u, ((before, after), (low, high)) in enumerate(zip(sides, ends)):
                low = jnp.where(lane[8:] % 64 == 0, low, before[8:])
                high = jnp.where(lane[8:] % 64 == 62, high, after[8:])
                sides[u] = (
                    jnp.concatenate([before[:8], low], axis=0),
                    jnp.concatenate([after[:8], high], axis=0),
                )
        cs = [h + _roll(h, -1, 1) + near * (before + after) for h, (before, after) in zip(hs, sides)]
        cs = [jnp.where(even, c, _roll(c, 1, 1)) * 0.125 for c in cs]
        for u, c in enumerate(cs):
            store(start + u, c)


def _step_masks(g, yb, zb):
    mask = _ring_mask(g, zb)[8:]
    masks = (mask * _tall(_fold_mask(yb), 24), mask)
    return masks, [0.2 * m for m in masks], [W * m for m in masks]


def _of_row(pair, i, own_first):
    if isinstance(i, int):
        return pair[i >= own_first]
    return jnp.where(i < own_first, *pair)


def _relax(even, odd, i, n, store, batch=4):
    for first in range(0, n, batch):
        us = range(first, min(first + batch, n))
        turned = []
        for u in us:
            e, o = even(u), odd(u)
            turned.append((_roll(e, 1, 1), _roll(e, -1, 1), _roll(o, 1, 1), _roll(o, -1, 1), _roll(o, 1, 0), _roll(e, -1, 0)))
        for u, (e1, e2, o1, o2, before, after) in zip(us, turned):
            e, o = even(u), odd(u)
            ye = ((even(u - 1) + even(u + 1)) + (e1 + e2)) + (o + before)
            yo = ((odd(u - 1) + odd(u + 1)) + (o1 + o2)) + (e + after)
            store(i + u, e, o, ye, yo)


def _smooth_to(step_masks, D, dst_e, dst_o):
    def store(i, e, o, ye, yo):
        m, n = _of_row(step_masks[1], i, 24), _of_row(step_masks[2], i, 24)
        if D is not None:
            ye, yo = ye + D[0](i), yo + D[1](i)
        _store(dst_e, i, e * m + ye * n, FINE - 1)
        _store(dst_o, i, o * m + yo * n, FINE - 1)

    return store


def _smooth(step_masks, src, D, dst_e, dst_o, first, count, size):
    def fn(i, n):
        even, odd = (_lazily(lambda u, v=v: v(i + u)) for v in src)
        _relax(even, odd, i, n, _smooth_to(step_masks, D, dst_e, dst_o))

    _blocks(first, count, size, fn)


def _correct_and_smooth(step_masks, base, D, correction, dst_e, dst_o, first, count, size):
    def fn(start, n):
        i = 2 * start
        c = _lazily(lambda u: correction(start + u))
        if base is None:
            even = odd = lambda u: c(u // 2)
        else:
            even, odd = (_lazily(lambda u, v=v: v(i + u) + c(u // 2)) for v in base)
        _relax(even, odd, i, 2 * n, _smooth_to(step_masks, D, dst_e, dst_o))

    _blocks(first, count, size, fn)


def _cycle_kernel(
    order, t1, t2, t3, Re, Ro, raw, Te, To, raw_one, part, across, pot, res, Be, Bo, cs, c0, c1, boxes, place, sem
):
    g, yb, zb = _position()
    fetch = pltpu.make_async_copy(order, place, sem.at[0])
    fetch.start()
    totals = part[...] + across[...]
    means = jnp.sum(totals, axis=1, keepdims=True) * (1.0 / CELLS)
    mean1 = jnp.broadcast_to(means[0:1], (24, LANES))
    mean2 = jnp.broadcast_to(means[1:2], (24, LANES))
    step_masks = _step_masks(g, yb, zb)
    masks = step_masks[0]

    all_of = lambda ref: lambda i: ref[i]

    De, Do = D = [_beside(s, t1, t2, t3) for s in range(2)]
    A = (lambda i: Re[i] - mean1 * Te[i], lambda i: Ro[i] - mean1 * To[i])

    for i in range(8, COARSE):
        c = raw[i] - mean1 * raw_one[i] - mean2
        _store(cs, i, c * (masks[i >= 12] * BETA), COARSE - 1)
    _sweep_rows(cs, c0, cs, 9, masks)
    _sweep_rows(c0, c1, cs, 10, masks)
    _sweep_rows(c1, c0, cs, 11, masks)
    _correct_and_smooth(step_masks, A, D, all_of(c0), Be, Bo, 11, 9, 9)

    fetch.wait()
    box_of = [place[h, 0] for h in range(4)]
    for q in (3, 4):
        i0 = 8 * q
        even = _lazily(lambda u: Be[i0 + u])
        odd = _lazily(lambda u: Bo[i0 + u])
        left = ([], [])

        def store(i, e, o, ye, yo):
            left[0].append(t2[0, i] - (6.0 * e - ye)[8:16])
            left[1].append(t2[1, i] - (6.0 * o - yo)[8:16])

        _relax(even, odd, i0, 8, store)
        tasks = [(f, s) for f in range(2) for s in range(2)]
        done = [[v(u)[8:16] for u in range(8)] for v in (even, odd)]
        groups = [(done, left)[f][s] for f, s in tasks]
        for (f, s), sides in zip(tasks, _refold(groups)):
            for o, pieces in zip((q - 3, 6 - q), sides):
                for h in range(2):
                    at = BLOCK * ((f * 4 + o) * 2 + h) + s
                    boxes[pl.ds(at, 8, stride=2), :] = pieces[h]
    for f, out in enumerate((pot, res)):
        for o in range(4):
            for h in range(2):
                v = _blk(boxes, (f * 4 + o) * 2 + h)
                out[box_of[(o // 2) * 2 + h], :, (o % 2) * LANES : (o % 2 + 1) * LANES] = v


def _lazily(fn):
    made = {}

    def get(u):
        if u not in made:
            made[u] = fn(u)
        return made[u]

    return get


def _shape(*dims):
    return jax.ShapeDtypeStruct(dims, F32)


def _rows(n):
    return _shape(n, LANES)


VMEM = pl.BlockSpec(memory_space=pltpu.VMEM)
HBM = pl.BlockSpec(memory_space=pltpu.HBM)


def _call(kernel, specs, outs, scratch=(), us=0.1, grant=40.0):
    return pl.pallas_call(
        kernel,
        out_shape=outs,
        in_specs=specs,
        out_specs=[VMEM] * len(outs),
        scratch_shapes=scratch,
        cost_estimate=pl.CostEstimate(flops=0, transcendentals=0, bytes_accessed=int(us * 3.5e6)),
        compiler_params=pltpu.CompilerParams(vmem_limit_bytes=int(grant * 2**20)),
    )


def _y_shift(n):
    return [(4 * y + z, 4 * ((y + n) % 4) + z) for y in range(4) for z in range(4)]


def _z_shift(n):
    return [(4 * y + z, 4 * y + (z + n) % 4) for y in range(4) for z in range(4)]


def _x_shift(n):
    return [(x, (x + n) % 8) for x in range(8)]


def _body(weights, divergence, box_coords, neighbors):
    coords = box_coords.T
    raw, weight = _call(
        _fetch_kernel,
        [HBM, HBM],
        [_shape(*divergence.shape), _shape(*weights.shape[1:])],
        [pltpu.SemaphoreType.DMA((2,))],
        us=1.0,
        grant=53.79,
    )(divergence, weights)
    own, sums, order, up, down = _call(
        _sort_kernel,
        [VMEM] * 3,
        [
            *(_rows(128), _rows(8), jax.ShapeDtypeStruct((8, LANES), jnp.int32)),
            *(_rows(Y_MESSAGE), _rows(Y_MESSAGE)),
        ],
        [pltpu.VMEM((128, LANES), F32)],
    )(coords, raw, weight)
    across = lax.ppermute(sums, "dev", _y_shift(2))
    below = lax.ppermute(up, "dev", _y_shift(1))
    above = lax.ppermute(down, "dev", _y_shift(-1))

    plane = pltpu.VMEM((COARSE + 1, 24, LANES), F32)
    fine = _shape(FINE + 1, 24, LANES)
    inner = pltpu.VMEM((FINE + 1, 24, LANES), F32)
    ones = _call(_ones_kernel, [], [fine, fine, _shape(COARSE, 24, LANES)], [inner, inner, plane, plane, plane], us=1.0)()
    sums, ones = lax.optimization_barrier((sums, ones))
    total = _call(_total_kernel, [VMEM] * 4, [_rows(8)])(sums, below, above, across)[0]
    zacross = lax.ppermute(total, "dev", _z_shift(2))
    up, down = _call(_z_kernel, [VMEM] * 4, [_rows(168), _rows(168)])(own, below, above, total)
    zbelow = lax.ppermute(up, "dev", _z_shift(1))
    zabove = lax.ppermute(down, "dev", _z_shift(-1))

    mine, up, down, high, low, part = _call(
        _x_kernel,
        [VMEM] * 7,
        [_rows(640), _rows(MESSAGE), _rows(MESSAGE), _rows(64), _rows(64), _rows(8)],
    )(own, below, above, zbelow, zabove, total, zacross)
    xm1 = lax.ppermute(up, "grp", _x_shift(1))
    xp1 = lax.ppermute(down, "grp", _x_shift(-1))
    xm2 = lax.ppermute(high, "grp", _x_shift(2))
    xp2 = lax.ppermute(low, "grp", _x_shift(-2))
    bricks = []
    for ref, at, rows in (
        (xm1, functools.partial(_Sent, from_below=True), slice(8, 16)),
        (mine, _Own, slice(16, 24)),
        (xp1, functools.partial(_Sent, from_below=False), slice(24, 32)),
    ):
        kernel = functools.partial(_brick_kernel, at=at, rows=rows)
        outs = [_shape(2, FINE + 1, 8, LANES), _shape(2, 26, 8, LANES)]
        bricks.append(_call(kernel, [VMEM], outs, us=0.8)(ref))
    part, bricks = lax.optimization_barrier((part, bricks))
    tiles, fars = zip(*bricks)
    part, send = _call(_window_kernel, [VMEM] * 5, [_rows(8), _rows(8)])(part, xm1, xp1, xm2, xp2)
    xacross = lax.ppermute(send, "grp", [(x, (x + 3 - 6 * (x % 2)) % 8) for x in range(8)])

    start = _call(
        _coarse_kernel,
        [VMEM] * 8,
        [fine, fine, _shape(COARSE, 24, LANES)],
        [
            inner,
            inner,
            pltpu.VMEM((2, FINE + 1, 8, LANES), F32),
            pltpu.VMEM((COARSE, 32, LANES), F32),
            pltpu.VMEM((12, 24, LANES), F32),
            plane,
            plane,
            plane,
        ],
        us=3,
    )(*tiles, *fars, xm2, xp2)

    boxes = pltpu.VMEM((16 * BLOCK, LANES), F32)
    pot, res = _call(
        _cycle_kernel,
        [VMEM] * 12,
        [_shape(4, 16, 256), _shape(4, 16, 256)],
        [inner, inner, plane, plane, plane, boxes, pltpu.SMEM((8, LANES), jnp.int32), pltpu.SemaphoreType.DMA((1,))],
    )(order, *tiles, *start, *ones, part, xacross)
    return pot, res


def solution(mesh):
    table = _mean_weights()

    def body(divergence, box_coords, neighbors):
        return _body(jnp.asarray(table), divergence, box_coords, neighbors)

    split = P(("grp", "dev"), None, None)
    return jax.shard_map(
        body, mesh=mesh, in_specs=(split, P(), P()), out_specs=(split, split), check_vma=False
    )
```
